32 devices in a mesh: meet: 2 (over x), tm: 16 (over z, y, core).
Axes of the slice: x: 2, y: 2, z: 4, core: 2. Of those that a mesh axis runs over, the one named last changes fastest.
Arguments:
- waveform: bfloat16 [8, 327680], P(None, ('meet', 'tm')), parts along dimension 1, may hold values from -16 to 16
- masks: int32 [2, 2048, 257], P(None, ('meet', 'tm')), parts along dimension 1, may hold values from 0 to 255, as said below
- valid: int32 [2], P('meet'), parts along dimension 0, may hold values from 512 to 1024, as said below
- ref_mic: int32 [2], P('meet'), parts along dimension 0, may hold values from 0 to 7
- conv1_w: bfloat16 [9, 256], replicated, may hold values from -2 to 2
- conv1_b: float32 [256], replicated, may hold values from -4 to 4
- conv2_w: bfloat16 [9, 256, 256], replicated, may hold values from -0.125 to 0.125
- conv2_b: float32 [256], replicated, may hold values from -4 to 4
- proj_w: bfloat16 [4864, 256], replicated, may hold values from -0.078125 to 0.078125
- proj_b: float32 [256], replicated, may hold values from -4 to 4
Outputs:
- features: bfloat16 [1, 512, 256], P(None, ('meet', 'tm')), parts along dimension 1
The draws below stay inside these ranges and needn't reach their ends.
There are 2 independent parts, one for each index of `meet`. The reference program is written for one: setup_inputs(seed, part) draws one part's arguments, and reference() takes and returns one part's arrays. A program takes and returns all parts, laid end to end along the dimension named above; an argument that names none is the same for every part. Nothing has to cross between parts.
Inputs may be any that keep to these rules, and one draw needn't show every extreme that they name: `masks`: mask levels; level / 255 is the weight of a time-frequency cell for a speaker or, in the last row, for the noise. `valid`: frames of the meeting that hold speech data; all 1024 in some meetings.
All inputs are finite; a program needn't handle non-finite values.
Results may differ from the reference program's by a relative error of at most 0.003.
The reference program's roundings to bfloat16 on the way count: a program that leaves them out, or rounds other values in their place, can miss the bound.
Values may be sent and summed in bfloat16 or wider, within the bound.
No kernel may reach another device: no remote copies, remote signals or barrier semaphores. Data moves between devices by JAX's collectives and lax.ppermute only.
A program may use at most 64 MiB of HBM per device.

```python
import math
import jax
import jax.numpy as jnp
from jax import lax

MICS = 8
NFFT = 512
HOP = 160
BINS = 257
MELS = 80
SPK = 1
CHANNELS = 256
D = 256
F_DEV = 64
FRAMES = 1024
Q2 = 19
OUTF = 256
N_TM = 16


block_frames = 16


echo_count = 3


def speaker_blocks(key):
    picker = jax.random.fold_in(key, 101)
    return jax.random.randint(picker, (FRAMES // block_frames,), 0, SPK + 1)


def draw_masks(key, part):
    owner = jnp.repeat(speaker_blocks(key), block_frames)
    high_key, low_key = jax.random.split(jax.random.fold_in(key, 102))
    strong = jax.random.randint(high_key, (SPK + 1, FRAMES, BINS), 128, 256)
    faint = jax.random.randint(low_key, (SPK + 1, FRAMES, BINS), 0, 96)
    chosen = jnp.arange(SPK + 1)[:, None, None] == owner[None, :, None]
    return jnp.where(chosen, strong, faint).astype(jnp.int32)


def draw_valid(key, part):
    cutoff = jax.random.randint(jax.random.fold_in(key, 104), (1,), 0, FRAMES // 2 + 1)
    return (FRAMES - cutoff * (1 - part % 2)).astype(jnp.int32)


def delayed_copy(signal, delays):
    length = signal.shape[0]
    positions = jnp.arange(length, dtype=jnp.int32)[None, :] - delays[:, None]
    picked = jnp.take(signal, jnp.clip(positions, 0, length - 1), axis=0)
    return jnp.where(positions >= 0, picked, 0.0)


def draw_waveform(key, part):
    length = FRAMES * HOP
    reach = NFFT // 4
    owner = jnp.repeat(speaker_blocks(key), block_frames * HOP)
    subkeys = jax.random.split(jax.random.fold_in(key, 103), 11)
    source = jax.random.normal(subkeys[0], (length,), jnp.float32)
    sensor = jax.random.normal(subkeys[1], (MICS, length), jnp.float32)
    shared = jax.random.normal(subkeys[2], (length,), jnp.float32)
    direct_delay = jax.random.randint(subkeys[3], (SPK, MICS), 0, reach + 1).astype(jnp.int32)
    echo_delay = jax.random.randint(subkeys[7], (SPK, echo_count, MICS), 0, reach + 1).astype(jnp.int32)
    noise_delay = jax.random.randint(subkeys[8], (MICS,), 0, reach + 1).astype(jnp.int32)
    direct_gain = jax.random.uniform(subkeys[9], (SPK, MICS), jnp.float32, 0.6, 1.2)
    echo_gain = jax.random.normal(subkeys[10], (SPK, echo_count, MICS), jnp.float32) * 0.35
    block_gain = jnp.exp(jax.random.uniform(subkeys[4], (FRAMES // block_frames,), jnp.float32, -0.7, 0.7))
    ramp = 1.0 + 2.0 * jnp.arange(length, dtype=jnp.float32) / length
    loudness = ramp * jnp.repeat(block_gain, block_frames * HOP) * 0.6
    speech = jnp.zeros((MICS, length), jnp.float32)
    for talker in range(SPK):
        imaged = direct_gain[talker][:, None] * delayed_copy(source, direct_delay[talker])
        for echo in range(echo_count):
            imaged = imaged + echo_gain[talker, echo][:, None] * delayed_copy(source, echo_delay[talker, echo])
        speech = jnp.where(owner[None, :] == talker, imaged, 0.0)
    sensor_gain = jnp.exp(jax.random.uniform(subkeys[5], (MICS,), jnp.float32, -1.6, -0.5))
    mixing = jax.random.normal(subkeys[6], (MICS,), jnp.float32) * 0.5
    noises = sensor_gain[:, None] * sensor + mixing[:, None] * delayed_copy(shared, noise_delay)
    combined = speech * loudness[None, :] + noises
    return jnp.clip(combined, -16.0, 16.0).astype(jnp.bfloat16)


def centred(own_key, dims, deviation, most, held_as=jnp.bfloat16):
    array = jax.random.normal(own_key, dims, jnp.float32) * deviation
    return jnp.minimum(jnp.maximum(array, -most), most).astype(held_as)


def setup_inputs(seed: int = 0, part: int = 0) -> dict:
    splits = jax.random.split(jax.random.key(seed), 11)
    own_keys = jax.random.split(jax.random.fold_in(splits[10], part), 11)
    waveform = draw_waveform(jax.random.fold_in(jax.random.fold_in(splits[10], part), 71), part)
    masks = draw_masks(jax.random.fold_in(jax.random.fold_in(splits[10], part), 71), part)
    valid = draw_valid(jax.random.fold_in(jax.random.fold_in(splits[10], part), 71), part)
    ref_mic = jax.random.randint(own_keys[3], (1,), 0, MICS).astype(jnp.int32)
    conv1_w = centred(splits[4], (9, CHANNELS), 9 ** -0.5, 2.0)
    conv1_b = centred(splits[5], (CHANNELS,), 1.0, 4.0, jnp.float32)
    conv2_w = centred(splits[6], (9, CHANNELS, CHANNELS), (9 * CHANNELS) ** -0.5, 0.125)
    conv2_b = centred(splits[7], (CHANNELS,), 1.0, 4.0, jnp.float32)
    proj_w = centred(splits[8], (Q2 * CHANNELS, D), (Q2 * CHANNELS) ** -0.5, 0.078125)
    proj_b = centred(splits[9], (D,), 1.0, 4.0, jnp.float32)
    return {"waveform": waveform, "masks": masks, "valid": valid, "ref_mic": ref_mic, "conv1_w": conv1_w, "conv1_b": conv1_b, "conv2_w": conv2_w, "conv2_b": conv2_b, "proj_w": proj_w, "proj_b": proj_b}


loading = 0.03
epsilon = 1e-6
sample_rate = 16000.0


def dft_tables(fft_len, bin_count):
    sample_pos = jnp.arange(fft_len, dtype=jnp.int32)
    bin_pos = jnp.arange(bin_count, dtype=jnp.int32)
    product = (sample_pos[:, None] * bin_pos[None, :]) % fft_len
    phase = product.astype(jnp.float32) * (2.0 * math.pi / fft_len)
    window = 0.5 - 0.5 * jnp.cos(sample_pos.astype(jnp.float32) * (2.0 * math.pi / fft_len))
    cosine_table = (window[:, None] * jnp.cos(phase)).astype(jnp.bfloat16)
    sine_table = (-window[:, None] * jnp.sin(phase)).astype(jnp.bfloat16)
    return cosine_table, sine_table


def mel_bank(bin_count, mel_count):
    mel_top = 2595.0 * math.log10(1.0 + sample_rate / 2.0 / 700.0)
    points = jnp.arange(mel_count + 2, dtype=jnp.float32) * (mel_top / (mel_count + 1))
    edges_hz = 700.0 * (jnp.power(10.0, points / 2595.0) - 1.0)
    freq_hz = jnp.arange(bin_count, dtype=jnp.float32) * (sample_rate / 2.0 / (bin_count - 1))
    lower_hz = edges_hz[:-2]
    centre_hz = edges_hz[1:-1]
    upper_hz = edges_hz[2:]
    rising = (freq_hz[:, None] - lower_hz[None, :]) / (centre_hz - lower_hz)[None, :]
    falling = (upper_hz[None, :] - freq_hz[:, None]) / (upper_hz - centre_hz)[None, :]
    return jnp.maximum(jnp.minimum(rising, falling), 0.0)


def spectra(extended, frames, hop_len, cosine_table, sine_table):
    mic_count = extended.shape[0]
    fft_len = cosine_table.shape[0]
    block_count = -(-fft_len // hop_len)
    pieces = extended.reshape(mic_count, frames + block_count - 1, hop_len)
    framed = jnp.concatenate([pieces[:, offset:offset + frames] for offset in range(block_count)], axis=2)
    framed = framed[:, :, :fft_len].reshape(mic_count * frames, fft_len)
    spec_re = jnp.dot(framed, cosine_table, preferred_element_type=jnp.float32)
    spec_im = jnp.dot(framed, sine_table, preferred_element_type=jnp.float32)
    return spec_re.reshape(mic_count, frames, -1), spec_im.reshape(mic_count, frames, -1)


def cov_partial(spec_re, spec_im, weight):
    highest = lax.Precision.HIGHEST
    scaled_re = weight[:, None] * spec_re[None]
    scaled_im = weight[:, None] * spec_im[None]

    def paired(left_part, right_part):
        return jnp.einsum('kmtf,ntf->kmnf', left_part, right_part, precision=highest)

    stats_re = paired(scaled_re, spec_re) + paired(scaled_im, spec_im)
    stats_im = paired(scaled_im, spec_re) - paired(scaled_re, spec_im)
    return stats_re, stats_im


def solve_beams(stats_re, stats_im, ref_mic):
    mic_count = stats_re.shape[1]
    identity = jnp.eye(mic_count, dtype=jnp.float32)[None, :, :, None]
    target_re = stats_re[:-1]
    target_im = stats_im[:-1]
    other_re = jnp.sum(stats_re, axis=0)[None] - target_re
    other_im = jnp.sum(stats_im, axis=0)[None] - target_im
    spread = jnp.sum(other_re * identity, axis=(1, 2))
    ridge = loading * spread / mic_count + epsilon
    matrix_re = other_re + ridge[:, None, None, :] * identity
    matrix_im = other_im
    answer_re = target_re
    answer_im = target_im
    row_index = jnp.arange(mic_count, dtype=jnp.int32)
    for pivot in range(mic_count):
        pivot_re = matrix_re[:, pivot, pivot]
        pivot_im = matrix_im[:, pivot, pivot]
        modulus = pivot_re * pivot_re + pivot_im * pivot_im
        inverse_re = (pivot_re / modulus)[:, None]
        inverse_im = (-pivot_im / modulus)[:, None]
        lead_re = matrix_re[:, pivot] * inverse_re - matrix_im[:, pivot] * inverse_im
        lead_im = matrix_re[:, pivot] * inverse_im + matrix_im[:, pivot] * inverse_re
        head_re = answer_re[:, pivot] * inverse_re - answer_im[:, pivot] * inverse_im
        head_im = answer_re[:, pivot] * inverse_im + answer_im[:, pivot] * inverse_re
        column_re = matrix_re[:, :, pivot][:, :, None]
        column_im = matrix_im[:, :, pivot][:, :, None]
        on_pivot = (row_index == pivot)[None, :, None, None]
        matrix_re, matrix_im = (
            jnp.where(on_pivot, lead_re[:, None], matrix_re - (column_re * lead_re[:, None] - column_im * lead_im[:, None])),
            jnp.where(on_pivot, lead_im[:, None], matrix_im - (column_re * lead_im[:, None] + column_im * lead_re[:, None])))
        answer_re, answer_im = (
            jnp.where(on_pivot, head_re[:, None], answer_re - (column_re * head_re[:, None] - column_im * head_im[:, None])),
            jnp.where(on_pivot, head_im[:, None], answer_im - (column_re * head_im[:, None] + column_im * head_re[:, None])))
    trace_ratio = jnp.sum(answer_re * identity, axis=(1, 2))
    chosen = (row_index == ref_mic[0]).astype(jnp.float32)[None, None, :, None]
    scale_by = 1.0 / (trace_ratio + epsilon)
    beam_re = jnp.sum(answer_re * chosen, axis=2) * scale_by[:, None, :]
    beam_im = jnp.sum(answer_im * chosen, axis=2) * scale_by[:, None, :]
    return beam_re, beam_im


def beam_logmel(spec_re, spec_im, beam_re, beam_im, melbank, live_rows):
    highest = lax.Precision.HIGHEST

    def mixed(beam_part, spec_part):
        return jnp.einsum('kmf,mtf->ktf', beam_part, spec_part, precision=highest)

    beamed_re = mixed(beam_re, spec_re) + mixed(beam_im, spec_im)
    beamed_im = mixed(beam_re, spec_im) - mixed(beam_im, spec_re)
    power_sum = beamed_re * beamed_re + beamed_im * beamed_im
    melspec = jnp.einsum('ktf,fj->ktj', power_sum, melbank, precision=highest)
    return (jnp.log(melspec + epsilon) * live_rows[None, :, None]).astype(jnp.bfloat16)


def stem(extended, row_live, out_live, conv1_w, conv1_b, conv2_w, conv2_b, proj_w, proj_b):
    streams, span, mel_count = extended.shape
    frames = span - 3
    halves = frames // 2 + 1
    quarter = frames // 4
    q_first = (mel_count - 3) // 2 + 1
    q_second = (q_first - 3) // 2 + 1
    channels = conv1_w.shape[1]
    kernel_one = conv1_w.astype(jnp.float32)
    layer_one = jnp.zeros((streams, halves, q_first, channels), jnp.float32)
    for shift_t in range(3):
        for shift_f in range(3):
            tap = extended[:, shift_t:shift_t + 2 * halves - 1:2, shift_f:shift_f + 2 * q_first - 1:2]
            layer_one = layer_one + tap.astype(jnp.float32)[..., None] * kernel_one[3 * shift_t + shift_f]
    layer_one = (jax.nn.relu(layer_one + conv1_b) * row_live[None, :, None, None]).astype(jnp.bfloat16)
    summed = jnp.zeros((streams * quarter * q_second, channels), jnp.float32)
    for shift_t in range(3):
        for shift_f in range(3):
            window = layer_one[:, shift_t:shift_t + 2 * quarter - 1:2, shift_f:shift_f + 2 * q_second - 1:2]
            summed = summed + jnp.dot(window.reshape(-1, channels), conv2_w[3 * shift_t + shift_f],
                                      preferred_element_type=jnp.float32)
    layer_two = jax.nn.relu(summed + conv2_b).astype(jnp.bfloat16).reshape(streams * quarter, q_second * channels)
    projected = jnp.dot(layer_two, proj_w, preferred_element_type=jnp.float32) + proj_b
    projected = projected.reshape(streams, quarter, -1) * out_live[None, :, None]
    return projected.astype(jnp.bfloat16)


def reference(waveform, masks, valid, ref_mic, conv1_w, conv1_b, conv2_w, conv2_b, proj_w, proj_b):
    mic_count = waveform.shape[0]
    block_count = -(-NFFT // HOP)
    cosine_table, sine_table = dft_tables(NFFT, BINS)
    melbank = mel_bank(BINS, MELS)
    padded = jnp.concatenate([waveform, jnp.zeros((mic_count, (block_count - 1) * HOP), waveform.dtype)], axis=1)
    shard_ids = jnp.arange(N_TM, dtype=jnp.int32)

    def shard_spectra(shard):
        extended = lax.dynamic_slice_in_dim(padded, (shard * (F_DEV * HOP)).astype(jnp.int32),
                                            (F_DEV + block_count - 1) * HOP, 1)
        return spectra(extended, F_DEV, HOP, cosine_table, sine_table)

    def shard_live(shard):
        return (shard * F_DEV + jnp.arange(F_DEV, dtype=jnp.int32) < valid[0]).astype(jnp.float32)

    def add_shard(carry, shard):
        spec_re, spec_im = shard_spectra(shard)
        shard_mask = lax.dynamic_slice_in_dim(masks, (shard * F_DEV).astype(jnp.int32), F_DEV, 1)
        weight = shard_mask.astype(jnp.float32) * shard_live(shard)[None, :, None] / 255.0
        part_re, part_im = cov_partial(spec_re, spec_im, weight)
        return (carry[0] + part_re, carry[1] + part_im), None

    zeros_cov = jnp.zeros((SPK + 1, mic_count, mic_count, BINS), jnp.float32)
    (stats_re, stats_im), _ = lax.scan(add_shard, (zeros_cov, zeros_cov), shard_ids)
    beam_re, beam_im = solve_beams(stats_re, stats_im, ref_mic)

    def shard_logmel(shard):
        spec_re, spec_im = shard_spectra(shard)
        return beam_logmel(spec_re, spec_im, beam_re, beam_im, melbank, shard_live(shard))

    logmel = lax.map(shard_logmel, shard_ids)
    logmel = jnp.transpose(logmel, (1, 0, 2, 3)).reshape(SPK, FRAMES, MELS)
    ext_all = jnp.concatenate([jnp.zeros((SPK, 3, MELS), logmel.dtype), logmel], axis=1)

    def shard_stem(shard):
        extended = lax.dynamic_slice_in_dim(ext_all, (shard * F_DEV).astype(jnp.int32), F_DEV + 3, 1)
        row_live = (shard * (F_DEV // 2) + jnp.arange(F_DEV // 2 + 1, dtype=jnp.int32) >= 1).astype(jnp.float32)
        quarter = F_DEV // 4
        out_live = (4 * (shard * quarter + jnp.arange(quarter, dtype=jnp.int32)) < valid[0]).astype(jnp.float32)
        return stem(extended, row_live, out_live, conv1_w, conv1_b, conv2_w, conv2_b, proj_w, proj_b)

    features = lax.map(shard_stem, shard_ids)
    return jnp.transpose(features, (1, 0, 2, 3)).reshape(SPK, OUTF, -1)
```

```python
import functools
import math

import jax
import jax.numpy as jnp
import numpy as np
from jax import lax
from jax.experimental import pallas as pl
from jax.experimental.pallas import tpu as pltpu
from jax.sharding import PartitionSpec as P

NFFT = 512
HOP = 160
MELS = 80
BINS = NFFT // 2 + 1
LANES = 128
MICS = 8
PAD_BINS = -(-BINS // LANES) * LANES
TILES = PAD_BINS // LANES
HALO = 3
LEAD = 512
TAIL = 384
STATS = 2 * MICS * MICS
SPAN = 42

loading = 0.03
epsilon = 1e-06
sample_rate = 16000.0


def passed_along(block, axis, distance):
    devices = range(lax.axis_size(axis))
    route = [(i - distance, i) for i in devices if i - distance in devices]
    return lax.ppermute(block, axis, route)


def dft_table():
    n = np.arange(NFFT)
    f = np.arange(BINS)
    phase = 2.0 * math.pi * ((n[:, None] * f[None, :]) % NFFT) / NFFT
    window = 0.5 - 0.5 * np.cos(2.0 * math.pi * n / NFFT)
    table = np.zeros((NFFT, 2, PAD_BINS), np.float32)
    table[:, 0, :BINS] = window[:, None] * np.cos(phase)
    table[:, 1, :BINS] = -window[:, None] * np.sin(phase)
    return jnp.asarray(table.reshape(NFFT, 2 * PAD_BINS)).astype(jnp.bfloat16)


def mel_bank():
    mel_top = 2595.0 * math.log10(1.0 + sample_rate / 2.0 / 700.0)
    points = np.arange(MELS + 2) * (mel_top / (MELS + 1))
    edges = 700.0 * (np.power(10.0, points / 2595.0) - 1.0)
    freq = np.arange(BINS) * (sample_rate / 2.0 / (BINS - 1))
    lower, centre, upper = edges[:-2], edges[1:-1], edges[2:]
    rising = (freq[:, None] - lower[None, :]) / (centre - lower)[None, :]
    falling = (upper[None, :] - freq[:, None]) / (upper - centre)[None, :]
    return np.maximum(np.minimum(rising, falling), 0.0).astype(np.float32)


def packed_mel_bank():
    bank = mel_bank()
    packed = np.zeros((PAD_BINS, 2, LANES), np.float32)
    for half in range(2):
        part = bank[:, half * 40 : half * 40 + SPAN]
        for copy in range(3):
            packed[:BINS, half, copy * SPAN : copy * SPAN + part.shape[1]] = part
    return jnp.asarray(packed.reshape(PAD_BINS, 2 * LANES))


def packed_conv1(conv1_w):
    rows = []
    for shift_t in range(3):
        rows.append(conv1_w[3 * shift_t : 3 * shift_t + 3])
        rows.append(jnp.zeros((SPAN - 3, conv1_w.shape[1]), conv1_w.dtype))
    rows.append(jnp.zeros((LANES - 3 * SPAN, conv1_w.shape[1]), conv1_w.dtype))
    return jnp.concatenate(rows, axis=0)


def stats_kernel(frames, prev_ref, wave_ref, next_ref, masks_ref, valid_ref, table_ref, spec_ref, stats_ref, framed_ref, weight_ref):
    position = lax.axis_index("tm")
    span = frames + HALO
    extended = jnp.concatenate(
        [prev_ref[...].astype(jnp.float32), wave_ref[...].astype(jnp.float32), next_ref[...].astype(jnp.float32)], axis=1
    )
    width = extended.shape[1]
    rolled = {}
    for frame in range(span):
        start = LEAD - HALO * HOP + frame * HOP
        base, shift = start // LANES * LANES, start % LANES
        if shift not in rolled:
            rolled[shift] = extended if shift == 0 else pltpu.roll(extended, width - shift, 1)
        framed_ref[MICS * frame : MICS * (frame + 1), :] = rolled[shift][:, base : base + NFFT]
    rest = framed_ref.shape[0] - MICS * span
    framed_ref[MICS * span :, :] = jnp.zeros((rest, NFFT), jnp.float32)
    spec = jnp.dot(framed_ref[...].astype(jnp.bfloat16), table_ref[...], preferred_element_type=jnp.float32)
    for tile in range(2 * TILES):
        spec_ref[tile] = spec[:, tile * LANES : (tile + 1) * LANES]

    row = lax.broadcasted_iota(jnp.int32, (frames, 1), 0)
    live = jnp.where(position * frames + row < valid_ref[0], 1.0 / 255.0, 0.0)
    weight_ref[:, :, PAD_BINS - LANES :] = jnp.zeros((2, frames, LANES), jnp.float32)
    for k in range(2):
        weight_ref[k, :, :BINS] = masks_ref[k].astype(jnp.float32) * live

    low = lax.broadcasted_iota(jnp.int32, (MICS, LANES), 0) < MICS // 2
    for tile in range(TILES):
        at_re = slice(tile * LANES, (tile + 1) * LANES)

        def add_frames(group, sums):
            first = pl.multiple_of(group * MICS, MICS)
            weights = [weight_ref[k, pl.ds(first, MICS), at_re] for k in range(2)]
            for frame in range(MICS):
                rows = pl.ds(pl.multiple_of((first + frame + HALO) * MICS, MICS), MICS)
                x_re = spec_ref[tile, rows, :]
                x_im = spec_ref[TILES + tile, rows, :]
                pairs = [x_re * x_re + x_im * x_im]
                for shift in range(1, MICS // 2 + 1):
                    y_re = pltpu.roll(x_re, MICS - shift, 0)
                    y_im = pltpu.roll(x_im, MICS - shift, 0)
                    pairs.append(x_re * y_re + x_im * y_im)
                    pairs.append(x_im * y_re - x_re * y_im)
                out = []
                for k in range(2):
                    w = jnp.broadcast_to(weights[k][frame : frame + 1], (MICS, LANES))
                    out.extend(sums[k * len(pairs) + i] + w * pair for i, pair in enumerate(pairs))
                sums = tuple(out)
            return sums

        zero = jnp.zeros((MICS, LANES), jnp.float32)
        sums = lax.fori_loop(0, frames // MICS, add_frames, (zero,) * 18)
        for k in range(2):
            own = sums[9 * k : 9 * k + 9]
            kept = list(own[:7]) + [jnp.where(low, own[7], own[8])]
            for i, value in enumerate(kept):
                first = tile * STATS + (k * MICS + i) * MICS
                stats_ref[first : first + MICS, :] = value


def columns_of(kept, sub):
    low = sub < MICS // 2
    diag_re = [kept[0], kept[1], kept[3], kept[5]]
    diag_im = [jnp.zeros_like(kept[0]), kept[2], kept[4], kept[6]]
    turned = pltpu.roll(kept[7], MICS // 2, 0)
    diag_re.append(jnp.where(low, kept[7], turned))
    diag_im.append(jnp.where(low, -turned, kept[7]))
    for shift in range(MICS // 2 + 1, MICS):
        diag_re.append(pltpu.roll(diag_re[MICS - shift], MICS - shift, 0))
        diag_im.append(-pltpu.roll(diag_im[MICS - shift], MICS - shift, 0))
    columns = []
    for n in range(MICS):
        re, im = diag_re[n], diag_im[n]
        for m in range(1, MICS):
            re = jnp.where(sub == m, diag_re[(n - m) % MICS], re)
            im = jnp.where(sub == m, diag_im[(n - m) % MICS], im)
        columns.append((re, im))
    return columns


def beams_of(stats, ref_mic):
    sub = lax.broadcasted_iota(jnp.int32, stats[0].shape, 0)
    answer = columns_of(stats[:MICS], sub)
    matrix = columns_of(stats[MICS:], sub)
    spread = jnp.sum(stats[MICS], axis=0, keepdims=True)
    ridge = loading * spread / MICS + epsilon
    matrix = [(jnp.where(sub == n, re + ridge, re), im) for n, (re, im) in enumerate(matrix)]
    for pivot in range(MICS):
        col_re, col_im = matrix[pivot]
        pivot_re = col_re[pivot : pivot + 1]
        pivot_im = col_im[pivot : pivot + 1]
        modulus = pivot_re * pivot_re + pivot_im * pivot_im
        inverse_re = pivot_re / modulus
        inverse_im = -pivot_im / modulus

        def eliminated(column):
            re, im = column
            row_re, row_im = re[pivot : pivot + 1], im[pivot : pivot + 1]
            lead_re = row_re * inverse_re - row_im * inverse_im
            lead_im = row_re * inverse_im + row_im * inverse_re
            return (
                jnp.where(sub == pivot, lead_re, re - (col_re * lead_re - col_im * lead_im)),
                jnp.where(sub == pivot, lead_im, im - (col_re * lead_im + col_im * lead_re)),
            )

        matrix = [eliminated(c) if n > pivot else c for n, c in enumerate(matrix)]
        answer = [eliminated(c) for c in answer]
    trace = answer[0][0][0:1]
    beam_re, beam_im = answer[0]
    for n in range(1, MICS):
        trace = trace + answer[n][0][n : n + 1]
        beam_re = jnp.where(ref_mic == n, answer[n][0], beam_re)
        beam_im = jnp.where(ref_mic == n, answer[n][1], beam_im)
    scale = 1.0 / (trace + epsilon)
    return beam_re * scale, beam_im * scale


def stem_kernel(frames, stats_ref, spec_ref, valid_ref, ref_mic_ref, bank_ref, conv1_w_ref, conv1_b_ref, conv2_w_ref, conv2_b_ref, proj_w_ref, proj_b_ref, out_ref, power_ref, logmel_ref):
    position = lax.axis_index("tm")
    valid = valid_ref[0]
    quarter = frames // 4
    groups = power_ref.shape[0] // MICS
    for tile in range(TILES):
        kept = [stats_ref[tile * STATS + i * MICS : tile * STATS + (i + 1) * MICS, :] for i in range(2 * MICS)]
        beam_re, beam_im = beams_of(kept, ref_mic_ref[0])
        at_re = slice(tile * LANES, (tile + 1) * LANES)
        for group in range(groups):
            sum_re = sum_im = None
            for m in range(MICS):
                rows = pl.ds(group * MICS * MICS + m, MICS, stride=MICS)
                x_re, x_im = spec_ref[tile, rows, :], spec_ref[TILES + tile, rows, :]
                b_re, b_im = beam_re[m : m + 1], beam_im[m : m + 1]
                part_re = b_re * x_re + b_im * x_im
                part_im = b_re * x_im - b_im * x_re
                sum_re = part_re if sum_re is None else sum_re + part_re
                sum_im = part_im if sum_im is None else sum_im + part_im
            power_ref[group * MICS : (group + 1) * MICS, at_re] = sum_re * sum_re + sum_im * sum_im
    mel = jnp.dot(power_ref[...], bank_ref[...], precision=lax.Precision.HIGHEST, preferred_element_type=jnp.float32)
    time = position * frames - HALO + lax.broadcasted_iota(jnp.int32, (power_ref.shape[0], 1), 0)
    live = (time >= 0) & (time < valid)
    logmel = jnp.where(live, jnp.log(mel + epsilon), 0.0)
    logmel = logmel.astype(jnp.bfloat16).astype(jnp.float32)
    for half in range(2):
        logmel_ref[half] = logmel[:, half * LANES : (half + 1) * LANES]

    q_first = (MELS - 3) // 2 + 1
    q_second = (q_first - 3) // 2 + 1
    order = list(range(0, q_first, 2)) + list(range(1, q_first, 2))
    evens = (q_first + 1) // 2
    lane = lax.broadcasted_iota(jnp.int32, (quarter, LANES), 1)
    row = lax.broadcasted_iota(jnp.int32, (quarter, 1), 0)
    windows = []
    for tap in range(3):
        packs = []
        for half in range(2):
            rows = [logmel_ref[half, pl.ds(2 * tap + a, quarter, stride=4), :] for a in range(3)]
            packs.append(jnp.where(lane < SPAN, rows[0], jnp.where(lane < 2 * SPAN, rows[1], rows[2])))
        patches = []
        for q in order:
            half, shift = (0, 2 * q) if q < 20 else (1, 2 * q - 40)
            patches.append(packs[half] if shift == 0 else pltpu.roll(packs[half], LANES - shift, 1))
        patches = jnp.concatenate(patches, axis=0).astype(jnp.bfloat16)
        layer = jnp.dot(patches, conv1_w_ref[...], preferred_element_type=jnp.float32) + conv1_b_ref[...]
        layer = jnp.maximum(layer, 0.0)
        if tap == 0:
            keep = jnp.concatenate([row + 2 * quarter * position >= 1] * q_first, axis=0)
            layer = jnp.where(keep, layer, 0.0)
        layer = layer.astype(jnp.bfloat16)
        count = quarter * q_second
        windows.append(layer[:count])
        windows.append(layer[quarter * evens : quarter * evens + count])
        windows.append(layer[quarter : quarter + count])
    second = jnp.dot(jnp.concatenate(windows, axis=1), conv2_w_ref[...], preferred_element_type=jnp.float32)
    second = jnp.maximum(second + conv2_b_ref[...], 0.0).astype(jnp.bfloat16)
    flat = jnp.concatenate([second[quarter * r : quarter * (r + 1)] for r in range(q_second)], axis=1)
    features = jnp.dot(flat, proj_w_ref[...], preferred_element_type=jnp.float32) + proj_b_ref[...]
    features = jnp.where(position * frames + 4 * row < valid, features, 0.0)
    out_ref[0] = features.astype(jnp.bfloat16)


def summed(block, axis):
    size = lax.axis_size(axis)
    if size & (size - 1):
        return lax.psum(block, axis)
    step = 1
    while step < size:
        block = block + lax.ppermute(block, axis, [(i, i ^ step) for i in range(size)])
        step *= 2
    return block


def per_device(waveform, masks, valid, ref_mic, conv1_w, conv1_b, conv2_w, conv2_b, proj_w, proj_b):
    frames = masks.shape[1]
    channels = conv1_w.shape[1]
    width = proj_w.shape[1]
    rows = -(-(frames + HALO) // MICS) * MICS
    prev_rim = passed_along(waveform[:, -LEAD:], "tm", 1)
    next_rim = passed_along(waveform[:, :TAIL], "tm", -1)
    vmem = pl.BlockSpec(memory_space=pltpu.VMEM)
    smem = pl.BlockSpec(memory_space=pltpu.SMEM)
    params = pltpu.CompilerParams(vmem_limit_bytes=48 * 1024 * 1024)
    spec, stats = pl.pallas_call(
        functools.partial(stats_kernel, frames),
        out_shape=(
            jax.ShapeDtypeStruct((2 * TILES, rows * MICS, LANES), jnp.float32),
            jax.ShapeDtypeStruct((TILES * STATS, LANES), jnp.float32),
        ),
        in_specs=[vmem, vmem, vmem, vmem, smem, vmem],
        out_specs=(vmem, vmem),
        scratch_shapes=[
            pltpu.VMEM((rows * MICS, NFFT), jnp.float32),
            pltpu.VMEM((2, frames, PAD_BINS), jnp.float32),
        ],
        compiler_params=params,
        name="stats",
    )(prev_rim, waveform, next_rim, masks, valid, dft_table())
    stats = summed(stats, "tm")
    return pl.pallas_call(
        functools.partial(stem_kernel, frames),
        out_shape=jax.ShapeDtypeStruct((1, frames // 4, width), jnp.bfloat16),
        in_specs=[vmem, vmem, smem, smem] + [vmem] * 7,
        out_specs=vmem,
        scratch_shapes=[
            pltpu.VMEM((rows, PAD_BINS), jnp.float32),
            pltpu.VMEM((2, rows, LANES), jnp.float32),
        ],
        compiler_params=params,
        name="stem",
    )(
        stats,
        spec,
        valid,
        ref_mic,
        packed_mel_bank(),
        packed_conv1(conv1_w),
        conv1_b[None],
        conv2_w.reshape(-1, channels),
        conv2_b[None],
        proj_w,
        proj_b[None],
    )


def solution(mesh):
    return jax.shard_map(
        per_device,
        mesh=mesh,
        in_specs=(
            P(None, ("meet", "tm")),
            P(None, ("meet", "tm"), None),
            P("meet"),
            P("meet"),
            P(),
            P(),
            P(),
            P(),
            P(),
            P(),
        ),
        out_specs=P(None, ("meet", "tm"), None),
        check_vma=False,
    )
```

```python
import functools
import math

import jax
import jax.numpy as jnp
import numpy as np
from jax import lax
from jax.experimental import pallas as pl
from jax.experimental.pallas import tpu as pltpu
from jax.sharding import PartitionSpec as P

NFFT = 512
HOP = 160
MELS = 80
BINS = NFFT // 2 + 1
LANES = 128
MICS = 8
PAD_BINS = -(-BINS // LANES) * LANES
TILES = PAD_BINS // LANES
HALO = 3
LEAD = 512
TAIL = 384
STATS = 2 * MICS * MICS
SPAN = 42

loading = 0.03
epsilon = 1e-06
sample_rate = 16000.0


def passed_along(block, axis, distance):
    devices = range(lax.axis_size(axis))
    route = [(i - distance, i) for i in devices if i - distance in devices]
    return lax.ppermute(block, axis, route)


def dft_table():
    n = np.arange(NFFT)
    f = np.arange(BINS)
    phase = 2.0 * math.pi * ((n[:, None] * f[None, :]) % NFFT) / NFFT
    window = 0.5 - 0.5 * np.cos(2.0 * math.pi * n / NFFT)
    table = np.zeros((NFFT, 2, PAD_BINS), np.float32)
    table[:, 0, :BINS] = window[:, None] * np.cos(phase)
    table[:, 1, :BINS] = -window[:, None] * np.sin(phase)
    return jnp.asarray(table.reshape(NFFT, 2 * PAD_BINS)).astype(jnp.bfloat16)


def mel_bank():
    mel_top = 2595.0 * math.log10(1.0 + sample_rate / 2.0 / 700.0)
    points = np.arange(MELS + 2) * (mel_top / (MELS + 1))
    edges = 700.0 * (np.power(10.0, points / 2595.0) - 1.0)
    freq = np.arange(BINS) * (sample_rate / 2.0 / (BINS - 1))
    lower, centre, upper = edges[:-2], edges[1:-1], edges[2:]
    rising = (freq[:, None] - lower[None, :]) / (centre - lower)[None, :]
    falling = (upper[None, :] - freq[:, None]) / (upper - centre)[None, :]
    return np.maximum(np.minimum(rising, falling), 0.0).astype(np.float32)


def packed_mel_bank():
    bank = mel_bank()
    packed = np.zeros((PAD_BINS, 2, LANES), np.float32)
    for half in range(2):
        part = bank[:, half * 40 : half * 40 + SPAN]
        for copy in range(3):
            packed[:BINS, half, copy * SPAN : copy * SPAN + part.shape[1]] = part
    return jnp.asarray(packed.reshape(PAD_BINS, 2 * LANES))


def packed_conv1(conv1_w):
    rows = []
    for shift_t in range(3):
        rows.append(conv1_w[3 * shift_t : 3 * shift_t + 3])
        rows.append(jnp.zeros((SPAN - 3, conv1_w.shape[1]), conv1_w.dtype))
    rows.append(jnp.zeros((LANES - 3 * SPAN, conv1_w.shape[1]), conv1_w.dtype))
    return jnp.concatenate(rows, axis=0)


def stats_kernel(frames, prev_ref, wave_ref, next_ref, masks_ref, valid_ref, table_ref, spec_ref, mine_ref, theirs_ref, framed_ref, weight_ref):
    position = lax.axis_index("tm")
    span = frames + HALO
    extended = jnp.concatenate(
        [prev_ref[...].astype(jnp.float32), wave_ref[...].astype(jnp.float32), next_ref[...].astype(jnp.float32)], axis=1
    )
    width = extended.shape[1]
    rolled = {}
    for frame in range(span):
        start = LEAD - HALO * HOP + frame * HOP
        base, shift = start // LANES * LANES, start % LANES
        if shift not in rolled:
            rolled[shift] = extended if shift == 0 else pltpu.roll(extended, width - shift, 1)
        framed_ref[MICS * frame : MICS * (frame + 1), :] = rolled[shift][:, base : base + NFFT]
    rest = framed_ref.shape[0] - MICS * span
    framed_ref[MICS * span :, :] = jnp.zeros((rest, NFFT), jnp.float32)
    spec = jnp.dot(framed_ref[...].astype(jnp.bfloat16), table_ref[...], preferred_element_type=jnp.float32)
    for tile in range(2 * TILES):
        spec_ref[tile] = spec[:, tile * LANES : (tile + 1) * LANES]

    row = lax.broadcasted_iota(jnp.int32, (frames, 1), 0)
    live = jnp.where(position * frames + row < valid_ref[0], 1.0 / 255.0, 0.0)
    weight_ref[TILES - 1] = jnp.zeros((2, frames, LANES), jnp.float32)
    for k in range(2):
        weight = masks_ref[k].astype(jnp.float32) * live
        for tile in range(TILES):
            kept_lanes = min(LANES, BINS - tile * LANES)
            weight_ref[tile, k, :, :kept_lanes] = weight[:, tile * LANES : tile * LANES + kept_lanes]

    low = lax.broadcasted_iota(jnp.int32, (MICS, LANES), 0) < MICS // 2
    core = position % 2
    for slot, tile in enumerate((core, 1 - core, TILES - 1)):

        def add_frames(group, sums):
            first = pl.multiple_of(group * MICS, MICS)
            weights = [weight_ref[tile, k, pl.ds(first, MICS), :] for k in range(2)]
            for frame in range(MICS):
                rows = pl.ds(pl.multiple_of((first + frame + HALO) * MICS, MICS), MICS)
                x_re = spec_ref[tile, rows, :]
                x_im = spec_ref[TILES + tile, rows, :]
                pairs = [x_re * x_re + x_im * x_im]
                for shift in range(1, MICS // 2 + 1):
                    y_re = pltpu.roll(x_re, MICS - shift, 0)
                    y_im = pltpu.roll(x_im, MICS - shift, 0)
                    pairs.append(x_re * y_re + x_im * y_im)
                    pairs.append(x_im * y_re - x_re * y_im)
                out = []
                for k in range(2):
                    w = jnp.broadcast_to(weights[k][frame : frame + 1], (MICS, LANES))
                    out.extend(sums[k * len(pairs) + i] + w * pair for i, pair in enumerate(pairs))
                sums = tuple(out)
            return sums

        zero = jnp.zeros((MICS, LANES), jnp.float32)
        sums = lax.fori_loop(0, frames // MICS, add_frames, (zero,) * 18)
        kept = []
        for k in range(2):
            own = sums[9 * k : 9 * k + 9]
            kept.extend(list(own[:7]) + [jnp.where(low, own[7], own[8])])
        kept = jnp.concatenate(kept, axis=0)
        if slot == 0:
            mine_ref[:STATS, :] = kept
        elif slot == 1:
            theirs_ref[:STATS, :] = kept
        else:
            last_bin = jnp.transpose(kept)[:MICS]
            mine_ref[STATS:, :] = last_bin
            theirs_ref[STATS:, :] = last_bin


def columns_of(kept, sub):
    low = sub < MICS // 2
    diag_re = [kept[0], kept[1], kept[3], kept[5]]
    diag_im = [jnp.zeros_like(kept[0]), kept[2], kept[4], kept[6]]
    turned = pltpu.roll(kept[7], MICS // 2, 0)
    diag_re.append(jnp.where(low, kept[7], turned))
    diag_im.append(jnp.where(low, -turned, kept[7]))
    for shift in range(MICS // 2 + 1, MICS):
        diag_re.append(pltpu.roll(diag_re[MICS - shift], MICS - shift, 0))
        diag_im.append(-pltpu.roll(diag_im[MICS - shift], MICS - shift, 0))
    columns = []
    for n in range(MICS):
        re, im = diag_re[n], diag_im[n]
        for m in range(1, MICS):
            re = jnp.where(sub == m, diag_re[(n - m) % MICS], re)
            im = jnp.where(sub == m, diag_im[(n - m) % MICS], im)
        columns.append((re, im))
    return columns


def beams_of(stats, ref_mic):
    sub = lax.broadcasted_iota(jnp.int32, stats[0].shape, 0)
    answer = columns_of(stats[:MICS], sub)
    matrix = columns_of(stats[MICS:], sub)
    spread = jnp.sum(stats[MICS], axis=0, keepdims=True)
    ridge = loading * spread / MICS + epsilon
    matrix = [(jnp.where(sub == n, re + ridge, re), im) for n, (re, im) in enumerate(matrix)]
    for pivot in range(MICS):
        col_re, col_im = matrix[pivot]
        pivot_re = col_re[pivot : pivot + 1]
        pivot_im = col_im[pivot : pivot + 1]
        modulus = pivot_re * pivot_re + pivot_im * pivot_im
        inverse_re = pivot_re / modulus
        inverse_im = -pivot_im / modulus

        def eliminated(column):
            re, im = column
            row_re, row_im = re[pivot : pivot + 1], im[pivot : pivot + 1]
            lead_re = row_re * inverse_re - row_im * inverse_im
            lead_im = row_re * inverse_im + row_im * inverse_re
            return (
                jnp.where(sub == pivot, lead_re, re - (col_re * lead_re - col_im * lead_im)),
                jnp.where(sub == pivot, lead_im, im - (col_re * lead_im + col_im * lead_re)),
            )

        matrix = [eliminated(c) if n > pivot else c for n, c in enumerate(matrix)]
        answer = [eliminated(c) for c in answer]
    trace = answer[0][0][0:1]
    beam_re, beam_im = answer[0]
    for n in range(1, MICS):
        trace = trace + answer[n][0][n : n + 1]
        beam_re = jnp.where(ref_mic == n, answer[n][0], beam_re)
        beam_im = jnp.where(ref_mic == n, answer[n][1], beam_im)
    scale = 1.0 / (trace + epsilon)
    return beam_re * scale, beam_im * scale


def solve_kernel(stats_ref, ref_mic_ref, beam_ref, last_ref):
    blank = jnp.zeros((LANES - MICS, LANES), jnp.float32)
    last_bin = jnp.transpose(jnp.concatenate([stats_ref[STATS:, :], blank], axis=0))
    for out_ref, stats in ((beam_ref, stats_ref[:STATS, :]), (last_ref, last_bin)):
        kept = [stats[i * MICS : (i + 1) * MICS] for i in range(2 * MICS)]
        beam_re, beam_im = beams_of(kept, ref_mic_ref[0])
        out_ref[:MICS, :] = beam_re
        out_ref[MICS:, :] = beam_im


def stem_kernel(frames, mine_ref, theirs_ref, last_ref, spec_ref, valid_ref, bank_ref, conv1_w_ref, conv1_b_ref, conv2_w_ref, conv2_b_ref, proj_w_ref, proj_b_ref, out_ref, power_ref, logmel_ref):
    position = lax.axis_index("tm")
    valid = valid_ref[0]
    quarter = frames // 4
    span = power_ref.shape[1]
    core = position % 2
    for beam_ref, tile in ((mine_ref, core), (theirs_ref, 1 - core), (last_ref, TILES - 1)):
        beam_re, beam_im = beam_ref[:MICS, :], beam_ref[MICS:, :]
        for group in range(span // MICS):
            sum_re = sum_im = None
            for m in range(MICS):
                rows = pl.ds(group * MICS * MICS + m, MICS, stride=MICS)
                x_re, x_im = spec_ref[tile, rows, :], spec_ref[TILES + tile, rows, :]
                b_re, b_im = beam_re[m : m + 1], beam_im[m : m + 1]
                part_re = b_re * x_re + b_im * x_im
                part_im = b_re * x_im - b_im * x_re
                sum_re = part_re if sum_re is None else sum_re + part_re
                sum_im = part_im if sum_im is None else sum_im + part_im
            power_ref[tile, group * MICS : (group + 1) * MICS, :] = sum_re * sum_re + sum_im * sum_im
    power = jnp.concatenate([power_ref[tile] for tile in range(TILES)], axis=1)
    mel = jnp.dot(power, bank_ref[...], precision=lax.Precision.HIGHEST, preferred_element_type=jnp.float32)
    time = position * frames - HALO + lax.broadcasted_iota(jnp.int32, (span, 1), 0)
    live = (time >= 0) & (time < valid)
    logmel = jnp.where(live, jnp.log(mel + epsilon), 0.0)
    logmel = logmel.astype(jnp.bfloat16).astype(jnp.float32)
    for half in range(2):
        logmel_ref[half] = logmel[:, half * LANES : (half + 1) * LANES]

    q_first = (MELS - 3) // 2 + 1
    q_second = (q_first - 3) // 2 + 1
    order = list(range(0, q_first, 2)) + list(range(1, q_first, 2))
    evens = (q_first + 1) // 2
    lane = lax.broadcasted_iota(jnp.int32, (quarter, LANES), 1)
    row = lax.broadcasted_iota(jnp.int32, (quarter, 1), 0)
    windows = []
    for tap in range(3):
        packs = []
        for half in range(2):
            rows = [logmel_ref[half, pl.ds(2 * tap + a, quarter, stride=4), :] for a in range(3)]
            packs.append(jnp.where(lane < SPAN, rows[0], jnp.where(lane < 2 * SPAN, rows[1], rows[2])))
        patches = []
        for q in order:
            half, shift = (0, 2 * q) if q < 20 else (1, 2 * q - 40)
            patches.append(packs[half] if shift == 0 else pltpu.roll(packs[half], LANES - shift, 1))
        patches = jnp.concatenate(patches, axis=0).astype(jnp.bfloat16)
        layer = jnp.dot(patches, conv1_w_ref[...], preferred_element_type=jnp.float32) + conv1_b_ref[...]
        layer = jnp.maximum(layer, 0.0)
        if tap == 0:
            keep = jnp.concatenate([row + 2 * quarter * position >= 1] * q_first, axis=0)
            layer = jnp.where(keep, layer, 0.0)
        layer = layer.astype(jnp.bfloat16)
        count = quarter * q_second
        windows.append(layer[:count])
        windows.append(layer[quarter * evens : quarter * evens + count])
        windows.append(layer[quarter : quarter + count])
    second = jnp.dot(jnp.concatenate(windows, axis=1), conv2_w_ref[...], preferred_element_type=jnp.float32)
    second = jnp.maximum(second + conv2_b_ref[...], 0.0).astype(jnp.bfloat16)
    flat = jnp.concatenate([second[quarter * r : quarter * (r + 1)] for r in range(q_second)], axis=1)
    features = jnp.dot(flat, proj_w_ref[...], preferred_element_type=jnp.float32) + proj_b_ref[...]
    features = jnp.where(position * frames + 4 * row < valid, features, 0.0)
    out_ref[0] = features.astype(jnp.bfloat16)


def flipped(block, axis, step):
    size = lax.axis_size(axis)
    return lax.ppermute(block, axis, [(i, i ^ step) for i in range(size)])


def summed_over_chips(block, axis):
    size = lax.axis_size(axis)
    if size & (size - 1):
        return lax.psum(block, axis, axis_index_groups=[list(range(c, size, 2)) for c in range(2)])
    step = 2
    while step < size:
        block = block + flipped(block, axis, step)
        step *= 2
    return block


def per_device(waveform, masks, valid, ref_mic, conv1_w, conv1_b, conv2_w, conv2_b, proj_w, proj_b):
    frames = masks.shape[1]
    channels = conv1_w.shape[1]
    width = proj_w.shape[1]
    rows = -(-(frames + HALO) // MICS) * MICS
    prev_rim = passed_along(waveform[:, -LEAD:], "tm", 1)
    next_rim = passed_along(waveform[:, :TAIL], "tm", -1)
    vmem = pl.BlockSpec(memory_space=pltpu.VMEM)
    smem = pl.BlockSpec(memory_space=pltpu.SMEM)
    params = pltpu.CompilerParams(vmem_limit_bytes=16 * 1024 * 1024)
    spec, mine, theirs = pl.pallas_call(
        functools.partial(stats_kernel, frames),
        out_shape=(
            jax.ShapeDtypeStruct((2 * TILES, rows * MICS, LANES), jnp.float32),
            jax.ShapeDtypeStruct((STATS + MICS, LANES), jnp.float32),
            jax.ShapeDtypeStruct((STATS + MICS, LANES), jnp.float32),
        ),
        in_specs=[vmem, vmem, vmem, vmem, smem, vmem],
        out_specs=(vmem, vmem, vmem),
        scratch_shapes=[
            pltpu.VMEM((rows * MICS, NFFT), jnp.float32),
            pltpu.VMEM((TILES, 2, frames, LANES), jnp.float32),
        ],
        compiler_params=params,
        name="stats",
    )(prev_rim, waveform, next_rim, masks, valid, dft_table())
    stats = summed_over_chips(mine + flipped(theirs, "tm", 1), "tm")
    beam = jax.ShapeDtypeStruct((2 * MICS, LANES), jnp.float32)
    beam_mine, beam_last = pl.pallas_call(
        solve_kernel,
        out_shape=(beam, beam),
        in_specs=[vmem, smem],
        out_specs=(vmem, vmem),
        compiler_params=params,
        name="solve",
    )(stats, ref_mic)
    beam_theirs = flipped(beam_mine, "tm", 1)
    return pl.pallas_call(
        functools.partial(stem_kernel, frames),
        out_shape=jax.ShapeDtypeStruct((1, frames // 4, width), jnp.bfloat16),
        in_specs=[vmem] * 4 + [smem] + [vmem] * 7,
        out_specs=vmem,
        scratch_shapes=[
            pltpu.VMEM((TILES, rows, LANES), jnp.float32),
            pltpu.VMEM((2, rows, LANES), jnp.float32),
        ],
        compiler_params=params,
        name="stem",
    )(
        beam_mine,
        beam_theirs,
        beam_last,
        spec,
        valid,
        packed_mel_bank(),
        packed_conv1(conv1_w),
        conv1_b[None],
        conv2_w.reshape(-1, channels),
        conv2_b[None],
        proj_w,
        proj_b[None],
    )


def solution(mesh):
    return jax.shard_map(
        per_device,
        mesh=mesh,
        in_specs=(
            P(None, ("meet", "tm")),
            P(None, ("meet", "tm"), None),
            P("meet"),
            P("meet"),
            P(),
            P(),
            P(),
            P(),
            P(),
            P(),
        ),
        out_specs=P(None, ("meet", "tm"), None),
        check_vma=False,
    )
```

```python
import functools
import math

import jax
import jax.numpy as jnp
import numpy as np
from jax import lax
from jax.experimental import pallas as pl
from jax.experimental.pallas import tpu as pltpu
from jax.sharding import PartitionSpec as P

NFFT = 512
HOP = 160
MELS = 80
BINS = NFFT // 2 + 1
LANES = 128
MICS = 8
PAD_BINS = -(-BINS // LANES) * LANES
TILES = PAD_BINS // LANES
HALO = 3
LEAD = 512
TAIL = 384
STATS = 2 * MICS * MICS
SPAN = 42

loading = 0.03
epsilon = 1e-06
sample_rate = 16000.0


def dft_table():
    n = np.arange(NFFT)
    f = np.arange(BINS)
    phase = 2.0 * math.pi * ((n[:, None] * f[None, :]) % NFFT) / NFFT
    window = 0.5 - 0.5 * np.cos(2.0 * math.pi * n / NFFT)
    table = np.zeros((NFFT, 2, PAD_BINS), np.float32)
    table[:, 0, :BINS] = window[:, None] * np.cos(phase)
    table[:, 1, :BINS] = -window[:, None] * np.sin(phase)
    return jnp.asarray(table.reshape(NFFT, 2 * PAD_BINS)).astype(jnp.bfloat16)


def mel_bank():
    mel_top = 2595.0 * math.log10(1.0 + sample_rate / 2.0 / 700.0)
    points = np.arange(MELS + 2) * (mel_top / (MELS + 1))
    edges = 700.0 * (np.power(10.0, points / 2595.0) - 1.0)
    freq = np.arange(BINS) * (sample_rate / 2.0 / (BINS - 1))
    lower, centre, upper = edges[:-2], edges[1:-1], edges[2:]
    rising = (freq[:, None] - lower[None, :]) / (centre - lower)[None, :]
    falling = (upper[None, :] - freq[:, None]) / (upper - centre)[None, :]
    return np.maximum(np.minimum(rising, falling), 0.0).astype(np.float32)


def packed_mel_bank():
    bank = mel_bank()
    packed = np.zeros((PAD_BINS, 2, LANES), np.float32)
    for half in range(2):
        part = bank[:, half * 40 : half * 40 + SPAN]
        for copy in range(3):
            packed[:BINS, half, copy * SPAN : copy * SPAN + part.shape[1]] = part
    return jnp.asarray(packed.reshape(PAD_BINS, 2 * LANES))


def cyclic_pairs(x_re, x_im):
    pairs = [x_re * x_re + x_im * x_im]
    for shift in range(1, MICS // 2 + 1):
        y_re = pltpu.roll(x_re, MICS - shift, 0)
        y_im = pltpu.roll(x_im, MICS - shift, 0)
        pairs.append(x_re * y_re + x_im * y_im)
        pairs.append(x_im * y_re - x_re * y_im)
    return pairs


def add_frame(sums, x_re, x_im, weights):
    pairs = cyclic_pairs(x_re, x_im)
    out = []
    for k in range(2):
        w = jnp.broadcast_to(weights[k], (MICS, LANES))
        out.extend(sums[k * len(pairs) + i] + w * pair for i, pair in enumerate(pairs))
    return tuple(out)


def kept_sums(sums):
    low = lax.broadcasted_iota(jnp.int32, (MICS, LANES), 0) < MICS // 2
    kept = []
    for k in range(2):
        own = sums[9 * k : 9 * k + 9]
        kept.extend(list(own[:7]) + [jnp.where(low, own[7], own[8])])
    return jnp.concatenate(kept, axis=0)


def slot_tiles(position):
    core = position % 2
    return core, 1 - core, TILES - 1


def rims_kernel(wave_ref, beside_ref, across_ref, sem):
    even = lax.axis_index("tm") % 2 == 0
    last = wave_ref.shape[1] - LEAD
    copies = []
    for i, (out_ref, start) in enumerate(((beside_ref, jnp.where(even, last, 0)), (across_ref, jnp.where(even, 0, last)))):
        lanes = pl.ds(pl.multiple_of(start, LANES), LEAD)
        copies.append(pltpu.make_async_copy(wave_ref.at[:, lanes], out_ref, sem.at[i]))
        copies[-1].start()
    for copy in copies:
        copy.wait()


def stats_kernel(frames, wave_hbm, masks_hbm, table_hbm, valid_ref, spec_ref, kept_ref, edge_weight_ref, table_ref, wave_ref, masks_ref, framed_ref, weight_ref, sem):
    copies = [
        pltpu.make_async_copy(source, target, sem.at[i])
        for i, (source, target) in enumerate(((wave_hbm, wave_ref), (table_hbm, table_ref), (masks_hbm, masks_ref)))
    ]
    for copy in copies:
        copy.start()
    position = lax.axis_index("tm")
    copies[0].wait()
    wave = wave_ref[...].astype(jnp.float32)
    width = wave.shape[1]
    rolled = {}
    for frame in range(frames - HALO):
        base, shift = frame * HOP // LANES * LANES, frame * HOP % LANES
        if shift not in rolled:
            rolled[shift] = wave if shift == 0 else pltpu.roll(wave, width - shift, 1)
        framed_ref[MICS * frame : MICS * (frame + 1), :] = rolled[shift][:, base : base + NFFT]
    framed_ref[MICS * (frames - HALO) :, :] = jnp.zeros((MICS * HALO, NFFT), jnp.float32)
    copies[1].wait()
    spec = jnp.dot(framed_ref[...].astype(jnp.bfloat16), table_ref[...], preferred_element_type=jnp.float32)
    for tile in range(2 * TILES):
        spec_ref[tile] = spec[:, tile * LANES : (tile + 1) * LANES]

    copies[2].wait()
    row = lax.broadcasted_iota(jnp.int32, (frames, 1), 0)
    live = jnp.where(position * frames + row < valid_ref[0], 1.0 / 255.0, 0.0)
    weight_ref[TILES - 1] = jnp.zeros((2, frames, LANES), jnp.float32)
    for k in range(2):
        weight = masks_ref[k].astype(jnp.float32) * live
        for tile in range(TILES):
            kept_lanes = min(LANES, BINS - tile * LANES)
            weight_ref[tile, k, :, :kept_lanes] = weight[:, tile * LANES : tile * LANES + kept_lanes]
    edge_weight_ref[...] = weight_ref[:, :, frames - MICS :, :]

    for slot, tile in enumerate(slot_tiles(position)):

        def add_frames(group, sums):
            first = pl.multiple_of(group * MICS, MICS)
            weights = [weight_ref[tile, k, pl.ds(first, MICS), :] for k in range(2)]
            for frame in range(MICS):
                rows = pl.ds(pl.multiple_of((first + frame) * MICS, MICS), MICS)
                sums = add_frame(
                    sums, spec_ref[tile, rows, :], spec_ref[TILES + tile, rows, :], [w[frame : frame + 1] for w in weights]
                )
            return sums

        zero = jnp.zeros((MICS, LANES), jnp.float32)
        kept_ref[slot] = kept_sums(lax.fori_loop(0, frames // MICS, add_frames, (zero,) * 18))


def edges_kernel(devices, own0_ref, own1_ref, got0_ref, got1_ref, table_ref, edge_weight_ref, kept_ref, spec_ref, mine_ref, theirs_ref, framed_ref):
    position = lax.axis_index("tm")
    even = position % 2 == 0
    own = [own0_ref[...].astype(jnp.float32), own1_ref[...].astype(jnp.float32)]
    got = [got0_ref[...].astype(jnp.float32), got1_ref[...].astype(jnp.float32)]
    head, tail = jnp.where(even, own[1], own[0]), jnp.where(even, own[0], own[1])
    prev, after = jnp.where(even, got[1], got[0]), jnp.where(even, got[0], got[1])
    prev = jnp.where(position > 0, prev, 0.0)
    after = jnp.where(position < devices - 1, after, 0.0)
    joined = jnp.concatenate(
        [jnp.concatenate([prev, head[:, :TAIL]], axis=1), jnp.concatenate([tail, after[:, :TAIL]], axis=1)], axis=0
    )
    for i in range(HALO):
        start = LEAD - HALO * HOP + i * HOP
        base, shift = start // LANES * LANES, start % LANES
        turned = joined if shift == 0 else pltpu.roll(joined, joined.shape[1] - shift, 1)
        framed_ref[2 * MICS * i : 2 * MICS * (i + 1), :] = turned[:, base : base + NFFT]
    used = 2 * MICS * HALO
    framed_ref[used:, :] = jnp.zeros((framed_ref.shape[0] - used, NFFT), jnp.float32)
    spec = jnp.dot(framed_ref[...].astype(jnp.bfloat16), table_ref[...], preferred_element_type=jnp.float32)
    for tile in range(2 * TILES):
        spec_ref[tile] = spec[:, tile * LANES : (tile + 1) * LANES]
    for slot, tile in enumerate(slot_tiles(position)):
        sums = (jnp.zeros((MICS, LANES), jnp.float32),) * 18
        for i in range(HALO):
            rows = slice((2 * i + 1) * MICS, (2 * i + 2) * MICS)
            at = MICS - HALO + i
            weights = [edge_weight_ref[tile, k, at : at + 1, :] for k in range(2)]
            sums = add_frame(sums, spec_ref[tile, rows, :], spec_ref[TILES + tile, rows, :], weights)
        total = kept_ref[slot] + kept_sums(sums)
        if slot == 0:
            mine_ref[:STATS, :] = total
        elif slot == 1:
            theirs_ref[:STATS, :] = total
        else:
            last_bin = jnp.transpose(total)[:MICS]
            mine_ref[STATS:, :] = last_bin
            theirs_ref[STATS:, :] = last_bin


def columns_of(kept, sub):
    low = sub < MICS // 2
    diag_re = [kept[0], kept[1], kept[3], kept[5]]
    diag_im = [jnp.zeros_like(kept[0]), kept[2], kept[4], kept[6]]
    turned = pltpu.roll(kept[7], MICS // 2, 0)
    diag_re.append(jnp.where(low, kept[7], turned))
    diag_im.append(jnp.where(low, -turned, kept[7]))
    for shift in range(MICS // 2 + 1, MICS):
        diag_re.append(pltpu.roll(diag_re[MICS - shift], MICS - shift, 0))
        diag_im.append(-pltpu.roll(diag_im[MICS - shift], MICS - shift, 0))
    columns = []
    for n in range(MICS):
        re, im = diag_re[n], diag_im[n]
        for m in range(1, MICS):
            re = jnp.where(sub == m, diag_re[(n - m) % MICS], re)
            im = jnp.where(sub == m, diag_im[(n - m) % MICS], im)
        columns.append((re, im))
    return columns


def beams_of(stats, ref_mic):
    sub = lax.broadcasted_iota(jnp.int32, stats[0].shape, 0)
    answer = columns_of(stats[:MICS], sub)
    matrix = columns_of(stats[MICS:], sub)
    spread = jnp.sum(stats[MICS], axis=0, keepdims=True)
    ridge = loading * spread / MICS + epsilon
    matrix = [(jnp.where(sub == n, re + ridge, re), im) for n, (re, im) in enumerate(matrix)]
    for pivot in range(MICS):
        col_re, col_im = matrix[pivot]
        pivot_re = col_re[pivot : pivot + 1]
        pivot_im = col_im[pivot : pivot + 1]
        modulus = pivot_re * pivot_re + pivot_im * pivot_im
        inverse_re = pivot_re / modulus
        inverse_im = -pivot_im / modulus

        def eliminated(column):
            re, im = column
            row_re, row_im = re[pivot : pivot + 1], im[pivot : pivot + 1]
            lead_re = row_re * inverse_re - row_im * inverse_im
            lead_im = row_re * inverse_im + row_im * inverse_re
            return (
                jnp.where(sub == pivot, lead_re, re - (col_re * lead_re - col_im * lead_im)),
                jnp.where(sub == pivot, lead_im, im - (col_re * lead_im + col_im * lead_re)),
            )

        matrix = [eliminated(c) if n > pivot else c for n, c in enumerate(matrix)]
        answer = [eliminated(c) for c in answer]
    trace = answer[0][0][0:1]
    beam_re, beam_im = answer[0]
    for n in range(1, MICS):
        trace = trace + answer[n][0][n : n + 1]
        beam_re = jnp.where(ref_mic == n, answer[n][0], beam_re)
        beam_im = jnp.where(ref_mic == n, answer[n][1], beam_im)
    scale = 1.0 / (trace + epsilon)
    return beam_re * scale, beam_im * scale


def solve_kernel(stats_ref, ref_mic_ref, beam_ref, last_ref):
    blank = jnp.zeros((LANES - MICS, LANES), jnp.float32)
    last_bin = jnp.transpose(jnp.concatenate([stats_ref[STATS:, :], blank], axis=0))
    for out_ref, stats in ((beam_ref, stats_ref[:STATS, :]), (last_ref, last_bin)):
        kept = [stats[i * MICS : (i + 1) * MICS] for i in range(2 * MICS)]
        beam_re, beam_im = beams_of(kept, ref_mic_ref[0])
        out_ref[:MICS, :] = beam_re
        out_ref[MICS:, :] = beam_im


def stem_kernel(frames, mine_ref, theirs_ref, last_ref, spec_ref, edge_spec_ref, valid_ref, bank_ref, conv1_w_ref, conv1_b_ref, conv2_w_hbm, conv2_b_ref, proj_w_hbm, proj_b_ref, out_ref, power_ref, logmel_ref, conv1_ref, conv2_w_ref, proj_w_ref, sem):
    copies = [
        pltpu.make_async_copy(source, target, sem.at[i])
        for i, (source, target) in enumerate(((conv2_w_hbm, conv2_w_ref), (proj_w_hbm, proj_w_ref)))
    ]
    for copy in copies:
        copy.start()
    position = lax.axis_index("tm")
    valid = valid_ref[0]
    quarter = frames // 4
    channels = conv1_w_ref.shape[1]
    conv1_ref[...] = jnp.zeros((LANES, channels), jnp.float32)
    for shift_t in range(3):
        conv1_ref[SPAN * shift_t : SPAN * shift_t + 3, :] = conv1_w_ref[3 * shift_t : 3 * shift_t + 3, :].astype(jnp.float32)
    conv1 = conv1_ref[...].astype(jnp.bfloat16)

    groups = frames // MICS
    for beam_ref, tile in zip((mine_ref, theirs_ref, last_ref), slot_tiles(position)):
        beam_re, beam_im = beam_ref[:MICS, :], beam_ref[MICS:, :]
        for group in range(groups + 1):
            from_ref, first = (spec_ref, group * MICS * MICS) if group < groups else (edge_spec_ref, 0)
            sum_re = sum_im = None
            for m in range(MICS):
                rows = pl.ds(first + m, MICS, stride=MICS)
                x_re, x_im = from_ref[tile, rows, :], from_ref[TILES + tile, rows, :]
                b_re, b_im = beam_re[m : m + 1], beam_im[m : m + 1]
                part_re = b_re * x_re + b_im * x_im
                part_im = b_re * x_im - b_im * x_re
                sum_re = part_re if sum_re is None else sum_re + part_re
                sum_im = part_im if sum_im is None else sum_im + part_im
            power_ref[tile, group * MICS : (group + 1) * MICS, :] = sum_re * sum_re + sum_im * sum_im
    power = jnp.concatenate([power_ref[tile] for tile in range(TILES)], axis=1)
    mel = jnp.dot(power, bank_ref[...], precision=lax.Precision.HIGHEST, preferred_element_type=jnp.float32)
    row = lax.broadcasted_iota(jnp.int32, (frames + MICS, 1), 0)
    edge = (row - frames) // 2 + jnp.where((row - frames) % 2 == 0, -HALO, frames - HALO)
    time = position * frames + jnp.where(row < frames, row, edge)
    live = (time >= 0) & (time < valid)
    logmel = jnp.where(live, jnp.log(mel + epsilon), 0.0)
    logmel = logmel.astype(jnp.bfloat16).astype(jnp.float32)
    for half in range(2):
        part = logmel[:, half * LANES : (half + 1) * LANES]
        logmel_ref[half, HALO : HALO + frames, :] = part[:frames]
        for i in range(HALO):
            logmel_ref[half, i : i + 1, :] = part[frames + 2 * i : frames + 2 * i + 1]
            logmel_ref[half, frames + i : frames + i + 1, :] = part[frames + 2 * i + 1 : frames + 2 * i + 2]

    q_first = (MELS - 3) // 2 + 1
    q_second = (q_first - 3) // 2 + 1
    order = list(range(0, q_first, 2)) + list(range(1, q_first, 2))
    evens = (q_first + 1) // 2
    lane = lax.broadcasted_iota(jnp.int32, (quarter, LANES), 1)
    row = lax.broadcasted_iota(jnp.int32, (quarter, 1), 0)
    windows = []
    for tap in range(3):
        packs = []
        for half in range(2):
            rows = [logmel_ref[half, pl.ds(2 * tap + a, quarter, stride=4), :] for a in range(3)]
            packs.append(jnp.where(lane < SPAN, rows[0], jnp.where(lane < 2 * SPAN, rows[1], rows[2])))
        patches = []
        for q in order:
            half, shift = (0, 2 * q) if q < 20 else (1, 2 * q - 40)
            patches.append(packs[half] if shift == 0 else pltpu.roll(packs[half], LANES - shift, 1))
        patches = jnp.concatenate(patches, axis=0).astype(jnp.bfloat16)
        layer = jnp.dot(patches, conv1, preferred_element_type=jnp.float32) + conv1_b_ref[...]
        layer = jnp.maximum(layer, 0.0)
        if tap == 0:
            keep = jnp.concatenate([row + 2 * quarter * position >= 1] * q_first, axis=0)
            layer = jnp.where(keep, layer, 0.0)
        layer = layer.astype(jnp.bfloat16)
        count = quarter * q_second
        windows.append(layer[:count])
        windows.append(layer[quarter * evens : quarter * evens + count])
        windows.append(layer[quarter : quarter + count])
    copies[0].wait()
    second = jnp.dot(jnp.concatenate(windows, axis=1), conv2_w_ref[...], preferred_element_type=jnp.float32)
    second = jnp.maximum(second + conv2_b_ref[...], 0.0).astype(jnp.bfloat16)
    flat = jnp.concatenate([second[quarter * r : quarter * (r + 1)] for r in range(q_second)], axis=1)
    copies[1].wait()
    features = jnp.dot(flat, proj_w_ref[...], preferred_element_type=jnp.float32) + proj_b_ref[...]
    features = jnp.where(position * frames + 4 * row < valid, features, 0.0)
    out_ref[0] = features.astype(jnp.bfloat16)


def flipped(block, axis, step):
    size = lax.axis_size(axis)
    return lax.ppermute(block, axis, [(i, i ^ step) for i in range(size)])


def summed_over_chips(block, axis):
    size = lax.axis_size(axis)
    if size & (size - 1):
        return lax.psum(block, axis, axis_index_groups=[list(range(c, size, 2)) for c in range(2)])
    step = 2
    while step < size:
        block = block + flipped(block, axis, step)
        step *= 2
    return block


def paired(block, axis, first):
    size = lax.axis_size(axis)
    lower = range(first, size, 2)
    route = [(i, (i + 1) % size) for i in lower] + [((i + 1) % size, i) for i in lower]
    return lax.ppermute(block, axis, route)


def per_device(waveform, masks, valid, ref_mic, conv1_w, conv1_b, conv2_w, conv2_b, proj_w, proj_b):
    frames = masks.shape[1]
    channels = conv1_w.shape[1]
    width = proj_w.shape[1]
    vmem = pl.BlockSpec(memory_space=pltpu.VMEM)
    smem = pl.BlockSpec(memory_space=pltpu.SMEM)
    hbm = pl.BlockSpec(memory_space=pltpu.HBM)
    params = pltpu.CompilerParams(vmem_limit_bytes=20 * 1024 * 1024)
    rim = jax.ShapeDtypeStruct((MICS, LEAD), waveform.dtype)
    beside, across = pl.pallas_call(
        rims_kernel,
        out_shape=(rim, rim),
        in_specs=[hbm],
        out_specs=(vmem, vmem),
        scratch_shapes=[pltpu.SemaphoreType.DMA((2,))],
        compiler_params=params,
        name="rims",
    )(waveform)
    got_across = paired(across, "tm", 1)
    got_beside = paired(beside, "tm", 0)
    table = dft_table()
    stat_block = jax.ShapeDtypeStruct((STATS + MICS, LANES), jnp.float32)
    spec, kept, edge_weight, table = pl.pallas_call(
        functools.partial(stats_kernel, frames),
        out_shape=(
            jax.ShapeDtypeStruct((2 * TILES, frames * MICS, LANES), jnp.float32),
            jax.ShapeDtypeStruct((TILES, STATS, LANES), jnp.float32),
            jax.ShapeDtypeStruct((TILES, 2, MICS, LANES), jnp.float32),
            jax.ShapeDtypeStruct(table.shape, table.dtype),
        ),
        in_specs=[hbm, hbm, hbm, smem],
        out_specs=(vmem,) * 4,
        scratch_shapes=[
            pltpu.VMEM(waveform.shape, waveform.dtype),
            pltpu.VMEM(masks.shape, masks.dtype),
            pltpu.VMEM((frames * MICS, NFFT), jnp.float32),
            pltpu.VMEM((TILES, 2, frames, LANES), jnp.float32),
            pltpu.SemaphoreType.DMA((3,)),
        ],
        compiler_params=params,
        name="stats",
    )(waveform, masks, table, valid)
    edge_spec, mine, theirs = pl.pallas_call(
        functools.partial(edges_kernel, lax.axis_size("tm")),
        out_shape=(jax.ShapeDtypeStruct((2 * TILES, MICS * MICS, LANES), jnp.float32), stat_block, stat_block),
        in_specs=[vmem] * 7,
        out_specs=(vmem,) * 3,
        scratch_shapes=[pltpu.VMEM((MICS * MICS, NFFT), jnp.float32)],
        compiler_params=params,
        name="edges",
    )(beside, across, got_beside, got_across, table, edge_weight, kept)
    stats = summed_over_chips(mine + flipped(theirs, "tm", 1), "tm")
    beam = jax.ShapeDtypeStruct((2 * MICS, LANES), jnp.float32)
    beam_mine, beam_last = pl.pallas_call(
        solve_kernel,
        out_shape=(beam, beam),
        in_specs=[vmem, smem],
        out_specs=(vmem, vmem),
        compiler_params=params,
        name="solve",
    )(stats, ref_mic)
    beam_theirs = flipped(beam_mine, "tm", 1)
    rows = frames + MICS
    return pl.pallas_call(
        functools.partial(stem_kernel, frames),
        out_shape=jax.ShapeDtypeStruct((1, frames // 4, width), jnp.bfloat16),
        in_specs=[vmem] * 5 + [smem] + [vmem] * 3 + [hbm, vmem, hbm, vmem],
        out_specs=vmem,
        scratch_shapes=[
            pltpu.VMEM((TILES, rows, LANES), jnp.float32),
            pltpu.VMEM((2, rows, LANES), jnp.float32),
            pltpu.VMEM((LANES, channels), jnp.float32),
            pltpu.VMEM((9 * channels, channels), conv2_w.dtype),
            pltpu.VMEM(proj_w.shape, proj_w.dtype),
            pltpu.SemaphoreType.DMA((2,)),
        ],
        compiler_params=params,
        name="stem",
    )(
        beam_mine,
        beam_theirs,
        beam_last,
        spec,
        edge_spec,
        valid,
        packed_mel_bank(),
        conv1_w,
        conv1_b[None],
        conv2_w.reshape(-1, channels),
        conv2_b[None],
        proj_w,
        proj_b[None],
    )


def solution(mesh):
    return jax.shard_map(
        per_device,
        mesh=mesh,
        in_specs=(
            P(None, ("meet", "tm")),
            P(None, ("meet", "tm"), None),
            P("meet"),
            P("meet"),
            P(),
            P(),
            P(),
            P(),
            P(),
            P(),
        ),
        out_specs=P(None, ("meet", "tm"), None),
        check_vma=False,
    )
```

```python
import functools
import math

import jax
import jax.numpy as jnp
import numpy as np
from jax import lax
from jax.experimental import pallas as pl
from jax.experimental.pallas import tpu as pltpu
from jax.sharding import PartitionSpec as P

NFFT = 512
HOP = 160
MELS = 80
BINS = NFFT // 2 + 1
LANES = 128
MICS = 8
PAD_BINS = -(-BINS // LANES) * LANES
TILES = PAD_BINS // LANES
HALO = 3
LEAD = 512
TAIL = 384
STATS = 2 * MICS * MICS
SPAN = 42

loading = 0.03
epsilon = 1e-06
sample_rate = 16000.0


def dft_table():
    n = np.arange(NFFT)
    f = np.arange(BINS)
    phase = 2.0 * math.pi * ((n[:, None] * f[None, :]) % NFFT) / NFFT
    window = 0.5 - 0.5 * np.cos(2.0 * math.pi * n / NFFT)
    table = np.zeros((NFFT, 2, PAD_BINS), np.float32)
    table[:, 0, :BINS] = window[:, None] * np.cos(phase)
    table[:, 1, :BINS] = -window[:, None] * np.sin(phase)
    return jnp.asarray(table.reshape(NFFT, 2 * PAD_BINS)).astype(jnp.bfloat16)


def mel_bank():
    mel_top = 2595.0 * math.log10(1.0 + sample_rate / 2.0 / 700.0)
    points = np.arange(MELS + 2) * (mel_top / (MELS + 1))
    edges = 700.0 * (np.power(10.0, points / 2595.0) - 1.0)
    freq = np.arange(BINS) * (sample_rate / 2.0 / (BINS - 1))
    lower, centre, upper = edges[:-2], edges[1:-1], edges[2:]
    rising = (freq[:, None] - lower[None, :]) / (centre - lower)[None, :]
    falling = (upper[None, :] - freq[:, None]) / (upper - centre)[None, :]
    return np.maximum(np.minimum(rising, falling), 0.0).astype(np.float32)


def packed_mel_bank():
    bank = mel_bank()
    packed = np.zeros((PAD_BINS, 2, LANES), np.float32)
    for half in range(2):
        part = bank[:, half * 40 : half * 40 + SPAN]
        for copy in range(3):
            packed[:BINS, half, copy * SPAN : copy * SPAN + part.shape[1]] = part
    return jnp.asarray(packed.reshape(PAD_BINS, 2 * LANES))


def cyclic_pairs(x_re, x_im):
    pairs = [x_re * x_re + x_im * x_im]
    for shift in range(1, MICS // 2 + 1):
        y_re = pltpu.roll(x_re, MICS - shift, 0)
        y_im = pltpu.roll(x_im, MICS - shift, 0)
        pairs.append(x_re * y_re + x_im * y_im)
        pairs.append(x_im * y_re - x_re * y_im)
    return pairs


def add_frame(sums, x_re, x_im, weights):
    pairs = cyclic_pairs(x_re, x_im)
    out = []
    for k in range(2):
        w = jnp.broadcast_to(weights[k], (MICS, LANES))
        out.extend(sums[k * len(pairs) + i] + w * pair for i, pair in enumerate(pairs))
    return tuple(out)


def kept_sums(sums):
    low = lax.broadcasted_iota(jnp.int32, (MICS, LANES), 0) < MICS // 2
    kept = []
    for k in range(2):
        own = sums[9 * k : 9 * k + 9]
        kept.extend(list(own[:7]) + [jnp.where(low, own[7], own[8])])
    return jnp.concatenate(kept, axis=0)


def slot_tiles(position):
    core = position % 2
    return core, 1 - core, TILES - 1


def rims_kernel(wave_ref, beside_ref, across_ref, sem):
    even = lax.axis_index("tm") % 2 == 0
    last = wave_ref.shape[1] - LEAD
    copies = []
    for i, (out_ref, start) in enumerate(((beside_ref, jnp.where(even, last, 0)), (across_ref, jnp.where(even, 0, last)))):
        lanes = pl.ds(pl.multiple_of(start, LANES), LEAD)
        copies.append(pltpu.make_async_copy(wave_ref.at[:, lanes], out_ref, sem.at[i]))
        copies[-1].start()
    for copy in copies:
        copy.wait()


def stats_kernel(frames, wave_hbm, masks_hbm, table_hbm, valid_ref, spec_ref, kept_ref, edge_weight_ref, table_ref, wave_ref, masks_ref, framed_ref, weight_ref, sem):
    copies = [
        pltpu.make_async_copy(source, target, sem.at[i])
        for i, (source, target) in enumerate(((wave_hbm, wave_ref), (table_hbm, table_ref), (masks_hbm, masks_ref)))
    ]
    for copy in copies:
        copy.start()
    position = lax.axis_index("tm")
    copies[0].wait()
    wave = wave_ref[...].astype(jnp.float32)
    width = wave.shape[1]
    rolled = {}
    for frame in range(frames - HALO):
        base, shift = frame * HOP // LANES * LANES, frame * HOP % LANES
        if shift not in rolled:
            rolled[shift] = wave if shift == 0 else pltpu.roll(wave, width - shift, 1)
        framed_ref[MICS * frame : MICS * (frame + 1), :] = rolled[shift][:, base : base + NFFT]
    framed_ref[MICS * (frames - HALO) :, :] = jnp.zeros((MICS * HALO, NFFT), jnp.float32)
    copies[1].wait()
    spec = jnp.dot(framed_ref[...].astype(jnp.bfloat16), table_ref[...], preferred_element_type=jnp.float32)
    for tile in range(2 * TILES):
        spec_ref[tile] = spec[:, tile * LANES : (tile + 1) * LANES]

    copies[2].wait()
    row = lax.broadcasted_iota(jnp.int32, (frames, 1), 0)
    live = jnp.where(position * frames + row < valid_ref[0], 1.0 / 255.0, 0.0)
    weight_ref[TILES - 1] = jnp.zeros((2, frames, LANES), jnp.float32)
    for k in range(2):
        weight = masks_ref[k].astype(jnp.float32) * live
        for tile in range(TILES):
            kept_lanes = min(LANES, BINS - tile * LANES)
            weight_ref[tile, k, :, :kept_lanes] = weight[:, tile * LANES : tile * LANES + kept_lanes]
    edge_weight_ref[...] = weight_ref[:, :, frames - MICS :, :]

    for slot, tile in enumerate(slot_tiles(position)):

        def add_frames(group, sums):
            first = pl.multiple_of(group * MICS, MICS)
            weights = [weight_ref[tile, k, pl.ds(first, MICS), :] for k in range(2)]
            for frame in range(MICS):
                rows = pl.ds(pl.multiple_of((first + frame) * MICS, MICS), MICS)
                sums = add_frame(
                    sums, spec_ref[tile, rows, :], spec_ref[TILES + tile, rows, :], [w[frame : frame + 1] for w in weights]
                )
            return sums

        zero = jnp.zeros((MICS, LANES), jnp.float32)
        kept_ref[slot] = kept_sums(lax.fori_loop(0, frames // MICS, add_frames, (zero,) * 18))


def edges_kernel(devices, own0_ref, own1_ref, got0_ref, got1_ref, table_ref, edge_weight_ref, kept_ref, spec_ref, mine_ref, theirs_ref, framed_ref):
    position = lax.axis_index("tm")
    even = position % 2 == 0
    own = [own0_ref[...].astype(jnp.float32), own1_ref[...].astype(jnp.float32)]
    got = [got0_ref[...].astype(jnp.float32), got1_ref[...].astype(jnp.float32)]
    head, tail = jnp.where(even, own[1], own[0]), jnp.where(even, own[0], own[1])
    prev, after = jnp.where(even, got[1], got[0]), jnp.where(even, got[0], got[1])
    prev = jnp.where(position > 0, prev, 0.0)
    after = jnp.where(position < devices - 1, after, 0.0)
    joined = jnp.concatenate(
        [jnp.concatenate([prev, head[:, :TAIL]], axis=1), jnp.concatenate([tail, after[:, :TAIL]], axis=1)], axis=0
    )
    for i in range(HALO):
        start = LEAD - HALO * HOP + i * HOP
        base, shift = start // LANES * LANES, start % LANES
        turned = joined if shift == 0 else pltpu.roll(joined, joined.shape[1] - shift, 1)
        framed_ref[2 * MICS * i : 2 * MICS * (i + 1), :] = turned[:, base : base + NFFT]
    used = 2 * MICS * HALO
    framed_ref[used:, :] = jnp.zeros((framed_ref.shape[0] - used, NFFT), jnp.float32)
    spec = jnp.dot(framed_ref[...].astype(jnp.bfloat16), table_ref[...], preferred_element_type=jnp.float32)
    for tile in range(2 * TILES):
        spec_ref[tile] = spec[:, tile * LANES : (tile + 1) * LANES]
    for slot, tile in enumerate(slot_tiles(position)):
        sums = (jnp.zeros((MICS, LANES), jnp.float32),) * 18
        for i in range(HALO):
            rows = slice((2 * i + 1) * MICS, (2 * i + 2) * MICS)
            at = MICS - HALO + i
            weights = [edge_weight_ref[tile, k, at : at + 1, :] for k in range(2)]
            sums = add_frame(sums, spec_ref[tile, rows, :], spec_ref[TILES + tile, rows, :], weights)
        total = kept_ref[slot] + kept_sums(sums)
        if slot == 0:
            mine_ref[:STATS, :] = total
        elif slot == 1:
            theirs_ref[:STATS, :] = total
        else:
            last_bin = jnp.transpose(total)[:MICS]
            mine_ref[STATS:, :] = last_bin
            theirs_ref[STATS:, :] = last_bin


def columns_of(kept, sub):
    low = sub < MICS // 2
    diag_re = [kept[0], kept[1], kept[3], kept[5]]
    diag_im = [jnp.zeros_like(kept[0]), kept[2], kept[4], kept[6]]
    turned = pltpu.roll(kept[7], MICS // 2, 0)
    diag_re.append(jnp.where(low, kept[7], turned))
    diag_im.append(jnp.where(low, -turned, kept[7]))
    for shift in range(MICS // 2 + 1, MICS):
        diag_re.append(pltpu.roll(diag_re[MICS - shift], MICS - shift, 0))
        diag_im.append(-pltpu.roll(diag_im[MICS - shift], MICS - shift, 0))
    columns = []
    for n in range(MICS):
        re, im = diag_re[n], diag_im[n]
        for m in range(1, MICS):
            re = jnp.where(sub == m, diag_re[(n - m) % MICS], re)
            im = jnp.where(sub == m, diag_im[(n - m) % MICS], im)
        columns.append((re, im))
    return columns


def beams_of(stats, ref_mic):
    sub = lax.broadcasted_iota(jnp.int32, stats[0].shape, 0)
    answer = columns_of(stats[:MICS], sub)
    matrix = columns_of(stats[MICS:], sub)
    spread = jnp.sum(stats[MICS], axis=0, keepdims=True)
    ridge = loading * spread / MICS + epsilon
    matrix = [(jnp.where(sub == n, re + ridge, re), im) for n, (re, im) in enumerate(matrix)]
    for pivot in range(MICS):
        col_re, col_im = matrix[pivot]
        pivot_re = col_re[pivot : pivot + 1]
        pivot_im = col_im[pivot : pivot + 1]
        modulus = pivot_re * pivot_re + pivot_im * pivot_im
        inverse_re = pivot_re / modulus
        inverse_im = -pivot_im / modulus

        def eliminated(column):
            re, im = column
            row_re, row_im = re[pivot : pivot + 1], im[pivot : pivot + 1]
            lead_re = row_re * inverse_re - row_im * inverse_im
            lead_im = row_re * inverse_im + row_im * inverse_re
            return (
                jnp.where(sub == pivot, lead_re, re - (col_re * lead_re - col_im * lead_im)),
                jnp.where(sub == pivot, lead_im, im - (col_re * lead_im + col_im * lead_re)),
            )

        matrix = [eliminated(c) if n > pivot else c for n, c in enumerate(matrix)]
        answer = [eliminated(c) for c in answer]
    trace = answer[0][0][0:1]
    beam_re, beam_im = answer[0]
    for n in range(1, MICS):
        trace = trace + answer[n][0][n : n + 1]
        beam_re = jnp.where(ref_mic == n, answer[n][0], beam_re)
        beam_im = jnp.where(ref_mic == n, answer[n][1], beam_im)
    scale = 1.0 / (trace + epsilon)
    return beam_re * scale, beam_im * scale


def solve_kernel(stats_ref, ref_mic_ref, beam_ref, last_ref):
    blank = jnp.zeros((LANES - MICS, LANES), jnp.float32)
    last_bin = jnp.transpose(jnp.concatenate([stats_ref[STATS:, :], blank], axis=0))
    for out_ref, stats in ((beam_ref, stats_ref[:STATS, :]), (last_ref, last_bin)):
        kept = [stats[i * MICS : (i + 1) * MICS] for i in range(2 * MICS)]
        beam_re, beam_im = beams_of(kept, ref_mic_ref[0])
        out_ref[:MICS, :] = beam_re
        out_ref[MICS:, :] = beam_im


def stem_kernel(frames, mine_ref, theirs_ref, last_ref, spec_ref, edge_spec_ref, valid_ref, bank_ref, conv1_w_ref, conv1_b_ref, conv2_w_hbm, conv2_b_ref, proj_w_hbm, proj_b_ref, out_ref, power_ref, logmel_ref, conv1_ref, conv2_w_ref, proj_w_ref, sem):
    copies = [
        pltpu.make_async_copy(source, target, sem.at[i])
        for i, (source, target) in enumerate(((conv2_w_hbm, conv2_w_ref), (proj_w_hbm, proj_w_ref)))
    ]
    for copy in copies:
        copy.start()
    position = lax.axis_index("tm")
    valid = valid_ref[0]
    quarter = frames // 4
    channels = conv1_w_ref.shape[1]
    conv1_ref[...] = jnp.zeros((LANES, channels), jnp.float32)
    for shift_t in range(3):
        conv1_ref[SPAN * shift_t : SPAN * shift_t + 3, :] = conv1_w_ref[3 * shift_t : 3 * shift_t + 3, :].astype(jnp.float32)
    conv1 = conv1_ref[...].astype(jnp.bfloat16)

    groups = frames // MICS
    for beam_ref, tile in zip((mine_ref, theirs_ref, last_ref), slot_tiles(position)):
        beam_re, beam_im = beam_ref[:MICS, :], beam_ref[MICS:, :]
        for group in range(groups + 1):
            from_ref, first = (spec_ref, group * MICS * MICS) if group < groups else (edge_spec_ref, 0)
            sum_re = sum_im = None
            for m in range(MICS):
                rows = pl.ds(first + m, MICS, stride=MICS)
                x_re, x_im = from_ref[tile, rows, :], from_ref[TILES + tile, rows, :]
                b_re, b_im = beam_re[m : m + 1], beam_im[m : m + 1]
                part_re = b_re * x_re + b_im * x_im
                part_im = b_re * x_im - b_im * x_re
                sum_re = part_re if sum_re is None else sum_re + part_re
                sum_im = part_im if sum_im is None else sum_im + part_im
            power_ref[tile, group * MICS : (group + 1) * MICS, :] = sum_re * sum_re + sum_im * sum_im
    power = jnp.concatenate([power_ref[tile] for tile in range(TILES)], axis=1)
    mel = jnp.dot(power, bank_ref[...], precision=lax.Precision.HIGHEST, preferred_element_type=jnp.float32)
    row = lax.broadcasted_iota(jnp.int32, (frames + MICS, 1), 0)
    edge = (row - frames) // 2 + jnp.where((row - frames) % 2 == 0, -HALO, frames - HALO)
    time = position * frames + jnp.where(row < frames, row, edge)
    live = (time >= 0) & (time < valid)
    logmel = jnp.where(live, jnp.log(mel + epsilon), 0.0)
    logmel = logmel.astype(jnp.bfloat16).astype(jnp.float32)
    for half in range(2):
        part = logmel[:, half * LANES : (half + 1) * LANES]
        logmel_ref[half, HALO : HALO + frames, :] = part[:frames]
        for i in range(HALO):
            logmel_ref[half, i : i + 1, :] = part[frames + 2 * i : frames + 2 * i + 1]
            logmel_ref[half, frames + i : frames + i + 1, :] = part[frames + 2 * i + 1 : frames + 2 * i + 2]

    q_first = (MELS - 3) // 2 + 1
    q_second = (q_first - 3) // 2 + 1
    order = list(range(0, q_first, 2)) + list(range(1, q_first, 2))
    evens = (q_first + 1) // 2
    lane = lax.broadcasted_iota(jnp.int32, (quarter, LANES), 1)
    row = lax.broadcasted_iota(jnp.int32, (quarter, 1), 0)
    windows = []
    for tap in range(3):
        packs = []
        for half in range(2):
            rows = [logmel_ref[half, pl.ds(2 * tap + a, quarter, stride=4), :] for a in range(3)]
            packs.append(jnp.where(lane < SPAN, rows[0], jnp.where(lane < 2 * SPAN, rows[1], rows[2])))
        patches = []
        for q in order:
            half, shift = (0, 2 * q) if q < 20 else (1, 2 * q - 40)
            patches.append(packs[half] if shift == 0 else pltpu.roll(packs[half], LANES - shift, 1))
        patches = jnp.concatenate(patches, axis=0).astype(jnp.bfloat16)
        layer = jnp.dot(patches, conv1, preferred_element_type=jnp.float32) + conv1_b_ref[...]
        layer = jnp.maximum(layer, 0.0)
        if tap == 0:
            keep = jnp.concatenate([row + 2 * quarter * position >= 1] * q_first, axis=0)
            layer = jnp.where(keep, layer, 0.0)
        layer = layer.astype(jnp.bfloat16)
        count = quarter * q_second
        windows.append(layer[:count])
        windows.append(layer[quarter * evens : quarter * evens + count])
        windows.append(layer[quarter : quarter + count])
    copies[0].wait()
    second = jnp.dot(jnp.concatenate(windows, axis=1), conv2_w_ref[...], preferred_element_type=jnp.float32)
    second = jnp.maximum(second + conv2_b_ref[...], 0.0).astype(jnp.bfloat16)
    flat = jnp.concatenate([second[quarter * r : quarter * (r + 1)] for r in range(q_second)], axis=1)
    copies[1].wait()
    features = jnp.dot(flat, proj_w_ref[...], preferred_element_type=jnp.float32) + proj_b_ref[...]
    features = jnp.where(position * frames + 4 * row < valid, features, 0.0)
    out_ref[0] = features.astype(jnp.bfloat16)


def flipped(block, axis, step):
    size = lax.axis_size(axis)
    return lax.ppermute(block, axis, [(i, i ^ step) for i in range(size)])


def summed_over_chips(block, axis):
    size = lax.axis_size(axis)
    if size & (size - 1):
        return lax.psum(block, axis, axis_index_groups=[list(range(c, size, 2)) for c in range(2)])
    step = 2
    while step < size:
        block = block + flipped(block, axis, step)
        step *= 2
    return block


def paired(block, axis, first):
    size = lax.axis_size(axis)
    lower = range(first, size, 2)
    route = [(i, (i + 1) % size) for i in lower] + [((i + 1) % size, i) for i in lower]
    return lax.ppermute(block, axis, route)


def per_device(waveform, masks, valid, ref_mic, conv1_w, conv1_b, conv2_w, conv2_b, proj_w, proj_b):
    frames = masks.shape[1]
    channels = conv1_w.shape[1]
    width = proj_w.shape[1]
    vmem = pl.BlockSpec(memory_space=pltpu.VMEM)
    smem = pl.BlockSpec(memory_space=pltpu.SMEM)
    hbm = pl.BlockSpec(memory_space=pltpu.HBM)
    in_hbm = functools.partial(pltpu.with_memory_space_constraint, memory_space=pltpu.HBM)
    params = pltpu.CompilerParams(vmem_limit_bytes=20 * 1024 * 1024)
    rim = jax.ShapeDtypeStruct((MICS, LEAD), waveform.dtype)
    beside, across = pl.pallas_call(
        rims_kernel,
        out_shape=(rim, rim),
        in_specs=[hbm],
        out_specs=(vmem, vmem),
        scratch_shapes=[pltpu.SemaphoreType.DMA((2,))],
        compiler_params=params,
        name="rims",
    )(in_hbm(waveform))
    got_across = paired(across, "tm", 1)
    got_beside = paired(beside, "tm", 0)
    table = dft_table()
    stat_block = jax.ShapeDtypeStruct((STATS + MICS, LANES), jnp.float32)
    spec, kept, edge_weight, table = pl.pallas_call(
        functools.partial(stats_kernel, frames),
        out_shape=(
            jax.ShapeDtypeStruct((2 * TILES, frames * MICS, LANES), jnp.float32),
            jax.ShapeDtypeStruct((TILES, STATS, LANES), jnp.float32),
            jax.ShapeDtypeStruct((TILES, 2, MICS, LANES), jnp.float32),
            jax.ShapeDtypeStruct(table.shape, table.dtype),
        ),
        in_specs=[hbm, hbm, hbm, smem],
        out_specs=(vmem,) * 4,
        scratch_shapes=[
            pltpu.VMEM(waveform.shape, waveform.dtype),
            pltpu.VMEM(masks.shape, masks.dtype),
            pltpu.VMEM((frames * MICS, NFFT), jnp.float32),
            pltpu.VMEM((TILES, 2, frames, LANES), jnp.float32),
            pltpu.SemaphoreType.DMA((3,)),
        ],
        compiler_params=params,
        name="stats",
    )(in_hbm(waveform), in_hbm(masks), in_hbm(table), valid)
    edge_spec, mine, theirs = pl.pallas_call(
        functools.partial(edges_kernel, lax.axis_size("tm")),
        out_shape=(jax.ShapeDtypeStruct((2 * TILES, MICS * MICS, LANES), jnp.float32), stat_block, stat_block),
        in_specs=[vmem] * 7,
        out_specs=(vmem,) * 3,
        scratch_shapes=[pltpu.VMEM((MICS * MICS, NFFT), jnp.float32)],
        compiler_params=params,
        name="edges",
    )(beside, across, got_beside, got_across, table, edge_weight, kept)
    stats = summed_over_chips(mine + flipped(theirs, "tm", 1), "tm")
    beam = jax.ShapeDtypeStruct((2 * MICS, LANES), jnp.float32)
    beam_mine, beam_last = pl.pallas_call(
        solve_kernel,
        out_shape=(beam, beam),
        in_specs=[vmem, smem],
        out_specs=(vmem, vmem),
        compiler_params=params,
        name="solve",
    )(stats, ref_mic)
    beam_theirs = flipped(beam_mine, "tm", 1)
    rows = frames + MICS
    return pl.pallas_call(
        functools.partial(stem_kernel, frames),
        out_shape=jax.ShapeDtypeStruct((1, frames // 4, width), jnp.bfloat16),
        in_specs=[vmem] * 5 + [smem] + [vmem] * 3 + [hbm, vmem, hbm, vmem],
        out_specs=vmem,
        scratch_shapes=[
            pltpu.VMEM((TILES, rows, LANES), jnp.float32),
            pltpu.VMEM((2, rows, LANES), jnp.float32),
            pltpu.VMEM((LANES, channels), jnp.float32),
            pltpu.VMEM((9 * channels, channels), conv2_w.dtype),
            pltpu.VMEM(proj_w.shape, proj_w.dtype),
            pltpu.SemaphoreType.DMA((2,)),
        ],
        compiler_params=params,
        name="stem",
    )(
        beam_mine,
        beam_theirs,
        beam_last,
        spec,
        edge_spec,
        valid,
        packed_mel_bank(),
        conv1_w,
        conv1_b[None],
        in_hbm(conv2_w.reshape(-1, channels)),
        conv2_b[None],
        in_hbm(proj_w),
        proj_b[None],
    )


def solution(mesh):
    return jax.shard_map(
        per_device,
        mesh=mesh,
        in_specs=(
            P(None, ("meet", "tm")),
            P(None, ("meet", "tm"), None),
            P("meet"),
            P("meet"),
            P(),
            P(),
            P(),
            P(),
            P(),
            P(),
        ),
        out_specs=P(None, ("meet", "tm"), None),
        check_vma=False,
    )
```

```python
import functools
import math

import jax
import jax.numpy as jnp
import numpy as np
from jax import lax
from jax.experimental import pallas as pl
from jax.experimental.pallas import tpu as pltpu
from jax.sharding import PartitionSpec as P

NFFT = 512
HOP = 160
MELS = 80
BINS = NFFT // 2 + 1
LANES = 128
MICS = 8
PAD_BINS = -(-BINS // LANES) * LANES
TILES = PAD_BINS // LANES
HALO = 3
LEAD = 512
TAIL = 384
STATS = 2 * MICS * MICS
SPAN = 42

loading = 0.03
epsilon = 1e-06
sample_rate = 16000.0


def dft_table():
    n = np.arange(NFFT)
    f = np.arange(BINS)
    phase = 2.0 * math.pi * ((n[:, None] * f[None, :]) % NFFT) / NFFT
    window = 0.5 - 0.5 * np.cos(2.0 * math.pi * n / NFFT)
    table = np.zeros((NFFT, 2, PAD_BINS), np.float32)
    table[:, 0, :BINS] = window[:, None] * np.cos(phase)
    table[:, 1, :BINS] = -window[:, None] * np.sin(phase)
    return jnp.asarray(table.reshape(NFFT, 2 * PAD_BINS)).astype(jnp.bfloat16)


def mel_bank():
    mel_top = 2595.0 * math.log10(1.0 + sample_rate / 2.0 / 700.0)
    points = np.arange(MELS + 2) * (mel_top / (MELS + 1))
    edges = 700.0 * (np.power(10.0, points / 2595.0) - 1.0)
    freq = np.arange(BINS) * (sample_rate / 2.0 / (BINS - 1))
    lower, centre, upper = edges[:-2], edges[1:-1], edges[2:]
    rising = (freq[:, None] - lower[None, :]) / (centre - lower)[None, :]
    falling = (upper[None, :] - freq[:, None]) / (upper - centre)[None, :]
    return np.maximum(np.minimum(rising, falling), 0.0).astype(np.float32)


def packed_mel_bank():
    bank = mel_bank()
    packed = np.zeros((PAD_BINS, 2, LANES), np.float32)
    for half in range(2):
        part = bank[:, half * 40 : half * 40 + SPAN]
        for copy in range(3):
            packed[:BINS, half, copy * SPAN : copy * SPAN + part.shape[1]] = part
    return jnp.asarray(packed.reshape(TILES, LANES, 2 * LANES))


def cyclic_pairs(x_re, x_im):
    pairs = [x_re * x_re + x_im * x_im]
    for shift in range(1, MICS // 2 + 1):
        y_re = pltpu.roll(x_re, MICS - shift, 0)
        y_im = pltpu.roll(x_im, MICS - shift, 0)
        pairs.append(x_re * y_re + x_im * y_im)
        pairs.append(x_im * y_re - x_re * y_im)
    return pairs


def add_frame(sums, x_re, x_im, weights):
    pairs = cyclic_pairs(x_re, x_im)
    out = []
    for k in range(2):
        w = jnp.broadcast_to(weights[k], (MICS, LANES))
        out.extend(sums[k * len(pairs) + i] + w * pair for i, pair in enumerate(pairs))
    return tuple(out)


def kept_sums(sums):
    low = lax.broadcasted_iota(jnp.int32, (MICS, LANES), 0) < MICS // 2
    kept = []
    for k in range(2):
        own = sums[9 * k : 9 * k + 9]
        kept.extend(list(own[:7]) + [jnp.where(low, own[7], own[8])])
    return jnp.concatenate(kept, axis=0)


def slot_tiles(position):
    core = position % 2
    return core, 1 - core, TILES - 1


def started(pairs, sem):
    copies = [pltpu.make_async_copy(source, target, sem.at[i]) for i, (source, target) in enumerate(pairs)]
    for copy in copies:
        copy.start()
    return copies


def rims_kernel(wave_hbm, masks_hbm, table_hbm, beside_ref, across_ref, wave_ref, masks_ref, table_ref, sem):
    copies = started(((wave_hbm, wave_ref), (table_hbm, table_ref), (masks_hbm, masks_ref)), sem)
    even = lax.axis_index("tm") % 2 == 0
    copies[0].wait()
    head = wave_ref[:, :LEAD].astype(jnp.float32)
    tail = wave_ref[:, wave_ref.shape[1] - LEAD :].astype(jnp.float32)
    beside_ref[...] = jnp.where(even, tail, head).astype(beside_ref.dtype)
    across_ref[...] = jnp.where(even, head, tail).astype(across_ref.dtype)
    copies[1].wait()
    copies[2].wait()


def stats_kernel(frames, wave_ref, masks_ref, table_ref, conv2_w_hbm, proj_w_hbm, valid_ref, spec_ref, kept_ref, edge_weight_ref, conv2_w_ref, proj_w_ref, framed_ref, weight_ref, sem):
    copies = started(((conv2_w_hbm, conv2_w_ref), (proj_w_hbm, proj_w_ref)), sem)
    position = lax.axis_index("tm")
    wave = wave_ref[...].astype(jnp.float32)
    width = wave.shape[1]
    rolled = {}
    for frame in range(frames - HALO):
        base, shift = frame * HOP // LANES * LANES, frame * HOP % LANES
        if shift not in rolled:
            rolled[shift] = wave if shift == 0 else pltpu.roll(wave, width - shift, 1)
        framed_ref[MICS * frame : MICS * (frame + 1), :] = rolled[shift][:, base : base + NFFT]
    framed_ref[MICS * (frames - HALO) :, :] = jnp.zeros((MICS * HALO, NFFT), jnp.float32)
    spec = jnp.dot(framed_ref[...].astype(jnp.bfloat16), table_ref[...], preferred_element_type=jnp.float32)
    for tile in range(2 * TILES):
        spec_ref[tile] = spec[:, tile * LANES : (tile + 1) * LANES]

    row = lax.broadcasted_iota(jnp.int32, (frames, 1), 0)
    live = jnp.where(position * frames + row < valid_ref[0], 1.0 / 255.0, 0.0)
    weight_ref[TILES - 1] = jnp.zeros((2, frames, LANES), jnp.float32)
    for k in range(2):
        weight = masks_ref[k].astype(jnp.float32) * live
        for tile in range(TILES):
            kept_lanes = min(LANES, BINS - tile * LANES)
            weight_ref[tile, k, :, :kept_lanes] = weight[:, tile * LANES : tile * LANES + kept_lanes]
    edge_weight_ref[...] = weight_ref[:, :, frames - MICS :, :]

    for slot, tile in enumerate(slot_tiles(position)):

        def add_frames(group, sums):
            first = pl.multiple_of(group * MICS, MICS)
            weights = [weight_ref[tile, k, pl.ds(first, MICS), :] for k in range(2)]
            for frame in range(MICS):
                rows = pl.ds(pl.multiple_of((first + frame) * MICS, MICS), MICS)
                sums = add_frame(
                    sums, spec_ref[tile, rows, :], spec_ref[TILES + tile, rows, :], [w[frame : frame + 1] for w in weights]
                )
            return sums

        zero = jnp.zeros((MICS, LANES), jnp.float32)
        kept_ref[slot] = kept_sums(lax.fori_loop(0, frames // MICS, add_frames, (zero,) * 18))
    for copy in copies:
        copy.wait()


def edges_kernel(own0_ref, own1_ref, got0_ref, got1_ref, table_ref, edge_weight_ref, kept_ref, spec_ref, mine_ref, theirs_ref, framed_ref):
    position = lax.axis_index("tm")
    even = position % 2 == 0
    own = [own0_ref[...].astype(jnp.float32), own1_ref[...].astype(jnp.float32)]
    got = [got0_ref[...].astype(jnp.float32), got1_ref[...].astype(jnp.float32)]
    head, tail = jnp.where(even, own[1], own[0]), jnp.where(even, own[0], own[1])
    prev, after = jnp.where(even, got[1], got[0]), jnp.where(even, got[0], got[1])
    joined = jnp.concatenate(
        [jnp.concatenate([prev, head[:, :TAIL]], axis=1), jnp.concatenate([tail, after[:, :TAIL]], axis=1)], axis=0
    )
    for i in range(HALO):
        start = LEAD - HALO * HOP + i * HOP
        base, shift = start // LANES * LANES, start % LANES
        turned = joined if shift == 0 else pltpu.roll(joined, joined.shape[1] - shift, 1)
        framed_ref[2 * MICS * i : 2 * MICS * (i + 1), :] = turned[:, base : base + NFFT]
    used = 2 * MICS * HALO
    framed_ref[used:, :] = jnp.zeros((framed_ref.shape[0] - used, NFFT), jnp.float32)
    spec = jnp.dot(framed_ref[...].astype(jnp.bfloat16), table_ref[...], preferred_element_type=jnp.float32)
    for tile in range(2 * TILES):
        spec_ref[tile] = spec[:, tile * LANES : (tile + 1) * LANES]
    for slot, tile in enumerate(slot_tiles(position)):
        sums = (jnp.zeros((MICS, LANES), jnp.float32),) * 18
        for i in range(HALO):
            rows = slice((2 * i + 1) * MICS, (2 * i + 2) * MICS)
            at = MICS - HALO + i
            weights = [edge_weight_ref[tile, k, at : at + 1, :] for k in range(2)]
            sums = add_frame(sums, spec_ref[tile, rows, :], spec_ref[TILES + tile, rows, :], weights)
        total = kept_ref[slot] + kept_sums(sums)
        if slot == 0:
            mine_ref[:STATS, :] = total
        elif slot == 1:
            theirs_ref[:STATS, :] = total
        else:
            last_bin = jnp.transpose(total)[:MICS]
            mine_ref[STATS:, :] = last_bin
            theirs_ref[STATS:, :] = last_bin


def columns_of(kept, sub):
    low = sub < MICS // 2
    diag_re = [kept[0], kept[1], kept[3], kept[5]]
    diag_im = [jnp.zeros_like(kept[0]), kept[2], kept[4], kept[6]]
    turned = pltpu.roll(kept[7], MICS // 2, 0)
    diag_re.append(jnp.where(low, kept[7], turned))
    diag_im.append(jnp.where(low, -turned, kept[7]))
    for shift in range(MICS // 2 + 1, MICS):
        diag_re.append(pltpu.roll(diag_re[MICS - shift], MICS - shift, 0))
        diag_im.append(-pltpu.roll(diag_im[MICS - shift], MICS - shift, 0))
    columns = []
    for n in range(MICS):
        re, im = diag_re[n], diag_im[n]
        for m in range(1, MICS):
            re = jnp.where(sub == m, diag_re[(n - m) % MICS], re)
            im = jnp.where(sub == m, diag_im[(n - m) % MICS], im)
        columns.append((re, im))
    return columns


def beams_of(stats, ref_mic):
    sub = lax.broadcasted_iota(jnp.int32, stats[0].shape, 0)
    answer = columns_of(stats[:MICS], sub)
    matrix = columns_of(stats[MICS:], sub)
    spread = jnp.sum(stats[MICS], axis=0, keepdims=True)
    ridge = loading * spread / MICS + epsilon
    matrix = [(jnp.where(sub == n, re + ridge, re), im) for n, (re, im) in enumerate(matrix)]
    for pivot in range(MICS):
        col_re, col_im = matrix[pivot]
        pivot_re = col_re[pivot : pivot + 1]
        pivot_im = col_im[pivot : pivot + 1]
        modulus = pivot_re * pivot_re + pivot_im * pivot_im
        inverse_re = pivot_re / modulus
        inverse_im = -pivot_im / modulus

        def eliminated(column):
            re, im = column
            row_re, row_im = re[pivot : pivot + 1], im[pivot : pivot + 1]
            lead_re = row_re * inverse_re - row_im * inverse_im
            lead_im = row_re * inverse_im + row_im * inverse_re
            return (
                jnp.where(sub == pivot, lead_re, re - (col_re * lead_re - col_im * lead_im)),
                jnp.where(sub == pivot, lead_im, im - (col_re * lead_im + col_im * lead_re)),
            )

        matrix = [eliminated(c) if n > pivot else c for n, c in enumerate(matrix)]
        answer = [eliminated(c) for c in answer]
    trace = answer[0][0][0:1]
    beam_re, beam_im = answer[0]
    for n in range(1, MICS):
        trace = trace + answer[n][0][n : n + 1]
        beam_re = jnp.where(ref_mic == n, answer[n][0], beam_re)
        beam_im = jnp.where(ref_mic == n, answer[n][1], beam_im)
    scale = 1.0 / (trace + epsilon)
    return beam_re * scale, beam_im * scale


def solve_kernel(stats_ref, ref_mic_ref, beam_ref, last_ref):
    blank = jnp.zeros((LANES - MICS, LANES), jnp.float32)
    last_bin = jnp.transpose(jnp.concatenate([stats_ref[STATS:, :], blank], axis=0))
    for out_ref, stats in ((beam_ref, stats_ref[:STATS, :]), (last_ref, last_bin)):
        kept = [stats[i * MICS : (i + 1) * MICS] for i in range(2 * MICS)]
        beam_re, beam_im = beams_of(kept, ref_mic_ref[0])
        out_ref[:MICS, :] = beam_re
        out_ref[MICS:, :] = beam_im


def power_of(beam_ref, tile, spec_ref, edge_spec_ref):
    beam_re, beam_im = beam_ref[:MICS, :], beam_ref[MICS:, :]
    groups = spec_ref.shape[1] // (MICS * MICS)
    power = []
    for group in range(groups + 1):
        from_ref, first = (spec_ref, group * MICS * MICS) if group < groups else (edge_spec_ref, 0)
        sum_re = sum_im = None
        for m in range(MICS):
            rows = pl.ds(first + m, MICS, stride=MICS)
            x_re, x_im = from_ref[tile, rows, :], from_ref[TILES + tile, rows, :]
            b_re, b_im = beam_re[m : m + 1], beam_im[m : m + 1]
            part_re = b_re * x_re + b_im * x_im
            part_im = b_re * x_im - b_im * x_re
            sum_re = part_re if sum_re is None else sum_re + part_re
            sum_im = part_im if sum_im is None else sum_im + part_im
        power.append(sum_re * sum_re + sum_im * sum_im)
    return jnp.concatenate(power, axis=0)


def mel_of(power, bank):
    return jnp.dot(power, bank, precision=lax.Precision.HIGHEST, preferred_element_type=jnp.float32)


def power_kernel(mine_ref, last_ref, spec_ref, edge_spec_ref, bank_ref, mel_ref):
    mine, _, last = slot_tiles(lax.axis_index("tm"))
    power = [power_of(beam_ref, tile, spec_ref, edge_spec_ref) for beam_ref, tile in ((mine_ref, mine), (last_ref, last))]
    bank = jnp.concatenate([bank_ref[mine], bank_ref[last]], axis=0)
    mel_ref[...] = mel_of(jnp.concatenate(power, axis=1), bank)


def stem_kernel(frames, theirs_ref, mel_ref, spec_ref, edge_spec_ref, valid_ref, bank_ref, conv1_w_ref, conv1_b_ref, conv2_w_ref, conv2_b_ref, proj_w_ref, proj_b_ref, out_ref, logmel_ref, conv1_ref):
    position = lax.axis_index("tm")
    valid = valid_ref[0]
    quarter = frames // 4
    channels = conv1_w_ref.shape[1]
    conv1_ref[...] = jnp.zeros((LANES, channels), jnp.float32)
    for shift_t in range(3):
        conv1_ref[SPAN * shift_t : SPAN * shift_t + 3, :] = conv1_w_ref[3 * shift_t : 3 * shift_t + 3, :].astype(jnp.float32)
    conv1 = conv1_ref[...].astype(jnp.bfloat16)

    theirs = slot_tiles(position)[1]
    mel = mel_ref[...] + mel_of(power_of(theirs_ref, theirs, spec_ref, edge_spec_ref), bank_ref[theirs])
    row = lax.broadcasted_iota(jnp.int32, (frames + MICS, 1), 0)
    edge = (row - frames) // 2 + jnp.where((row - frames) % 2 == 0, -HALO, frames - HALO)
    time = position * frames + jnp.where(row < frames, row, edge)
    live = (time >= 0) & (time < valid)
    logmel = jnp.where(live, jnp.log(mel + epsilon), 0.0)
    logmel = logmel.astype(jnp.bfloat16).astype(jnp.float32)
    for half in range(2):
        part = logmel[:, half * LANES : (half + 1) * LANES]
        logmel_ref[half, HALO : HALO + frames, :] = part[:frames]
        for i in range(HALO):
            logmel_ref[half, i : i + 1, :] = part[frames + 2 * i : frames + 2 * i + 1]
            logmel_ref[half, frames + i : frames + i + 1, :] = part[frames + 2 * i + 1 : frames + 2 * i + 2]

    q_first = (MELS - 3) // 2 + 1
    q_second = (q_first - 3) // 2 + 1
    order = list(range(0, q_first, 2)) + list(range(1, q_first, 2))
    evens = (q_first + 1) // 2
    lane = lax.broadcasted_iota(jnp.int32, (quarter, LANES), 1)
    row = lax.broadcasted_iota(jnp.int32, (quarter, 1), 0)
    windows = []
    for tap in range(3):
        packs = []
        for half in range(2):
            rows = [logmel_ref[half, pl.ds(2 * tap + a, quarter, stride=4), :] for a in range(3)]
            packs.append(jnp.where(lane < SPAN, rows[0], jnp.where(lane < 2 * SPAN, rows[1], rows[2])))
        patches = []
        for q in order:
            half, shift = (0, 2 * q) if q < 20 else (1, 2 * q - 40)
            patches.append(packs[half] if shift == 0 else pltpu.roll(packs[half], LANES - shift, 1))
        patches = jnp.concatenate(patches, axis=0).astype(jnp.bfloat16)
        layer = jnp.dot(patches, conv1, preferred_element_type=jnp.float32) + conv1_b_ref[...]
        layer = jnp.maximum(layer, 0.0)
        if tap == 0:
            keep = jnp.concatenate([row + 2 * quarter * position >= 1] * q_first, axis=0)
            layer = jnp.where(keep, layer, 0.0)
        layer = layer.astype(jnp.bfloat16)
        count = quarter * q_second
        windows.append(layer[:count])
        windows.append(layer[quarter * evens : quarter * evens + count])
        windows.append(layer[quarter : quarter + count])
    second = jnp.dot(jnp.concatenate(windows, axis=1), conv2_w_ref[...], preferred_element_type=jnp.float32)
    second = jnp.maximum(second + conv2_b_ref[...], 0.0).astype(jnp.bfloat16)
    flat = jnp.concatenate([second[quarter * r : quarter * (r + 1)] for r in range(q_second)], axis=1)
    features = jnp.dot(flat, proj_w_ref[...], preferred_element_type=jnp.float32) + proj_b_ref[...]
    features = jnp.where(position * frames + 4 * row < valid, features, 0.0)
    out_ref[0] = features.astype(jnp.bfloat16)


def flipped(block, axis, step):
    size = lax.axis_size(axis)
    return lax.ppermute(block, axis, [(i, i ^ step) for i in range(size)])


def summed_over_chips(block, axis):
    size = lax.axis_size(axis)
    if size & (size - 1):
        return lax.psum(block, axis, axis_index_groups=[list(range(c, size, 2)) for c in range(2)])
    step = 2
    while step < size:
        block = block + flipped(block, axis, step)
        step *= 2
    return block


def paired(block, axis, first):
    lower = range(first, lax.axis_size(axis) - 1, 2)
    return lax.ppermute(block, axis, [(i, i + 1) for i in lower] + [(i + 1, i) for i in lower])


def per_device(waveform, masks, valid, ref_mic, conv1_w, conv1_b, conv2_w, conv2_b, proj_w, proj_b):
    frames = masks.shape[1]
    channels = conv1_w.shape[1]
    width = proj_w.shape[1]
    vmem = pl.BlockSpec(memory_space=pltpu.VMEM)
    smem = pl.BlockSpec(memory_space=pltpu.SMEM)
    hbm = pl.BlockSpec(memory_space=pltpu.HBM)
    in_hbm = functools.partial(pltpu.with_memory_space_constraint, memory_space=pltpu.HBM)
    params = pltpu.CompilerParams(vmem_limit_bytes=16 * 1024 * 1024)
    rim = jax.ShapeDtypeStruct((MICS, LEAD), waveform.dtype)
    table = dft_table()
    conv2_w = conv2_w.reshape(-1, channels)
    beside, across, waves, levels, table = pl.pallas_call(
        rims_kernel,
        out_shape=(rim, rim) + tuple(jax.ShapeDtypeStruct(x.shape, x.dtype) for x in (waveform, masks, table)),
        in_specs=[hbm] * 3,
        out_specs=(vmem,) * 5,
        scratch_shapes=[pltpu.SemaphoreType.DMA((3,))],
        compiler_params=params,
        name="rims",
    )(in_hbm(waveform), in_hbm(masks), in_hbm(table))
    got_across = paired(across, "tm", 1)
    got_beside = paired(beside, "tm", 0)
    stat_block = jax.ShapeDtypeStruct((STATS + MICS, LANES), jnp.float32)
    spec, kept, edge_weight, conv2_w, proj_w = pl.pallas_call(
        functools.partial(stats_kernel, frames),
        out_shape=(
            jax.ShapeDtypeStruct((2 * TILES, frames * MICS, LANES), jnp.float32),
            jax.ShapeDtypeStruct((TILES, STATS, LANES), jnp.float32),
            jax.ShapeDtypeStruct((TILES, 2, MICS, LANES), jnp.float32),
            jax.ShapeDtypeStruct(conv2_w.shape, conv2_w.dtype),
            jax.ShapeDtypeStruct(proj_w.shape, proj_w.dtype),
        ),
        in_specs=[vmem] * 3 + [hbm] * 2 + [smem],
        out_specs=(vmem,) * 5,
        scratch_shapes=[
            pltpu.VMEM((frames * MICS, NFFT), jnp.float32),
            pltpu.VMEM((TILES, 2, frames, LANES), jnp.float32),
            pltpu.SemaphoreType.DMA((2,)),
        ],
        compiler_params=params,
        name="stats",
    )(waves, levels, table, in_hbm(conv2_w), in_hbm(proj_w), valid)
    edge_spec, mine, theirs = pl.pallas_call(
        edges_kernel,
        out_shape=(jax.ShapeDtypeStruct((2 * TILES, MICS * MICS, LANES), jnp.float32), stat_block, stat_block),
        in_specs=[vmem] * 7,
        out_specs=(vmem,) * 3,
        scratch_shapes=[pltpu.VMEM((MICS * MICS, NFFT), jnp.float32)],
        compiler_params=params,
        name="edges",
    )(beside, across, got_beside, got_across, table, edge_weight, kept)
    stats = summed_over_chips(mine + flipped(theirs, "tm", 1), "tm")
    beam = jax.ShapeDtypeStruct((2 * MICS, LANES), jnp.float32)
    beam_mine, beam_last = pl.pallas_call(
        solve_kernel,
        out_shape=(beam, beam),
        in_specs=[vmem, smem],
        out_specs=(vmem, vmem),
        compiler_params=params,
        name="solve",
    )(stats, ref_mic)
    beam_theirs = flipped(beam_mine, "tm", 1)
    rows = frames + MICS
    bank = packed_mel_bank()
    mel = pl.pallas_call(
        power_kernel,
        out_shape=jax.ShapeDtypeStruct((rows, 2 * LANES), jnp.float32),
        in_specs=[vmem] * 5,
        out_specs=vmem,
        compiler_params=params,
        name="power",
    )(beam_mine, beam_last, spec, edge_spec, bank)
    return pl.pallas_call(
        functools.partial(stem_kernel, frames),
        out_shape=jax.ShapeDtypeStruct((1, frames // 4, width), jnp.bfloat16),
        in_specs=[vmem] * 4 + [smem] + [vmem] * 7,
        out_specs=vmem,
        scratch_shapes=[pltpu.VMEM((2, rows, LANES), jnp.float32), pltpu.VMEM((LANES, channels), jnp.float32)],
        compiler_params=params,
        name="stem",
    )(
        beam_theirs,
        mel,
        spec,
        edge_spec,
        valid,
        bank,
        conv1_w,
        conv1_b[None],
        conv2_w,
        conv2_b[None],
        proj_w,
        proj_b[None],
    )


def solution(mesh):
    return jax.shard_map(
        per_device,
        mesh=mesh,
        in_specs=(
            P(None, ("meet", "tm")),
            P(None, ("meet", "tm"), None),
            P("meet"),
            P("meet"),
            P(),
            P(),
            P(),
            P(),
            P(),
            P(),
        ),
        out_specs=P(None, ("meet", "tm"), None),
        check_vma=False,
    )
```

```python
import functools
import math

import jax
import jax.numpy as jnp
import numpy as np
from jax import lax
from jax.experimental import pallas as pl
from jax.experimental.pallas import tpu as pltpu
from jax.sharding import PartitionSpec as P

NFFT = 512
HOP = 160
MELS = 80
BINS = NFFT // 2 + 1
LANES = 128
MICS = 8
PAD_BINS = -(-BINS // LANES) * LANES
TILES = PAD_BINS // LANES
HALO = 3
LEAD = 512
TAIL = 384
STATS = 2 * MICS * MICS
SPAN = 42

loading = 0.03
epsilon = 1e-06
sample_rate = 16000.0


def dft_table():
    n = np.arange(NFFT)
    f = np.arange(BINS)
    phase = 2.0 * math.pi * ((n[:, None] * f[None, :]) % NFFT) / NFFT
    window = 0.5 - 0.5 * np.cos(2.0 * math.pi * n / NFFT)
    table = np.zeros((NFFT, 2, PAD_BINS), np.float32)
    table[:, 0, :BINS] = window[:, None] * np.cos(phase)
    table[:, 1, :BINS] = -window[:, None] * np.sin(phase)
    return jnp.asarray(table.reshape(NFFT, 2 * PAD_BINS)).astype(jnp.bfloat16)


def mel_bank():
    mel_top = 2595.0 * math.log10(1.0 + sample_rate / 2.0 / 700.0)
    points = np.arange(MELS + 2) * (mel_top / (MELS + 1))
    edges = 700.0 * (np.power(10.0, points / 2595.0) - 1.0)
    freq = np.arange(BINS) * (sample_rate / 2.0 / (BINS - 1))
    lower, centre, upper = edges[:-2], edges[1:-1], edges[2:]
    rising = (freq[:, None] - lower[None, :]) / (centre - lower)[None, :]
    falling = (upper[None, :] - freq[:, None]) / (upper - centre)[None, :]
    return np.maximum(np.minimum(rising, falling), 0.0).astype(np.float32)


def packed_mel_bank():
    bank = mel_bank()
    packed = np.zeros((PAD_BINS, 2, LANES), np.float32)
    for half in range(2):
        part = bank[:, half * 40 : half * 40 + SPAN]
        for copy in range(3):
            packed[:BINS, half, copy * SPAN : copy * SPAN + part.shape[1]] = part
    return jnp.asarray(packed.reshape(TILES, LANES, 2 * LANES))


def cyclic_pairs(x_re, x_im):
    pairs = [x_re * x_re + x_im * x_im]
    for shift in range(1, MICS // 2 + 1):
        y_re = pltpu.roll(x_re, MICS - shift, 0)
        y_im = pltpu.roll(x_im, MICS - shift, 0)
        pairs.append(x_re * y_re + x_im * y_im)
        pairs.append(x_im * y_re - x_re * y_im)
    return pairs


def add_frame(sums, x_re, x_im, weights):
    pairs = cyclic_pairs(x_re, x_im)
    out = []
    for k in range(2):
        w = jnp.broadcast_to(weights[k], (MICS, LANES))
        out.extend(sums[k * len(pairs) + i] + w * pair for i, pair in enumerate(pairs))
    return tuple(out)


def kept_sums(sums):
    low = lax.broadcasted_iota(jnp.int32, (MICS, LANES), 0) < MICS // 2
    kept = []
    for k in range(2):
        own = sums[9 * k : 9 * k + 9]
        kept.extend(list(own[:7]) + [jnp.where(low, own[7], own[8])])
    return jnp.concatenate(kept, axis=0)


def slot_tiles(position):
    core = position % 2
    return core, 1 - core, TILES - 1


def started(pairs, sem):
    copies = [pltpu.make_async_copy(source, target, sem.at[i]) for i, (source, target) in enumerate(pairs)]
    for copy in copies:
        copy.start()
    return copies


def rims_kernel(wave_hbm, masks_hbm, table_hbm, beside_ref, across_ref, wave_ref, masks_ref, table_ref, sem):
    copies = started(((wave_hbm, wave_ref), (table_hbm, table_ref), (masks_hbm, masks_ref)), sem)
    even = lax.axis_index("tm") % 2 == 0
    copies[0].wait()
    head = wave_ref[:, :LEAD].astype(jnp.float32)
    tail = wave_ref[:, wave_ref.shape[1] - LEAD :].astype(jnp.float32)
    beside_ref[...] = jnp.where(even, tail, head).astype(beside_ref.dtype)
    across_ref[...] = jnp.where(even, head, tail).astype(across_ref.dtype)
    copies[1].wait()
    copies[2].wait()


def stats_kernel(frames, wave_ref, masks_ref, table_ref, conv2_w_hbm, proj_w_hbm, valid_ref, spec_ref, kept_ref, edge_weight_ref, conv2_w_ref, proj_w_ref, framed_ref, weight_ref, sem):
    copies = started(((conv2_w_hbm, conv2_w_ref), (proj_w_hbm, proj_w_ref)), sem)
    position = lax.axis_index("tm")
    wave = wave_ref[...].astype(jnp.float32)
    width = wave.shape[1]
    rolled = {}
    for frame in range(frames - HALO):
        base, shift = frame * HOP // LANES * LANES, frame * HOP % LANES
        if shift not in rolled:
            rolled[shift] = wave if shift == 0 else pltpu.roll(wave, width - shift, 1)
        framed_ref[MICS * frame : MICS * (frame + 1), :] = rolled[shift][:, base : base + NFFT]
    framed_ref[MICS * (frames - HALO) :, :] = jnp.zeros((MICS * HALO, NFFT), jnp.float32)
    spec = jnp.dot(framed_ref[...].astype(jnp.bfloat16), table_ref[...], preferred_element_type=jnp.float32)
    for tile in range(2 * TILES):
        spec_ref[tile] = spec[:, tile * LANES : (tile + 1) * LANES]

    row = lax.broadcasted_iota(jnp.int32, (frames, 1), 0)
    live = jnp.where(position * frames + row < valid_ref[0], 1.0 / 255.0, 0.0)
    weight_ref[TILES - 1] = jnp.zeros((2, frames, LANES), jnp.float32)
    for k in range(2):
        weight = masks_ref[k].astype(jnp.float32) * live
        for tile in range(TILES):
            kept_lanes = min(LANES, BINS - tile * LANES)
            weight_ref[tile, k, :, :kept_lanes] = weight[:, tile * LANES : tile * LANES + kept_lanes]
    edge_weight_ref[...] = weight_ref[:, :, frames - MICS :, :]

    for slot, tile in enumerate(slot_tiles(position)):

        def add_frames(group, sums):
            first = pl.multiple_of(group * MICS, MICS)
            weights = [weight_ref[tile, k, pl.ds(first, MICS), :] for k in range(2)]
            for frame in range(MICS):
                rows = pl.ds(pl.multiple_of((first + frame) * MICS, MICS), MICS)
                sums = add_frame(
                    sums, spec_ref[tile, rows, :], spec_ref[TILES + tile, rows, :], [w[frame : frame + 1] for w in weights]
                )
            return sums

        zero = jnp.zeros((MICS, LANES), jnp.float32)
        kept_ref[slot] = kept_sums(lax.fori_loop(0, frames // MICS, add_frames, (zero,) * 18))
    for copy in copies:
        copy.wait()


def edges_kernel(devices, own0_ref, own1_ref, got0_ref, got1_ref, table_ref, edge_weight_ref, kept_ref, spec_ref, mine_ref, theirs_ref, framed_ref):
    position = lax.axis_index("tm")
    even = position % 2 == 0
    own = [own0_ref[...].astype(jnp.float32), own1_ref[...].astype(jnp.float32)]
    got = [got0_ref[...].astype(jnp.float32), got1_ref[...].astype(jnp.float32)]
    head, tail = jnp.where(even, own[1], own[0]), jnp.where(even, own[0], own[1])
    prev, after = jnp.where(even, got[1], got[0]), jnp.where(even, got[0], got[1])
    prev = jnp.where(position > 0, prev, 0.0)
    after = jnp.where(position < devices - 1, after, 0.0)
    joined = jnp.concatenate(
        [jnp.concatenate([prev, head[:, :TAIL]], axis=1), jnp.concatenate([tail, after[:, :TAIL]], axis=1)], axis=0
    )
    for i in range(HALO):
        start = LEAD - HALO * HOP + i * HOP
        base, shift = start // LANES * LANES, start % LANES
        turned = joined if shift == 0 else pltpu.roll(joined, joined.shape[1] - shift, 1)
        framed_ref[2 * MICS * i : 2 * MICS * (i + 1), :] = turned[:, base : base + NFFT]
    used = 2 * MICS * HALO
    framed_ref[used:, :] = jnp.zeros((framed_ref.shape[0] - used, NFFT), jnp.float32)
    spec = jnp.dot(framed_ref[...].astype(jnp.bfloat16), table_ref[...], preferred_element_type=jnp.float32)
    for tile in range(2 * TILES):
        spec_ref[tile] = spec[:, tile * LANES : (tile + 1) * LANES]
    for slot, tile in enumerate(slot_tiles(position)):
        sums = (jnp.zeros((MICS, LANES), jnp.float32),) * 18
        for i in range(HALO):
            rows = slice((2 * i + 1) * MICS, (2 * i + 2) * MICS)
            at = MICS - HALO + i
            weights = [edge_weight_ref[tile, k, at : at + 1, :] for k in range(2)]
            sums = add_frame(sums, spec_ref[tile, rows, :], spec_ref[TILES + tile, rows, :], weights)
        total = kept_ref[slot] + kept_sums(sums)
        if slot == 0:
            mine_ref[:STATS, :] = total
        elif slot == 1:
            theirs_ref[:STATS, :] = total
        else:
            last_bin = jnp.transpose(total)[:MICS]
            mine_ref[STATS:, :] = last_bin
            theirs_ref[STATS:, :] = last_bin


def columns_of(kept, sub):
    low = sub < MICS // 2
    diag_re = [kept[0], kept[1], kept[3], kept[5]]
    diag_im = [jnp.zeros_like(kept[0]), kept[2], kept[4], kept[6]]
    turned = pltpu.roll(kept[7], MICS // 2, 0)
    diag_re.append(jnp.where(low, kept[7], turned))
    diag_im.append(jnp.where(low, -turned, kept[7]))
    for shift in range(MICS // 2 + 1, MICS):
        diag_re.append(pltpu.roll(diag_re[MICS - shift], MICS - shift, 0))
        diag_im.append(-pltpu.roll(diag_im[MICS - shift], MICS - shift, 0))
    columns = []
    for n in range(MICS):
        re, im = diag_re[n], diag_im[n]
        for m in range(1, MICS):
            re = jnp.where(sub == m, diag_re[(n - m) % MICS], re)
            im = jnp.where(sub == m, diag_im[(n - m) % MICS], im)
        columns.append((re, im))
    return columns


def beams_of(stats, ref_mic):
    sub = lax.broadcasted_iota(jnp.int32, stats[0].shape, 0)
    answer = columns_of(stats[:MICS], sub)
    matrix = columns_of(stats[MICS:], sub)
    spread = jnp.sum(stats[MICS], axis=0, keepdims=True)
    ridge = loading * spread / MICS + epsilon
    matrix = [(jnp.where(sub == n, re + ridge, re), im) for n, (re, im) in enumerate(matrix)]
    for pivot in range(MICS):
        col_re, col_im = matrix[pivot]
        pivot_re = col_re[pivot : pivot + 1]
        pivot_im = col_im[pivot : pivot + 1]
        modulus = pivot_re * pivot_re + pivot_im * pivot_im
        inverse_re = pivot_re / modulus
        inverse_im = -pivot_im / modulus

        def eliminated(column):
            re, im = column
            row_re, row_im = re[pivot : pivot + 1], im[pivot : pivot + 1]
            lead_re = row_re * inverse_re - row_im * inverse_im
            lead_im = row_re * inverse_im + row_im * inverse_re
            return (
                jnp.where(sub == pivot, lead_re, re - (col_re * lead_re - col_im * lead_im)),
                jnp.where(sub == pivot, lead_im, im - (col_re * lead_im + col_im * lead_re)),
            )

        matrix = [eliminated(c) if n > pivot else c for n, c in enumerate(matrix)]
        answer = [eliminated(c) for c in answer]
    trace = answer[0][0][0:1]
    beam_re, beam_im = answer[0]
    for n in range(1, MICS):
        trace = trace + answer[n][0][n : n + 1]
        beam_re = jnp.where(ref_mic == n, answer[n][0], beam_re)
        beam_im = jnp.where(ref_mic == n, answer[n][1], beam_im)
    scale = 1.0 / (trace + epsilon)
    return beam_re * scale, beam_im * scale


def solve_kernel(stats_ref, ref_mic_ref, beam_ref, last_ref):
    blank = jnp.zeros((LANES - MICS, LANES), jnp.float32)
    last_bin = jnp.transpose(jnp.concatenate([stats_ref[STATS:, :], blank], axis=0))
    for out_ref, stats in ((beam_ref, stats_ref[:STATS, :]), (last_ref, last_bin)):
        kept = [stats[i * MICS : (i + 1) * MICS] for i in range(2 * MICS)]
        beam_re, beam_im = beams_of(kept, ref_mic_ref[0])
        out_ref[:MICS, :] = beam_re
        out_ref[MICS:, :] = beam_im


def power_of(beam_ref, tile, spec_ref, edge_spec_ref):
    beam_re, beam_im = beam_ref[:MICS, :], beam_ref[MICS:, :]
    groups = spec_ref.shape[1] // (MICS * MICS)
    power = []
    for group in range(groups + 1):
        from_ref, first = (spec_ref, group * MICS * MICS) if group < groups else (edge_spec_ref, 0)
        sum_re = sum_im = None
        for m in range(MICS):
            rows = pl.ds(first + m, MICS, stride=MICS)
            x_re, x_im = from_ref[tile, rows, :], from_ref[TILES + tile, rows, :]
            b_re, b_im = beam_re[m : m + 1], beam_im[m : m + 1]
            part_re = b_re * x_re + b_im * x_im
            part_im = b_re * x_im - b_im * x_re
            sum_re = part_re if sum_re is None else sum_re + part_re
            sum_im = part_im if sum_im is None else sum_im + part_im
        power.append(sum_re * sum_re + sum_im * sum_im)
    return jnp.concatenate(power, axis=0)


def mel_of(power, bank):
    return jnp.dot(power, bank, precision=lax.Precision.HIGHEST, preferred_element_type=jnp.float32)


def power_kernel(mine_ref, last_ref, spec_ref, edge_spec_ref, bank_ref, mel_ref):
    mine, _, last = slot_tiles(lax.axis_index("tm"))
    power = [power_of(beam_ref, tile, spec_ref, edge_spec_ref) for beam_ref, tile in ((mine_ref, mine), (last_ref, last))]
    bank = jnp.concatenate([bank_ref[mine], bank_ref[last]], axis=0)
    mel_ref[...] = mel_of(jnp.concatenate(power, axis=1), bank)


def stem_kernel(frames, theirs_ref, mel_ref, spec_ref, edge_spec_ref, valid_ref, bank_ref, conv1_w_ref, conv1_b_ref, conv2_w_ref, conv2_b_ref, proj_w_ref, proj_b_ref, out_ref, logmel_ref, conv1_ref):
    position = lax.axis_index("tm")
    valid = valid_ref[0]
    quarter = frames // 4
    channels = conv1_w_ref.shape[1]
    conv1_ref[...] = jnp.zeros((LANES, channels), jnp.float32)
    for shift_t in range(3):
        conv1_ref[SPAN * shift_t : SPAN * shift_t + 3, :] = conv1_w_ref[3 * shift_t : 3 * shift_t + 3, :].astype(jnp.float32)
    conv1 = conv1_ref[...].astype(jnp.bfloat16)

    theirs = slot_tiles(position)[1]
    mel = mel_ref[...] + mel_of(power_of(theirs_ref, theirs, spec_ref, edge_spec_ref), bank_ref[theirs])
    row = lax.broadcasted_iota(jnp.int32, (frames + MICS, 1), 0)
    edge = (row - frames) // 2 + jnp.where((row - frames) % 2 == 0, -HALO, frames - HALO)
    time = position * frames + jnp.where(row < frames, row, edge)
    live = (time >= 0) & (time < valid)
    logmel = jnp.where(live, jnp.log(mel + epsilon), 0.0)
    logmel = logmel.astype(jnp.bfloat16).astype(jnp.float32)
    for half in range(2):
        part = logmel[:, half * LANES : (half + 1) * LANES]
        logmel_ref[half, HALO : HALO + frames, :] = part[:frames]
        for i in range(HALO):
            logmel_ref[half, i : i + 1, :] = part[frames + 2 * i : frames + 2 * i + 1]
            logmel_ref[half, frames + i : frames + i + 1, :] = part[frames + 2 * i + 1 : frames + 2 * i + 2]

    q_first = (MELS - 3) // 2 + 1
    q_second = (q_first - 3) // 2 + 1
    order = list(range(0, q_first, 2)) + list(range(1, q_first, 2))
    evens = (q_first + 1) // 2
    lane = lax.broadcasted_iota(jnp.int32, (quarter, LANES), 1)
    row = lax.broadcasted_iota(jnp.int32, (quarter, 1), 0)
    windows = []
    for tap in range(3):
        packs = []
        for half in range(2):
            rows = [logmel_ref[half, pl.ds(2 * tap + a, quarter, stride=4), :] for a in range(3)]
            packs.append(jnp.where(lane < SPAN, rows[0], jnp.where(lane < 2 * SPAN, rows[1], rows[2])))
        patches = []
        for q in order:
            half, shift = (0, 2 * q) if q < 20 else (1, 2 * q - 40)
            patches.append(packs[half] if shift == 0 else pltpu.roll(packs[half], LANES - shift, 1))
        patches = jnp.concatenate(patches, axis=0).astype(jnp.bfloat16)
        layer = jnp.dot(patches, conv1, preferred_element_type=jnp.float32) + conv1_b_ref[...]
        layer = jnp.maximum(layer, 0.0)
        if tap == 0:
            keep = jnp.concatenate([row + 2 * quarter * position >= 1] * q_first, axis=0)
            layer = jnp.where(keep, layer, 0.0)
        layer = layer.astype(jnp.bfloat16)
        count = quarter * q_second
        windows.append(layer[:count])
        windows.append(layer[quarter * evens : quarter * evens + count])
        windows.append(layer[quarter : quarter + count])
    second = jnp.dot(jnp.concatenate(windows, axis=1), conv2_w_ref[...], preferred_element_type=jnp.float32)
    second = jnp.maximum(second + conv2_b_ref[...], 0.0).astype(jnp.bfloat16)
    flat = jnp.concatenate([second[quarter * r : quarter * (r + 1)] for r in range(q_second)], axis=1)
    features = jnp.dot(flat, proj_w_ref[...], preferred_element_type=jnp.float32) + proj_b_ref[...]
    features = jnp.where(position * frames + 4 * row < valid, features, 0.0)
    out_ref[0] = features.astype(jnp.bfloat16)


def flipped(block, axis, step):
    size = lax.axis_size(axis)
    return lax.ppermute(block, axis, [(i, i ^ step) for i in range(size)])


def summed_over_chips(block, axis):
    size = lax.axis_size(axis)
    if size & (size - 1):
        return lax.psum(block, axis, axis_index_groups=[list(range(c, size, 2)) for c in range(2)])
    step = 2
    while step < size:
        others = [step] if 2 * step >= size else [step, 2 * step, 3 * step]
        block = sum([flipped(block, axis, other) for other in others], block)
        step *= 4
    return block


def paired(block, axis, first):
    size = lax.axis_size(axis)
    lower = range(first, size, 2)
    return lax.ppermute(block, axis, [(i, (i + 1) % size) for i in lower] + [((i + 1) % size, i) for i in lower])


def per_device(waveform, masks, valid, ref_mic, conv1_w, conv1_b, conv2_w, conv2_b, proj_w, proj_b):
    frames = masks.shape[1]
    channels = conv1_w.shape[1]
    width = proj_w.shape[1]
    vmem = pl.BlockSpec(memory_space=pltpu.VMEM)
    smem = pl.BlockSpec(memory_space=pltpu.SMEM)
    hbm = pl.BlockSpec(memory_space=pltpu.HBM)
    in_hbm = functools.partial(pltpu.with_memory_space_constraint, memory_space=pltpu.HBM)
    params = pltpu.CompilerParams(vmem_limit_bytes=16 * 1024 * 1024)
    rim = jax.ShapeDtypeStruct((MICS, LEAD), waveform.dtype)
    table = dft_table()
    conv2_w = conv2_w.reshape(-1, channels)
    beside, across, waves, levels, table = pl.pallas_call(
        rims_kernel,
        out_shape=(rim, rim) + tuple(jax.ShapeDtypeStruct(x.shape, x.dtype) for x in (waveform, masks, table)),
        in_specs=[hbm] * 3,
        out_specs=(vmem,) * 5,
        scratch_shapes=[pltpu.SemaphoreType.DMA((3,))],
        compiler_params=params,
        name="rims",
    )(in_hbm(waveform), in_hbm(masks), in_hbm(table))
    got_across = paired(across, "tm", 1)
    got_beside = paired(beside, "tm", 0)
    stat_block = jax.ShapeDtypeStruct((STATS + MICS, LANES), jnp.float32)
    spec, kept, edge_weight, conv2_w, proj_w = pl.pallas_call(
        functools.partial(stats_kernel, frames),
        out_shape=(
            jax.ShapeDtypeStruct((2 * TILES, frames * MICS, LANES), jnp.float32),
            jax.ShapeDtypeStruct((TILES, STATS, LANES), jnp.float32),
            jax.ShapeDtypeStruct((TILES, 2, MICS, LANES), jnp.float32),
            jax.ShapeDtypeStruct(conv2_w.shape, conv2_w.dtype),
            jax.ShapeDtypeStruct(proj_w.shape, proj_w.dtype),
        ),
        in_specs=[vmem] * 3 + [hbm] * 2 + [smem],
        out_specs=(vmem,) * 5,
        scratch_shapes=[
            pltpu.VMEM((frames * MICS, NFFT), jnp.float32),
            pltpu.VMEM((TILES, 2, frames, LANES), jnp.float32),
            pltpu.SemaphoreType.DMA((2,)),
        ],
        compiler_params=params,
        name="stats",
    )(waves, levels, table, in_hbm(conv2_w), in_hbm(proj_w), valid)
    edge_spec, mine, theirs = pl.pallas_call(
        functools.partial(edges_kernel, lax.axis_size("tm")),
        out_shape=(jax.ShapeDtypeStruct((2 * TILES, MICS * MICS, LANES), jnp.float32), stat_block, stat_block),
        in_specs=[vmem] * 7,
        out_specs=(vmem,) * 3,
        scratch_shapes=[pltpu.VMEM((MICS * MICS, NFFT), jnp.float32)],
        compiler_params=params,
        name="edges",
    )(beside, across, got_beside, got_across, table, edge_weight, kept)
    stats = summed_over_chips(mine + flipped(theirs, "tm", 1), "tm")
    beam = jax.ShapeDtypeStruct((2 * MICS, LANES), jnp.float32)
    beam_mine, beam_last = pl.pallas_call(
        solve_kernel,
        out_shape=(beam, beam),
        in_specs=[vmem, smem],
        out_specs=(vmem, vmem),
        compiler_params=params,
        name="solve",
    )(stats, ref_mic)
    beam_theirs = flipped(beam_mine, "tm", 1)
    rows = frames + MICS
    bank = packed_mel_bank()
    mel = pl.pallas_call(
        power_kernel,
        out_shape=jax.ShapeDtypeStruct((rows, 2 * LANES), jnp.float32),
        in_specs=[vmem] * 5,
        out_specs=vmem,
        compiler_params=params,
        name="power",
    )(beam_mine, beam_last, spec, edge_spec, bank)
    return pl.pallas_call(
        functools.partial(stem_kernel, frames),
        out_shape=jax.ShapeDtypeStruct((1, frames // 4, width), jnp.bfloat16),
        in_specs=[vmem] * 4 + [smem] + [vmem] * 7,
        out_specs=vmem,
        scratch_shapes=[pltpu.VMEM((2, rows, LANES), jnp.float32), pltpu.VMEM((LANES, channels), jnp.float32)],
        compiler_params=params,
        name="stem",
    )(
        beam_theirs,
        mel,
        spec,
        edge_spec,
        valid,
        bank,
        conv1_w,
        conv1_b[None],
        conv2_w,
        conv2_b[None],
        proj_w,
        proj_b[None],
    )


def solution(mesh):
    return jax.shard_map(
        per_device,
        mesh=mesh,
        in_specs=(
            P(None, ("meet", "tm")),
            P(None, ("meet", "tm"), None),
            P("meet"),
            P("meet"),
            P(),
            P(),
            P(),
            P(),
            P(),
            P(),
        ),
        out_specs=P(None, ("meet", "tm"), None),
        check_vma=False,
    )
```

```python
import functools
import math

import jax
import jax.numpy as jnp
import numpy as np
from jax import lax
from jax.experimental import pallas as pl
from jax.experimental.pallas import tpu as pltpu
from jax.sharding import PartitionSpec as P

NFFT = 512
HOP = 160
MELS = 80
BINS = NFFT // 2 + 1
LANES = 128
MICS = 8
PAD_BINS = -(-BINS // LANES) * LANES
TILES = PAD_BINS // LANES
HALO = 3
LEAD = 512
TAIL = 384
STATS = 2 * MICS * MICS
SPAN = 42

loading = 0.03
epsilon = 1e-06
sample_rate = 16000.0


def dft_table():
    n = np.arange(NFFT)
    f = np.arange(BINS)
    phase = 2.0 * math.pi * ((n[:, None] * f[None, :]) % NFFT) / NFFT
    window = 0.5 - 0.5 * np.cos(2.0 * math.pi * n / NFFT)
    table = np.zeros((NFFT, 2, PAD_BINS), np.float32)
    table[:, 0, :BINS] = window[:, None] * np.cos(phase)
    table[:, 1, :BINS] = -window[:, None] * np.sin(phase)
    return jnp.asarray(table.reshape(NFFT, 2 * PAD_BINS)).astype(jnp.bfloat16)


def mel_bank():
    mel_top = 2595.0 * math.log10(1.0 + sample_rate / 2.0 / 700.0)
    points = np.arange(MELS + 2) * (mel_top / (MELS + 1))
    edges = 700.0 * (np.power(10.0, points / 2595.0) - 1.0)
    freq = np.arange(BINS) * (sample_rate / 2.0 / (BINS - 1))
    lower, centre, upper = edges[:-2], edges[1:-1], edges[2:]
    rising = (freq[:, None] - lower[None, :]) / (centre - lower)[None, :]
    falling = (upper[None, :] - freq[:, None]) / (upper - centre)[None, :]
    return np.maximum(np.minimum(rising, falling), 0.0).astype(np.float32)


def packed_mel_bank():
    bank = mel_bank()
    packed = np.zeros((PAD_BINS, 2, LANES), np.float32)
    for half in range(2):
        part = bank[:, half * 40 : half * 40 + SPAN]
        for copy in range(3):
            packed[:BINS, half, copy * SPAN : copy * SPAN + part.shape[1]] = part
    return jnp.asarray(packed.reshape(TILES, LANES, 2 * LANES))


def cyclic_pairs(x_re, x_im):
    pairs = [x_re * x_re + x_im * x_im]
    for shift in range(1, MICS // 2 + 1):
        y_re = pltpu.roll(x_re, MICS - shift, 0)
        y_im = pltpu.roll(x_im, MICS - shift, 0)
        pairs.append(x_re * y_re + x_im * y_im)
        pairs.append(x_im * y_re - x_re * y_im)
    return pairs


def add_frame(sums, x_re, x_im, weights):
    pairs = cyclic_pairs(x_re, x_im)
    out = []
    for k in range(2):
        w = jnp.broadcast_to(weights[k], (MICS, LANES))
        out.extend(sums[k * len(pairs) + i] + w * pair for i, pair in enumerate(pairs))
    return tuple(out)


def kept_sums(sums):
    low = lax.broadcasted_iota(jnp.int32, (MICS, LANES), 0) < MICS // 2
    kept = []
    for k in range(2):
        own = sums[9 * k : 9 * k + 9]
        kept.extend(list(own[:7]) + [jnp.where(low, own[7], own[8])])
    return jnp.concatenate(kept, axis=0)


def slot_tiles(position):
    core = position % 2
    return core, 1 - core, TILES - 1


def started(pairs, sem):
    copies = [pltpu.make_async_copy(source, target, sem.at[i]) for i, (source, target) in enumerate(pairs)]
    for copy in copies:
        copy.start()
    return copies


def rims_kernel(wave_hbm, masks_hbm, table_hbm, beside_ref, across_ref, wave_ref, masks_ref, table_ref, sem):
    copies = started(((wave_hbm, wave_ref), (table_hbm, table_ref), (masks_hbm, masks_ref)), sem)
    even = lax.axis_index("tm") % 2 == 0
    copies[0].wait()
    head = wave_ref[:, :LEAD].astype(jnp.float32)
    tail = wave_ref[:, wave_ref.shape[1] - LEAD :].astype(jnp.float32)
    beside_ref[...] = jnp.where(even, tail, head).astype(beside_ref.dtype)
    across_ref[...] = jnp.where(even, head, tail).astype(across_ref.dtype)
    copies[1].wait()
    copies[2].wait()


def stats_kernel(frames, wave_ref, masks_ref, table_ref, conv2_w_hbm, proj_w_hbm, valid_ref, spec_ref, kept_ref, edge_weight_ref, conv2_w_ref, proj_w_ref, framed_ref, weight_ref, sem):
    copies = started(((conv2_w_hbm, conv2_w_ref), (proj_w_hbm, proj_w_ref)), sem)
    position = lax.axis_index("tm")
    wave = wave_ref[...].astype(jnp.float32)
    width = wave.shape[1]
    rolled = {}
    for frame in range(frames - HALO):
        base, shift = frame * HOP // LANES * LANES, frame * HOP % LANES
        if shift not in rolled:
            rolled[shift] = wave if shift == 0 else pltpu.roll(wave, width - shift, 1)
        framed_ref[MICS * frame : MICS * (frame + 1), :] = rolled[shift][:, base : base + NFFT]
    framed_ref[MICS * (frames - HALO) :, :] = jnp.zeros((MICS * HALO, NFFT), jnp.float32)
    spec = jnp.dot(framed_ref[...].astype(jnp.bfloat16), table_ref[...], preferred_element_type=jnp.float32)
    for tile in range(2 * TILES):
        spec_ref[tile] = spec[:, tile * LANES : (tile + 1) * LANES]

    row = lax.broadcasted_iota(jnp.int32, (frames, 1), 0)
    live = jnp.where(position * frames + row < valid_ref[0], 1.0 / 255.0, 0.0)
    weight_ref[TILES - 1] = jnp.zeros((2, frames, LANES), jnp.float32)
    for k in range(2):
        weight = masks_ref[k].astype(jnp.float32) * live
        for tile in range(TILES):
            kept_lanes = min(LANES, BINS - tile * LANES)
            weight_ref[tile, k, :, :kept_lanes] = weight[:, tile * LANES : tile * LANES + kept_lanes]
    edge_weight_ref[...] = weight_ref[:, :, frames - MICS :, :]

    for slot, tile in enumerate(slot_tiles(position)):

        def add_frames(group, sums):
            first = pl.multiple_of(group * MICS, MICS)
            weights = [weight_ref[tile, k, pl.ds(first, MICS), :] for k in range(2)]
            for frame in range(MICS):
                rows = pl.ds(pl.multiple_of((first + frame) * MICS, MICS), MICS)
                sums = add_frame(
                    sums, spec_ref[tile, rows, :], spec_ref[TILES + tile, rows, :], [w[frame : frame + 1] for w in weights]
                )
            return sums

        zero = jnp.zeros((MICS, LANES), jnp.float32)
        kept_ref[slot] = kept_sums(lax.fori_loop(0, frames // MICS, add_frames, (zero,) * 18))
    for copy in copies:
        copy.wait()


def edges_kernel(devices, own0_ref, own1_ref, got0_ref, got1_ref, table_ref, edge_weight_ref, kept_ref, spec_ref, mine_ref, theirs_ref, framed_ref):
    position = lax.axis_index("tm")
    even = position % 2 == 0
    own = [own0_ref[...].astype(jnp.float32), own1_ref[...].astype(jnp.float32)]
    got = [got0_ref[...].astype(jnp.float32), got1_ref[...].astype(jnp.float32)]
    head, tail = jnp.where(even, own[1], own[0]), jnp.where(even, own[0], own[1])
    prev, after = jnp.where(even, got[1], got[0]), jnp.where(even, got[0], got[1])
    prev = jnp.where(position > 0, prev, 0.0)
    after = jnp.where(position < devices - 1, after, 0.0)
    joined = jnp.concatenate(
        [jnp.concatenate([prev, head[:, :TAIL]], axis=1), jnp.concatenate([tail, after[:, :TAIL]], axis=1)], axis=0
    )
    for i in range(HALO):
        start = LEAD - HALO * HOP + i * HOP
        base, shift = start // LANES * LANES, start % LANES
        turned = joined if shift == 0 else pltpu.roll(joined, joined.shape[1] - shift, 1)
        framed_ref[2 * MICS * i : 2 * MICS * (i + 1), :] = turned[:, base : base + NFFT]
    used = 2 * MICS * HALO
    framed_ref[used:, :] = jnp.zeros((framed_ref.shape[0] - used, NFFT), jnp.float32)
    spec = jnp.dot(framed_ref[...].astype(jnp.bfloat16), table_ref[...], preferred_element_type=jnp.float32)
    for tile in range(2 * TILES):
        spec_ref[tile] = spec[:, tile * LANES : (tile + 1) * LANES]
    for slot, tile in enumerate(slot_tiles(position)):
        sums = (jnp.zeros((MICS, LANES), jnp.float32),) * 18
        for i in range(HALO):
            rows = slice((2 * i + 1) * MICS, (2 * i + 2) * MICS)
            at = MICS - HALO + i
            weights = [edge_weight_ref[tile, k, at : at + 1, :] for k in range(2)]
            sums = add_frame(sums, spec_ref[tile, rows, :], spec_ref[TILES + tile, rows, :], weights)
        total = kept_ref[slot] + kept_sums(sums)
        if slot == 0:
            mine_ref[:STATS, :] = total
        elif slot == 1:
            theirs_ref[:STATS, :] = total
        else:
            last_bin = jnp.transpose(total)[:MICS]
            mine_ref[STATS:, :] = last_bin
            theirs_ref[STATS:, :] = last_bin


def columns_of(kept, sub):
    low = sub < MICS // 2
    diag_re = [kept[0], kept[1], kept[3], kept[5]]
    diag_im = [jnp.zeros_like(kept[0]), kept[2], kept[4], kept[6]]
    turned = pltpu.roll(kept[7], MICS // 2, 0)
    diag_re.append(jnp.where(low, kept[7], turned))
    diag_im.append(jnp.where(low, -turned, kept[7]))
    for shift in range(MICS // 2 + 1, MICS):
        diag_re.append(pltpu.roll(diag_re[MICS - shift], MICS - shift, 0))
        diag_im.append(-pltpu.roll(diag_im[MICS - shift], MICS - shift, 0))
    columns = []
    for n in range(MICS):
        re, im = diag_re[n], diag_im[n]
        for m in range(1, MICS):
            re = jnp.where(sub == m, diag_re[(n - m) % MICS], re)
            im = jnp.where(sub == m, diag_im[(n - m) % MICS], im)
        columns.append((re, im))
    return columns


def beams_of(stats, ref_mic):
    sub = lax.broadcasted_iota(jnp.int32, stats[0].shape, 0)
    answer = columns_of(stats[:MICS], sub)
    matrix = columns_of(stats[MICS:], sub)
    spread = jnp.sum(stats[MICS], axis=0, keepdims=True)
    ridge = loading * spread / MICS + epsilon
    matrix = [(jnp.where(sub == n, re + ridge, re), im) for n, (re, im) in enumerate(matrix)]
    for pivot in range(MICS):
        col_re, col_im = matrix[pivot]
        pivot_re = col_re[pivot : pivot + 1]
        pivot_im = col_im[pivot : pivot + 1]
        modulus = pivot_re * pivot_re + pivot_im * pivot_im
        inverse_re = pivot_re / modulus
        inverse_im = -pivot_im / modulus

        def eliminated(column):
            re, im = column
            row_re, row_im = re[pivot : pivot + 1], im[pivot : pivot + 1]
            lead_re = row_re * inverse_re - row_im * inverse_im
            lead_im = row_re * inverse_im + row_im * inverse_re
            return (
                jnp.where(sub == pivot, lead_re, re - (col_re * lead_re - col_im * lead_im)),
                jnp.where(sub == pivot, lead_im, im - (col_re * lead_im + col_im * lead_re)),
            )

        matrix = [eliminated(c) if n > pivot else c for n, c in enumerate(matrix)]
        answer = [eliminated(c) for c in answer]
    trace = answer[0][0][0:1]
    beam_re, beam_im = answer[0]
    for n in range(1, MICS):
        trace = trace + answer[n][0][n : n + 1]
        beam_re = jnp.where(ref_mic == n, answer[n][0], beam_re)
        beam_im = jnp.where(ref_mic == n, answer[n][1], beam_im)
    scale = 1.0 / (trace + epsilon)
    return beam_re * scale, beam_im * scale


def solve_kernel(stats_ref, ref_mic_ref, beam_ref, last_ref):
    blank = jnp.zeros((LANES - MICS, LANES), jnp.float32)
    last_bin = jnp.transpose(jnp.concatenate([stats_ref[STATS:, :], blank], axis=0))
    for out_ref, stats in ((beam_ref, stats_ref[:STATS, :]), (last_ref, last_bin)):
        kept = [stats[i * MICS : (i + 1) * MICS] for i in range(2 * MICS)]
        beam_re, beam_im = beams_of(kept, ref_mic_ref[0])
        out_ref[:MICS, :] = beam_re
        out_ref[MICS:, :] = beam_im


def power_of(beam_ref, tile, spec_ref, edge_spec_ref):
    beam_re, beam_im = beam_ref[:MICS, :], beam_ref[MICS:, :]
    groups = spec_ref.shape[1] // (MICS * MICS)
    power = []
    for group in range(groups + 1):
        from_ref, first = (spec_ref, group * MICS * MICS) if group < groups else (edge_spec_ref, 0)
        sum_re = sum_im = None
        for m in range(MICS):
            rows = pl.ds(first + m, MICS, stride=MICS)
            x_re, x_im = from_ref[tile, rows, :], from_ref[TILES + tile, rows, :]
            b_re, b_im = beam_re[m : m + 1], beam_im[m : m + 1]
            part_re = b_re * x_re + b_im * x_im
            part_im = b_re * x_im - b_im * x_re
            sum_re = part_re if sum_re is None else sum_re + part_re
            sum_im = part_im if sum_im is None else sum_im + part_im
        power.append(sum_re * sum_re + sum_im * sum_im)
    return jnp.concatenate(power, axis=0)


def mel_of(power, bank):
    return jnp.dot(power, bank, precision=lax.Precision.HIGHEST, preferred_element_type=jnp.float32)


def power_kernel(mine_ref, last_ref, spec_ref, edge_spec_ref, bank_ref, mel_ref):
    mine, _, last = slot_tiles(lax.axis_index("tm"))
    power = [power_of(beam_ref, tile, spec_ref, edge_spec_ref) for beam_ref, tile in ((mine_ref, mine), (last_ref, last))]
    bank = jnp.concatenate([bank_ref[mine], bank_ref[last]], axis=0)
    mel_ref[...] = mel_of(jnp.concatenate(power, axis=1), bank)


def stem_kernel(frames, theirs_ref, mel_ref, spec_ref, edge_spec_ref, valid_ref, bank_ref, conv1_w_ref, conv1_b_ref, conv2_w_ref, conv2_b_ref, proj_w_ref, proj_b_ref, out_ref, logmel_ref, conv1_ref):
    position = lax.axis_index("tm")
    valid = valid_ref[0]
    quarter = frames // 4
    channels = conv1_w_ref.shape[1]
    conv1_ref[...] = jnp.zeros((LANES, channels), jnp.float32)
    for shift_t in range(3):
        conv1_ref[SPAN * shift_t : SPAN * shift_t + 3, :] = conv1_w_ref[3 * shift_t : 3 * shift_t + 3, :].astype(jnp.float32)
    conv1 = conv1_ref[...].astype(jnp.bfloat16)

    theirs = slot_tiles(position)[1]
    mel = mel_ref[...] + mel_of(power_of(theirs_ref, theirs, spec_ref, edge_spec_ref), bank_ref[theirs])
    row = lax.broadcasted_iota(jnp.int32, (frames + MICS, 1), 0)
    edge = (row - frames) // 2 + jnp.where((row - frames) % 2 == 0, -HALO, frames - HALO)
    time = position * frames + jnp.where(row < frames, row, edge)
    live = (time >= 0) & (time < valid)
    logmel = jnp.where(live, jnp.log(mel + epsilon), 0.0)
    logmel = logmel.astype(jnp.bfloat16).astype(jnp.float32)
    for half in range(2):
        part = logmel[:, half * LANES : (half + 1) * LANES]
        logmel_ref[half, HALO : HALO + frames, :] = part[:frames]
        for i in range(HALO):
            logmel_ref[half, i : i + 1, :] = part[frames + 2 * i : frames + 2 * i + 1]
            logmel_ref[half, frames + i : frames + i + 1, :] = part[frames + 2 * i + 1 : frames + 2 * i + 2]

    q_first = (MELS - 3) // 2 + 1
    q_second = (q_first - 3) // 2 + 1
    order = list(range(0, q_first, 2)) + list(range(1, q_first, 2))
    evens = (q_first + 1) // 2
    lane = lax.broadcasted_iota(jnp.int32, (quarter, LANES), 1)
    row = lax.broadcasted_iota(jnp.int32, (quarter, 1), 0)
    windows = []
    for tap in range(3):
        packs = []
        for half in range(2):
            rows = [logmel_ref[half, pl.ds(2 * tap + a, quarter, stride=4), :] for a in range(3)]
            packs.append(jnp.where(lane < SPAN, rows[0], jnp.where(lane < 2 * SPAN, rows[1], rows[2])))
        patches = []
        for q in order:
            half, shift = (0, 2 * q) if q < 20 else (1, 2 * q - 40)
            patches.append(packs[half] if shift == 0 else pltpu.roll(packs[half], LANES - shift, 1))
        patches = jnp.concatenate(patches, axis=0).astype(jnp.bfloat16)
        layer = jnp.dot(patches, conv1, preferred_element_type=jnp.float32) + conv1_b_ref[...]
        layer = jnp.maximum(layer, 0.0)
        if tap == 0:
            keep = jnp.concatenate([row + 2 * quarter * position >= 1] * q_first, axis=0)
            layer = jnp.where(keep, layer, 0.0)
        layer = layer.astype(jnp.bfloat16)
        count = quarter * q_second
        windows.append(layer[:count])
        windows.append(layer[quarter * evens : quarter * evens + count])
        windows.append(layer[quarter : quarter + count])
    second = jnp.dot(jnp.concatenate(windows, axis=1), conv2_w_ref[...], preferred_element_type=jnp.float32)
    second = jnp.maximum(second + conv2_b_ref[...], 0.0).astype(jnp.bfloat16)
    flat = jnp.concatenate([second[quarter * r : quarter * (r + 1)] for r in range(q_second)], axis=1)
    features = jnp.dot(flat, proj_w_ref[...], preferred_element_type=jnp.float32) + proj_b_ref[...]
    features = jnp.where(position * frames + 4 * row < valid, features, 0.0)
    out_ref[0] = features.astype(jnp.bfloat16)


def flipped(block, axis, step):
    size = lax.axis_size(axis)
    return lax.ppermute(block, axis, [(i, i ^ step) for i in range(size)])


def summed_over_chips(block, axis):
    size = lax.axis_size(axis)
    if size & (size - 1):
        return lax.psum(block, axis, axis_index_groups=[list(range(c, size, 2)) for c in range(2)])
    step = 2
    while step < size:
        others = [step] if 2 * step >= size else [step, 2 * step, 3 * step]
        block = sum([flipped(block, axis, other) for other in others], block)
        step *= 4
    return block


def paired(block, first):
    size, meets = lax.axis_size("tm"), lax.axis_size("meet")
    pairs = []
    for meet in range(meets):
        at = meet * size
        pairs += [(at + i, at + i + 1) for i in range(first, size - 1, 2)]
        if first and meets % 2:
            pairs.append((at, at + size - 1))
        elif first and meet % 2 == 0:
            pairs += [(at + end, at + size + end) for end in (0, size - 1)]
    return lax.ppermute(block, ("meet", "tm"), pairs + [(j, i) for i, j in pairs])


def per_device(waveform, masks, valid, ref_mic, conv1_w, conv1_b, conv2_w, conv2_b, proj_w, proj_b):
    frames = masks.shape[1]
    channels = conv1_w.shape[1]
    width = proj_w.shape[1]
    vmem = pl.BlockSpec(memory_space=pltpu.VMEM)
    smem = pl.BlockSpec(memory_space=pltpu.SMEM)
    hbm = pl.BlockSpec(memory_space=pltpu.HBM)
    in_hbm = functools.partial(pltpu.with_memory_space_constraint, memory_space=pltpu.HBM)
    params = pltpu.CompilerParams(vmem_limit_bytes=16 * 1024 * 1024)
    rim = jax.ShapeDtypeStruct((MICS, LEAD), waveform.dtype)
    table = dft_table()
    conv2_w = conv2_w.reshape(-1, channels)
    beside, across, waves, levels, table = pl.pallas_call(
        rims_kernel,
        out_shape=(rim, rim) + tuple(jax.ShapeDtypeStruct(x.shape, x.dtype) for x in (waveform, masks, table)),
        in_specs=[hbm] * 3,
        out_specs=(vmem,) * 5,
        scratch_shapes=[pltpu.SemaphoreType.DMA((3,))],
        compiler_params=params,
        name="rims",
    )(in_hbm(waveform), in_hbm(masks), in_hbm(table))
    got_across = paired(across, 1)
    got_beside = paired(beside, 0)
    stat_block = jax.ShapeDtypeStruct((STATS + MICS, LANES), jnp.float32)
    spec, kept, edge_weight, conv2_w, proj_w = pl.pallas_call(
        functools.partial(stats_kernel, frames),
        out_shape=(
            jax.ShapeDtypeStruct((2 * TILES, frames * MICS, LANES), jnp.float32),
            jax.ShapeDtypeStruct((TILES, STATS, LANES), jnp.float32),
            jax.ShapeDtypeStruct((TILES, 2, MICS, LANES), jnp.float32),
            jax.ShapeDtypeStruct(conv2_w.shape, conv2_w.dtype),
            jax.ShapeDtypeStruct(proj_w.shape, proj_w.dtype),
        ),
        in_specs=[vmem] * 3 + [hbm] * 2 + [smem],
        out_specs=(vmem,) * 5,
        scratch_shapes=[
            pltpu.VMEM((frames * MICS, NFFT), jnp.float32),
            pltpu.VMEM((TILES, 2, frames, LANES), jnp.float32),
            pltpu.SemaphoreType.DMA((2,)),
        ],
        compiler_params=params,
        name="stats",
    )(waves, levels, table, in_hbm(conv2_w), in_hbm(proj_w), valid)
    edge_spec, mine, theirs = pl.pallas_call(
        functools.partial(edges_kernel, lax.axis_size("tm")),
        out_shape=(jax.ShapeDtypeStruct((2 * TILES, MICS * MICS, LANES), jnp.float32), stat_block, stat_block),
        in_specs=[vmem] * 7,
        out_specs=(vmem,) * 3,
        scratch_shapes=[pltpu.VMEM((MICS * MICS, NFFT), jnp.float32)],
        compiler_params=params,
        name="edges",
    )(beside, across, got_beside, got_across, table, edge_weight, kept)
    stats = summed_over_chips(mine + flipped(theirs, "tm", 1), "tm")
    beam = jax.ShapeDtypeStruct((2 * MICS, LANES), jnp.float32)
    beam_mine, beam_last = pl.pallas_call(
        solve_kernel,
        out_shape=(beam, beam),
        in_specs=[vmem, smem],
        out_specs=(vmem, vmem),
        compiler_params=params,
        name="solve",
    )(stats, ref_mic)
    beam_theirs = flipped(beam_mine, "tm", 1)
    rows = frames + MICS
    bank = packed_mel_bank()
    mel = pl.pallas_call(
        power_kernel,
        out_shape=jax.ShapeDtypeStruct((rows, 2 * LANES), jnp.float32),
        in_specs=[vmem] * 5,
        out_specs=vmem,
        compiler_params=params,
        name="power",
    )(beam_mine, beam_last, spec, edge_spec, bank)
    return pl.pallas_call(
        functools.partial(stem_kernel, frames),
        out_shape=jax.ShapeDtypeStruct((1, frames // 4, width), jnp.bfloat16),
        in_specs=[vmem] * 4 + [smem] + [vmem] * 7,
        out_specs=vmem,
        scratch_shapes=[pltpu.VMEM((2, rows, LANES), jnp.float32), pltpu.VMEM((LANES, channels), jnp.float32)],
        compiler_params=params,
        name="stem",
    )(
        beam_theirs,
        mel,
        spec,
        edge_spec,
        valid,
        bank,
        conv1_w,
        conv1_b[None],
        conv2_w,
        conv2_b[None],
        proj_w,
        proj_b[None],
    )


def solution(mesh):
    return jax.shard_map(
        per_device,
        mesh=mesh,
        in_specs=(
            P(None, ("meet", "tm")),
            P(None, ("meet", "tm"), None),
            P("meet"),
            P("meet"),
            P(),
            P(),
            P(),
            P(),
            P(),
            P(),
        ),
        out_specs=P(None, ("meet", "tm"), None),
        check_vma=False,
    )
```

```python
import functools
import math

import jax
import jax.numpy as jnp
import numpy as np
from jax import lax
from jax.experimental import pallas as pl
from jax.experimental.pallas import tpu as pltpu
from jax.sharding import PartitionSpec as P

NFFT = 512
HOP = 160
MELS = 80
BINS = NFFT // 2 + 1
LANES = 128
MICS = 8
PAD_BINS = -(-BINS // LANES) * LANES
TILES = PAD_BINS // LANES
HALO = 3
LEAD = 512
TAIL = 384
STATS = 2 * MICS * MICS
SPAN = 42

loading = 0.03
epsilon = 1e-06
sample_rate = 16000.0


def dft_table():
    n = np.arange(NFFT)
    f = np.arange(BINS)
    phase = 2.0 * math.pi * ((n[:, None] * f[None, :]) % NFFT) / NFFT
    window = 0.5 - 0.5 * np.cos(2.0 * math.pi * n / NFFT)
    table = np.zeros((NFFT, 2, PAD_BINS), np.float32)
    table[:, 0, :BINS] = window[:, None] * np.cos(phase)
    table[:, 1, :BINS] = -window[:, None] * np.sin(phase)
    return jnp.asarray(table.reshape(NFFT, 2 * PAD_BINS)).astype(jnp.bfloat16)


def mel_bank():
    mel_top = 2595.0 * math.log10(1.0 + sample_rate / 2.0 / 700.0)
    points = np.arange(MELS + 2) * (mel_top / (MELS + 1))
    edges = 700.0 * (np.power(10.0, points / 2595.0) - 1.0)
    freq = np.arange(BINS) * (sample_rate / 2.0 / (BINS - 1))
    lower, centre, upper = edges[:-2], edges[1:-1], edges[2:]
    rising = (freq[:, None] - lower[None, :]) / (centre - lower)[None, :]
    falling = (upper[None, :] - freq[:, None]) / (upper - centre)[None, :]
    return np.maximum(np.minimum(rising, falling), 0.0).astype(np.float32)


def packed_mel_bank():
    bank = mel_bank()
    packed = np.zeros((PAD_BINS, 2, LANES), np.float32)
    for half in range(2):
        part = bank[:, half * 40 : half * 40 + SPAN]
        for copy in range(3):
            packed[:BINS, half, copy * SPAN : copy * SPAN + part.shape[1]] = part
    return jnp.asarray(packed.reshape(TILES, LANES, 2 * LANES))


def cyclic_pairs(x_re, x_im):
    pairs = [x_re * x_re + x_im * x_im]
    for shift in range(1, MICS // 2 + 1):
        y_re = pltpu.roll(x_re, MICS - shift, 0)
        y_im = pltpu.roll(x_im, MICS - shift, 0)
        pairs.append(x_re * y_re + x_im * y_im)
        pairs.append(x_im * y_re - x_re * y_im)
    return pairs


def add_frame(sums, x_re, x_im, weights):
    pairs = cyclic_pairs(x_re, x_im)
    out = []
    for k in range(2):
        w = jnp.broadcast_to(weights[k], (MICS, LANES))
        out.extend(sums[k * len(pairs) + i] + w * pair for i, pair in enumerate(pairs))
    return tuple(out)


def kept_sums(sums):
    low = lax.broadcasted_iota(jnp.int32, (MICS, LANES), 0) < MICS // 2
    kept = []
    for k in range(2):
        own = sums[9 * k : 9 * k + 9]
        kept.extend(list(own[:7]) + [jnp.where(low, own[7], own[8])])
    return jnp.concatenate(kept, axis=0)


def slot_tiles(position):
    core = position % 2
    return core, 1 - core, TILES - 1


def started(pairs, sem):
    copies = [pltpu.make_async_copy(source, target, sem.at[i]) for i, (source, target) in enumerate(pairs)]
    for copy in copies:
        copy.start()
    return copies


def rims_kernel(frames, wave_hbm, masks_hbm, table_hbm, beside_ref, across_ref, framed_ref, masks_ref, table_ref, wave_ref, sem):
    copies = started(((wave_hbm, wave_ref), (table_hbm, table_ref), (masks_hbm, masks_ref)), sem)
    even = lax.axis_index("tm") % 2 == 0
    copies[0].wait()
    head = wave_ref[:, :LEAD].astype(jnp.float32)
    tail = wave_ref[:, wave_ref.shape[1] - LEAD :].astype(jnp.float32)
    beside_ref[...] = jnp.where(even, tail, head).astype(beside_ref.dtype)
    across_ref[...] = jnp.where(even, head, tail).astype(across_ref.dtype)
    wave = wave_ref[...].astype(jnp.float32)
    width = wave.shape[1]
    rolled = {}

    def frame_of(frame):
        if frame >= frames - HALO:
            return jnp.zeros((MICS, NFFT), jnp.float32)
        base, shift = frame * HOP // LANES * LANES, frame * HOP % LANES
        if shift not in rolled:
            rolled[shift] = wave if shift == 0 else pltpu.roll(wave, width - shift, 1)
        return rolled[shift][:, base : base + NFFT]

    for frame in range(0, frames, 2):
        pair = jnp.concatenate([frame_of(frame), frame_of(frame + 1)], axis=0)
        framed_ref[MICS * frame : MICS * (frame + 2), :] = pair.astype(framed_ref.dtype)
    copies[1].wait()
    copies[2].wait()


def last_bin_sums(frames, spec_ref, weight_ref):
    x_re = x_im = jnp.zeros((MICS, LANES), jnp.float32)
    for frame in range(frames):
        rows = slice(MICS * frame, MICS * (frame + 1))
        part_re, part_im = spec_ref[TILES - 1, rows, :], spec_ref[2 * TILES - 1, rows, :]
        x_re = x_re + (pltpu.roll(part_re, frame, 1) if frame else part_re)
        x_im = x_im + (pltpu.roll(part_im, frame, 1) if frame else part_im)
    frame = lax.broadcasted_iota(jnp.int32, (frames, LANES), 0)
    lane = lax.broadcasted_iota(jnp.int32, (frames, LANES), 1)
    sums = []
    for k in range(2):
        weight = weight_ref[TILES - 1, k][:, :1]
        weight = jnp.sum(jnp.where(frame == lane, weight, 0.0), axis=0, keepdims=True)
        for pair in cyclic_pairs(x_re, x_im):
            total = jnp.sum(pair * weight, axis=1, keepdims=True)
            sums.append(jnp.where(lane[:MICS] == 0, total, 0.0))
    return kept_sums(sums)


def stats_kernel(frames, framed_ref, masks_ref, table_ref, conv2_w_hbm, proj_w_hbm, valid_ref, spec_ref, kept_ref, edge_weight_ref, conv2_w_ref, proj_w_ref, weight_ref, sem):
    copies = started(((conv2_w_hbm, conv2_w_ref), (proj_w_hbm, proj_w_ref)), sem)
    position = lax.axis_index("tm")
    spec = jnp.dot(framed_ref[...], table_ref[...], preferred_element_type=jnp.float32)
    for tile in range(2 * TILES):
        spec_ref[tile] = spec[:, tile * LANES : (tile + 1) * LANES]

    row = lax.broadcasted_iota(jnp.int32, (frames, 1), 0)
    live = jnp.where(position * frames + row < valid_ref[0], 1.0 / 255.0, 0.0)
    weight_ref[TILES - 1] = jnp.zeros((2, frames, LANES), jnp.float32)
    for k in range(2):
        weight = masks_ref[k].astype(jnp.float32) * live
        for tile in range(TILES):
            kept_lanes = min(LANES, BINS - tile * LANES)
            weight_ref[tile, k, :, :kept_lanes] = weight[:, tile * LANES : tile * LANES + kept_lanes]
    edge_weight_ref[...] = weight_ref[:, :, frames - MICS :, :]

    for slot, tile in enumerate(slot_tiles(position)[:2]):

        def add_frames(group, sums):
            first = pl.multiple_of(group * MICS, MICS)
            weights = [weight_ref[tile, k, pl.ds(first, MICS), :] for k in range(2)]
            for frame in range(MICS):
                rows = pl.ds(pl.multiple_of((first + frame) * MICS, MICS), MICS)
                sums = add_frame(
                    sums, spec_ref[tile, rows, :], spec_ref[TILES + tile, rows, :], [w[frame : frame + 1] for w in weights]
                )
            return sums

        zero = jnp.zeros((MICS, LANES), jnp.float32)
        kept_ref[slot] = kept_sums(lax.fori_loop(0, frames // MICS, add_frames, (zero,) * 18))
    kept_ref[2] = last_bin_sums(frames, spec_ref, weight_ref)
    for copy in copies:
        copy.wait()


def edges_kernel(devices, own0_ref, own1_ref, got0_ref, got1_ref, table_ref, edge_weight_ref, kept_ref, spec_ref, mine_ref, theirs_ref, framed_ref):
    position = lax.axis_index("tm")
    even = position % 2 == 0
    own = [own0_ref[...].astype(jnp.float32), own1_ref[...].astype(jnp.float32)]
    got = [got0_ref[...].astype(jnp.float32), got1_ref[...].astype(jnp.float32)]
    head, tail = jnp.where(even, own[1], own[0]), jnp.where(even, own[0], own[1])
    prev, after = jnp.where(even, got[1], got[0]), jnp.where(even, got[0], got[1])
    prev = jnp.where(position > 0, prev, 0.0)
    after = jnp.where(position < devices - 1, after, 0.0)
    joined = jnp.concatenate(
        [jnp.concatenate([prev, head[:, :TAIL]], axis=1), jnp.concatenate([tail, after[:, :TAIL]], axis=1)], axis=0
    )
    for i in range(HALO):
        start = LEAD - HALO * HOP + i * HOP
        base, shift = start // LANES * LANES, start % LANES
        turned = joined if shift == 0 else pltpu.roll(joined, joined.shape[1] - shift, 1)
        framed_ref[2 * MICS * i : 2 * MICS * (i + 1), :] = turned[:, base : base + NFFT]
    used = 2 * MICS * HALO
    framed_ref[used:, :] = jnp.zeros((framed_ref.shape[0] - used, NFFT), jnp.float32)
    spec = jnp.dot(framed_ref[...].astype(jnp.bfloat16), table_ref[...], preferred_element_type=jnp.float32)
    for tile in range(2 * TILES):
        spec_ref[tile] = spec[:, tile * LANES : (tile + 1) * LANES]
    for slot, tile in enumerate(slot_tiles(position)):
        sums = (jnp.zeros((MICS, LANES), jnp.float32),) * 18
        for i in range(HALO):
            rows = slice((2 * i + 1) * MICS, (2 * i + 2) * MICS)
            at = MICS - HALO + i
            weights = [edge_weight_ref[tile, k, at : at + 1, :] for k in range(2)]
            sums = add_frame(sums, spec_ref[tile, rows, :], spec_ref[TILES + tile, rows, :], weights)
        total = kept_ref[slot] + kept_sums(sums)
        if slot == 0:
            mine_ref[:STATS, :] = total
        elif slot == 1:
            theirs_ref[:STATS, :] = total
        else:
            last_bin = jnp.transpose(total)[:MICS]
            mine_ref[STATS:, :] = last_bin
            theirs_ref[STATS:, :] = last_bin


def columns_of(kept, sub):
    low = sub < MICS // 2
    diag_re = [kept[0], kept[1], kept[3], kept[5]]
    diag_im = [jnp.zeros_like(kept[0]), kept[2], kept[4], kept[6]]
    turned = pltpu.roll(kept[7], MICS // 2, 0)
    diag_re.append(jnp.where(low, kept[7], turned))
    diag_im.append(jnp.where(low, -turned, kept[7]))
    for shift in range(MICS // 2 + 1, MICS):
        diag_re.append(pltpu.roll(diag_re[MICS - shift], MICS - shift, 0))
        diag_im.append(-pltpu.roll(diag_im[MICS - shift], MICS - shift, 0))
    columns = []
    for n in range(MICS):
        re, im = diag_re[n], diag_im[n]
        for m in range(1, MICS):
            re = jnp.where(sub == m, diag_re[(n - m) % MICS], re)
            im = jnp.where(sub == m, diag_im[(n - m) % MICS], im)
        columns.append((re, im))
    return columns


def beams_of(stats, ref_mic):
    sub = lax.broadcasted_iota(jnp.int32, stats[0].shape, 0)
    answer = columns_of(stats[:MICS], sub)
    matrix = columns_of(stats[MICS:], sub)
    spread = jnp.sum(stats[MICS], axis=0, keepdims=True)
    ridge = loading * spread / MICS + epsilon
    matrix = [(jnp.where(sub == n, re + ridge, re), im) for n, (re, im) in enumerate(matrix)]
    for pivot in range(MICS):
        col_re, col_im = matrix[pivot]
        pivot_re = col_re[pivot : pivot + 1]
        pivot_im = col_im[pivot : pivot + 1]
        modulus = pivot_re * pivot_re + pivot_im * pivot_im
        inverse_re = pivot_re / modulus
        inverse_im = -pivot_im / modulus

        def eliminated(column):
            re, im = column
            row_re, row_im = re[pivot : pivot + 1], im[pivot : pivot + 1]
            lead_re = row_re * inverse_re - row_im * inverse_im
            lead_im = row_re * inverse_im + row_im * inverse_re
            return (
                jnp.where(sub == pivot, lead_re, re - (col_re * lead_re - col_im * lead_im)),
                jnp.where(sub == pivot, lead_im, im - (col_re * lead_im + col_im * lead_re)),
            )

        matrix = [eliminated(c) if n > pivot else c for n, c in enumerate(matrix)]
        answer = [eliminated(c) for c in answer]
    trace = answer[0][0][0:1]
    beam_re, beam_im = answer[0]
    for n in range(1, MICS):
        trace = trace + answer[n][0][n : n + 1]
        beam_re = jnp.where(ref_mic == n, answer[n][0], beam_re)
        beam_im = jnp.where(ref_mic == n, answer[n][1], beam_im)
    scale = 1.0 / (trace + epsilon)
    return beam_re * scale, beam_im * scale


def solve_kernel(stats_ref, ref_mic_ref, beam_ref, last_ref):
    blank = jnp.zeros((LANES - MICS, LANES), jnp.float32)
    last_bin = jnp.transpose(jnp.concatenate([stats_ref[STATS:, :], blank], axis=0))
    for out_ref, stats in ((beam_ref, stats_ref[:STATS, :]), (last_ref, last_bin)):
        kept = [stats[i * MICS : (i + 1) * MICS] for i in range(2 * MICS)]
        beam_re, beam_im = beams_of(kept, ref_mic_ref[0])
        out_ref[:MICS, :] = beam_re
        out_ref[MICS:, :] = beam_im


def power_of(beam_ref, tile, spec_ref, edge_spec_ref):
    beam_re, beam_im = beam_ref[:MICS, :], beam_ref[MICS:, :]
    groups = spec_ref.shape[1] // (MICS * MICS)
    power = []
    for group in range(groups + 1):
        from_ref, first = (spec_ref, group * MICS * MICS) if group < groups else (edge_spec_ref, 0)
        sum_re = sum_im = None
        for m in range(MICS):
            rows = pl.ds(first + m, MICS, stride=MICS)
            x_re, x_im = from_ref[tile, rows, :], from_ref[TILES + tile, rows, :]
            b_re, b_im = beam_re[m : m + 1], beam_im[m : m + 1]
            part_re = b_re * x_re + b_im * x_im
            part_im = b_re * x_im - b_im * x_re
            sum_re = part_re if sum_re is None else sum_re + part_re
            sum_im = part_im if sum_im is None else sum_im + part_im
        power.append(sum_re * sum_re + sum_im * sum_im)
    return jnp.concatenate(power, axis=0)


def mel_of(power, bank):
    return jnp.dot(power, bank, precision=lax.Precision.HIGHEST, preferred_element_type=jnp.float32)


def power_kernel(mine_ref, last_ref, spec_ref, edge_spec_ref, bank_ref, mel_ref):
    mine, _, last = slot_tiles(lax.axis_index("tm"))
    power = [power_of(beam_ref, tile, spec_ref, edge_spec_ref) for beam_ref, tile in ((mine_ref, mine), (last_ref, last))]
    bank = jnp.concatenate([bank_ref[mine], bank_ref[last]], axis=0)
    mel_ref[...] = mel_of(jnp.concatenate(power, axis=1), bank)


def stem_kernel(frames, theirs_ref, mel_ref, spec_ref, edge_spec_ref, valid_ref, bank_ref, conv1_w_ref, conv1_b_ref, conv2_w_ref, conv2_b_ref, proj_w_ref, proj_b_ref, out_ref, logmel_ref, conv1_ref):
    position = lax.axis_index("tm")
    valid = valid_ref[0]
    quarter = frames // 4
    channels = conv1_w_ref.shape[1]
    conv1_ref[...] = jnp.zeros((LANES, channels), jnp.float32)
    for shift_t in range(3):
        conv1_ref[SPAN * shift_t : SPAN * shift_t + 3, :] = conv1_w_ref[3 * shift_t : 3 * shift_t + 3, :].astype(jnp.float32)
    conv1 = conv1_ref[...].astype(jnp.bfloat16)

    theirs = slot_tiles(position)[1]
    mel = mel_ref[...] + mel_of(power_of(theirs_ref, theirs, spec_ref, edge_spec_ref), bank_ref[theirs])
    row = lax.broadcasted_iota(jnp.int32, (frames + MICS, 1), 0)
    edge = (row - frames) // 2 + jnp.where((row - frames) % 2 == 0, -HALO, frames - HALO)
    time = position * frames + jnp.where(row < frames, row, edge)
    live = (time >= 0) & (time < valid)
    logmel = jnp.where(live, jnp.log(mel + epsilon), 0.0)
    logmel = logmel.astype(jnp.bfloat16).astype(jnp.float32)
    for half in range(2):
        part = logmel[:, half * LANES : (half + 1) * LANES]
        logmel_ref[half, HALO : HALO + frames, :] = part[:frames]
        for i in range(HALO):
            logmel_ref[half, i : i + 1, :] = part[frames + 2 * i : frames + 2 * i + 1]
            logmel_ref[half, frames + i : frames + i + 1, :] = part[frames + 2 * i + 1 : frames + 2 * i + 2]

    q_first = (MELS - 3) // 2 + 1
    q_second = (q_first - 3) // 2 + 1
    order = list(range(0, q_first, 2)) + list(range(1, q_first, 2))
    evens = (q_first + 1) // 2
    lane = lax.broadcasted_iota(jnp.int32, (quarter, LANES), 1)
    row = lax.broadcasted_iota(jnp.int32, (quarter, 1), 0)
    windows = []
    for tap in range(3):
        packs = []
        for half in range(2):
            rows = [logmel_ref[half, pl.ds(2 * tap + a, quarter, stride=4), :] for a in range(3)]
            packs.append(jnp.where(lane < SPAN, rows[0], jnp.where(lane < 2 * SPAN, rows[1], rows[2])))
        patches = []
        for q in order:
            half, shift = (0, 2 * q) if q < 20 else (1, 2 * q - 40)
            patches.append(packs[half] if shift == 0 else pltpu.roll(packs[half], LANES - shift, 1))
        patches = jnp.concatenate(patches, axis=0).astype(jnp.bfloat16)
        layer = jnp.dot(patches, conv1, preferred_element_type=jnp.float32) + conv1_b_ref[...]
        layer = jnp.maximum(layer, 0.0)
        if tap == 0:
            keep = jnp.concatenate([row + 2 * quarter * position >= 1] * q_first, axis=0)
            layer = jnp.where(keep, layer, 0.0)
        layer = layer.astype(jnp.bfloat16)
        count = quarter * q_second
        windows.append(layer[:count])
        windows.append(layer[quarter * evens : quarter * evens + count])
        windows.append(layer[quarter : quarter + count])
    second = jnp.dot(jnp.concatenate(windows, axis=1), conv2_w_ref[...], preferred_element_type=jnp.float32)
    second = jnp.maximum(second + conv2_b_ref[...], 0.0).astype(jnp.bfloat16)
    flat = jnp.concatenate([second[quarter * r : quarter * (r + 1)] for r in range(q_second)], axis=1)
    features = jnp.dot(flat, proj_w_ref[...], preferred_element_type=jnp.float32) + proj_b_ref[...]
    features = jnp.where(position * frames + 4 * row < valid, features, 0.0)
    out_ref[0] = features.astype(jnp.bfloat16)


def flipped(block, axis, step):
    size = lax.axis_size(axis)
    return lax.ppermute(block, axis, [(i, i ^ step) for i in range(size)])


def summed_over_chips(block, axis):
    size = lax.axis_size(axis)
    if size & (size - 1):
        return lax.psum(block, axis, axis_index_groups=[list(range(c, size, 2)) for c in range(2)])
    step = 2
    while step < size:
        others = [step] if 2 * step >= size else [step, 2 * step, 3 * step]
        block = sum([flipped(block, axis, other) for other in others], block)
        step *= 4
    return block


def paired(block, first):
    size, meets = lax.axis_size("tm"), lax.axis_size("meet")
    pairs = []
    for meet in range(meets):
        at = meet * size
        pairs += [(at + i, at + i + 1) for i in range(first, size - 1, 2)]
        if first and meets % 2:
            pairs.append((at, at + size - 1))
        elif first and meet % 2 == 0:
            pairs += [(at + end, at + size + end) for end in (0, size - 1)]
    return lax.ppermute(block, ("meet", "tm"), pairs + [(j, i) for i, j in pairs])


def per_device(waveform, masks, valid, ref_mic, conv1_w, conv1_b, conv2_w, conv2_b, proj_w, proj_b):
    frames = masks.shape[1]
    channels = conv1_w.shape[1]
    width = proj_w.shape[1]
    vmem = pl.BlockSpec(memory_space=pltpu.VMEM)
    smem = pl.BlockSpec(memory_space=pltpu.SMEM)
    hbm = pl.BlockSpec(memory_space=pltpu.HBM)
    in_hbm = functools.partial(pltpu.with_memory_space_constraint, memory_space=pltpu.HBM)
    params = pltpu.CompilerParams(vmem_limit_bytes=16 * 1024 * 1024)
    rim = jax.ShapeDtypeStruct((MICS, LEAD), waveform.dtype)
    table = dft_table()
    conv2_w = conv2_w.reshape(-1, channels)
    beside, across, framed, levels, table = pl.pallas_call(
        functools.partial(rims_kernel, frames),
        out_shape=(rim, rim, jax.ShapeDtypeStruct((frames * MICS, NFFT), waveform.dtype))
        + tuple(jax.ShapeDtypeStruct(x.shape, x.dtype) for x in (masks, table)),
        in_specs=[hbm] * 3,
        out_specs=(vmem,) * 5,
        scratch_shapes=[pltpu.VMEM(waveform.shape, waveform.dtype), pltpu.SemaphoreType.DMA((3,))],
        compiler_params=params,
        name="rims",
    )(in_hbm(waveform), in_hbm(masks), in_hbm(table))
    got_across = paired(across, 1)
    got_beside = paired(beside, 0)
    stat_block = jax.ShapeDtypeStruct((STATS + MICS, LANES), jnp.float32)
    spec, kept, edge_weight, conv2_w, proj_w = pl.pallas_call(
        functools.partial(stats_kernel, frames),
        out_shape=(
            jax.ShapeDtypeStruct((2 * TILES, frames * MICS, LANES), jnp.float32),
            jax.ShapeDtypeStruct((TILES, STATS, LANES), jnp.float32),
            jax.ShapeDtypeStruct((TILES, 2, MICS, LANES), jnp.float32),
            jax.ShapeDtypeStruct(conv2_w.shape, conv2_w.dtype),
            jax.ShapeDtypeStruct(proj_w.shape, proj_w.dtype),
        ),
        in_specs=[vmem] * 3 + [hbm] * 2 + [smem],
        out_specs=(vmem,) * 5,
        scratch_shapes=[
            pltpu.VMEM((TILES, 2, frames, LANES), jnp.float32),
            pltpu.SemaphoreType.DMA((2,)),
        ],
        compiler_params=params,
        name="stats",
    )(framed, levels, table, in_hbm(conv2_w), in_hbm(proj_w), valid)
    edge_spec, mine, theirs = pl.pallas_call(
        functools.partial(edges_kernel, lax.axis_size("tm")),
        out_shape=(jax.ShapeDtypeStruct((2 * TILES, MICS * MICS, LANES), jnp.float32), stat_block, stat_block),
        in_specs=[vmem] * 7,
        out_specs=(vmem,) * 3,
        scratch_shapes=[pltpu.VMEM((MICS * MICS, NFFT), jnp.float32)],
        compiler_params=params,
        name="edges",
    )(beside, across, got_beside, got_across, table, edge_weight, kept)
    stats = summed_over_chips(mine + flipped(theirs, "tm", 1), "tm")
    beam = jax.ShapeDtypeStruct((2 * MICS, LANES), jnp.float32)
    beam_mine, beam_last = pl.pallas_call(
        solve_kernel,
        out_shape=(beam, beam),
        in_specs=[vmem, smem],
        out_specs=(vmem, vmem),
        compiler_params=params,
        name="solve",
    )(stats, ref_mic)
    beam_theirs = flipped(beam_mine, "tm", 1)
    rows = frames + MICS
    bank = packed_mel_bank()
    mel = pl.pallas_call(
        power_kernel,
        out_shape=jax.ShapeDtypeStruct((rows, 2 * LANES), jnp.float32),
        in_specs=[vmem] * 5,
        out_specs=vmem,
        compiler_params=params,
        name="power",
    )(beam_mine, beam_last, spec, edge_spec, bank)
    return pl.pallas_call(
        functools.partial(stem_kernel, frames),
        out_shape=jax.ShapeDtypeStruct((1, frames // 4, width), jnp.bfloat16),
        in_specs=[vmem] * 4 + [smem] + [vmem] * 7,
        out_specs=vmem,
        scratch_shapes=[pltpu.VMEM((2, rows, LANES), jnp.float32), pltpu.VMEM((LANES, channels), jnp.float32)],
        compiler_params=params,
        name="stem",
    )(
        beam_theirs,
        mel,
        spec,
        edge_spec,
        valid,
        bank,
        conv1_w,
        conv1_b[None],
        conv2_w,
        conv2_b[None],
        proj_w,
        proj_b[None],
    )


def solution(mesh):
    return jax.shard_map(
        per_device,
        mesh=mesh,
        in_specs=(
            P(None, ("meet", "tm")),
            P(None, ("meet", "tm"), None),
            P("meet"),
            P("meet"),
            P(),
            P(),
            P(),
            P(),
            P(),
            P(),
        ),
        out_specs=P(None, ("meet", "tm"), None),
        check_vma=False,
    )
```

```python
import functools
import math

import jax
import jax.numpy as jnp
import numpy as np
from jax import lax
from jax.experimental import pallas as pl
from jax.experimental.pallas import tpu as pltpu
from jax.sharding import PartitionSpec as P

NFFT = 512
HOP = 160
MELS = 80
BINS = NFFT // 2 + 1
LANES = 128
MICS = 8
PAD_BINS = -(-BINS // LANES) * LANES
TILES = PAD_BINS // LANES
HALO = 3
LEAD = 512
TAIL = 384
STATS = 2 * MICS * MICS
SPAN = 42

loading = 0.03
epsilon = 1e-06
sample_rate = 16000.0


def dft_table():
    n = np.arange(NFFT)
    f = np.arange(BINS)
    phase = 2.0 * math.pi * ((n[:, None] * f[None, :]) % NFFT) / NFFT
    window = 0.5 - 0.5 * np.cos(2.0 * math.pi * n / NFFT)
    table = np.zeros((NFFT, 2, PAD_BINS), np.float32)
    table[:, 0, :BINS] = window[:, None] * np.cos(phase)
    table[:, 1, :BINS] = -window[:, None] * np.sin(phase)
    return jnp.asarray(table.reshape(NFFT, 2 * PAD_BINS)).astype(jnp.bfloat16)


def mel_bank():
    mel_top = 2595.0 * math.log10(1.0 + sample_rate / 2.0 / 700.0)
    points = np.arange(MELS + 2) * (mel_top / (MELS + 1))
    edges = 700.0 * (np.power(10.0, points / 2595.0) - 1.0)
    freq = np.arange(BINS) * (sample_rate / 2.0 / (BINS - 1))
    lower, centre, upper = edges[:-2], edges[1:-1], edges[2:]
    rising = (freq[:, None] - lower[None, :]) / (centre - lower)[None, :]
    falling = (upper[None, :] - freq[:, None]) / (upper - centre)[None, :]
    return np.maximum(np.minimum(rising, falling), 0.0).astype(np.float32)


def packed_mel_bank():
    bank = mel_bank()
    packed = np.zeros((PAD_BINS, 2, LANES), np.float32)
    for half in range(2):
        part = bank[:, half * 40 : half * 40 + SPAN]
        for copy in range(3):
            packed[:BINS, half, copy * SPAN : copy * SPAN + part.shape[1]] = part
    return jnp.asarray(packed.reshape(TILES, LANES, 2 * LANES))


def cyclic_pairs(x_re, x_im):
    pairs = [x_re * x_re + x_im * x_im]
    for shift in range(1, MICS // 2 + 1):
        y_re = pltpu.roll(x_re, MICS - shift, 0)
        y_im = pltpu.roll(x_im, MICS - shift, 0)
        pairs.append(x_re * y_re + x_im * y_im)
        pairs.append(x_im * y_re - x_re * y_im)
    return pairs


def add_frame(sums, x_re, x_im, weights):
    pairs = cyclic_pairs(x_re, x_im)
    out = []
    for k in range(2):
        w = jnp.broadcast_to(weights[k], (MICS, LANES))
        out.extend(sums[k * len(pairs) + i] + w * pair for i, pair in enumerate(pairs))
    return tuple(out)


def kept_sums(sums):
    low = lax.broadcasted_iota(jnp.int32, (MICS, LANES), 0) < MICS // 2
    kept = []
    for k in range(2):
        own = sums[9 * k : 9 * k + 9]
        kept.extend(list(own[:7]) + [jnp.where(low, own[7], own[8])])
    return jnp.concatenate(kept, axis=0)


def slot_tiles(position):
    core = position % 2
    return core, 1 - core, TILES - 1


def started(pairs, sem):
    copies = [pltpu.make_async_copy(source, target, sem.at[i]) for i, (source, target) in enumerate(pairs)]
    for copy in copies:
        copy.start()
    return copies


def rims_kernel(frames, wave_hbm, masks_hbm, table_hbm, beside_ref, across_ref, framed_ref, masks_ref, table_ref, wave_ref, sem):
    copies = started(((wave_hbm, wave_ref), (table_hbm, table_ref), (masks_hbm, masks_ref)), sem)
    even = lax.axis_index("tm") % 2 == 0
    copies[0].wait()
    head = wave_ref[:, :LEAD].astype(jnp.float32)
    tail = wave_ref[:, wave_ref.shape[1] - LEAD :].astype(jnp.float32)
    beside_ref[...] = jnp.where(even, tail, head).astype(beside_ref.dtype)
    across_ref[...] = jnp.where(even, head, tail).astype(across_ref.dtype)
    wave = wave_ref[...].astype(jnp.float32)
    width = wave.shape[1]
    rolled = {}

    def frame_of(frame):
        if frame >= frames - HALO:
            return jnp.zeros((MICS, NFFT), jnp.float32)
        base, shift = frame * HOP // LANES * LANES, frame * HOP % LANES
        if shift not in rolled:
            rolled[shift] = wave if shift == 0 else pltpu.roll(wave, width - shift, 1)
        return rolled[shift][:, base : base + NFFT]

    for frame in range(0, frames, 2):
        pair = jnp.concatenate([frame_of(frame), frame_of(frame + 1)], axis=0)
        framed_ref[MICS * frame : MICS * (frame + 2), :] = pair.astype(framed_ref.dtype)
    copies[1].wait()
    copies[2].wait()


def last_bin_sums(frames, spec_ref, weight_ref):
    x_re = x_im = jnp.zeros((MICS, LANES), jnp.float32)
    for frame in range(frames):
        rows = slice(MICS * frame, MICS * (frame + 1))
        part_re, part_im = spec_ref[TILES - 1, rows, :], spec_ref[2 * TILES - 1, rows, :]
        x_re = x_re + (pltpu.roll(part_re, frame, 1) if frame else part_re)
        x_im = x_im + (pltpu.roll(part_im, frame, 1) if frame else part_im)
    frame = lax.broadcasted_iota(jnp.int32, (frames, LANES), 0)
    lane = lax.broadcasted_iota(jnp.int32, (frames, LANES), 1)
    sums = []
    for k in range(2):
        weight = weight_ref[TILES - 1, k][:, :1]
        weight = jnp.sum(jnp.where(frame == lane, weight, 0.0), axis=0, keepdims=True)
        for pair in cyclic_pairs(x_re, x_im):
            total = jnp.sum(pair * weight, axis=1, keepdims=True)
            sums.append(jnp.where(lane[:MICS] == 0, total, 0.0))
    return kept_sums(sums)


def stats_kernel(frames, framed_ref, masks_ref, table_ref, conv2_w_hbm, valid_ref, spec_ref, kept_ref, edge_weight_ref, conv2_w_ref, weight_ref, sem):
    copies = started(((conv2_w_hbm, conv2_w_ref),), sem)
    position = lax.axis_index("tm")
    spec = jnp.dot(framed_ref[...], table_ref[...], preferred_element_type=jnp.float32)
    for tile in range(2 * TILES):
        spec_ref[tile] = spec[:, tile * LANES : (tile + 1) * LANES]

    row = lax.broadcasted_iota(jnp.int32, (frames, 1), 0)
    live = jnp.where(position * frames + row < valid_ref[0], 1.0 / 255.0, 0.0)
    weight_ref[TILES - 1] = jnp.zeros((2, frames, LANES), jnp.float32)
    for k in range(2):
        weight = masks_ref[k].astype(jnp.float32) * live
        for tile in range(TILES):
            kept_lanes = min(LANES, BINS - tile * LANES)
            weight_ref[tile, k, :, :kept_lanes] = weight[:, tile * LANES : tile * LANES + kept_lanes]
    edge_weight_ref[...] = weight_ref[:, :, frames - MICS :, :]

    for slot, tile in enumerate(slot_tiles(position)[:2]):

        def add_frames(group, sums):
            first = pl.multiple_of(group * MICS, MICS)
            weights = [weight_ref[tile, k, pl.ds(first, MICS), :] for k in range(2)]
            for frame in range(MICS):
                rows = pl.ds(pl.multiple_of((first + frame) * MICS, MICS), MICS)
                sums = add_frame(
                    sums, spec_ref[tile, rows, :], spec_ref[TILES + tile, rows, :], [w[frame : frame + 1] for w in weights]
                )
            return sums

        zero = jnp.zeros((MICS, LANES), jnp.float32)
        kept_ref[slot] = kept_sums(lax.fori_loop(0, frames // MICS, add_frames, (zero,) * 18))
    kept_ref[2] = last_bin_sums(frames, spec_ref, weight_ref)
    for copy in copies:
        copy.wait()


def edges_kernel(devices, own0_ref, own1_ref, got0_ref, got1_ref, table_ref, edge_weight_ref, kept_ref, spec_ref, mine_ref, theirs_ref, framed_ref):
    position = lax.axis_index("tm")
    even = position % 2 == 0
    own = [own0_ref[...].astype(jnp.float32), own1_ref[...].astype(jnp.float32)]
    got = [got0_ref[...].astype(jnp.float32), got1_ref[...].astype(jnp.float32)]
    head, tail = jnp.where(even, own[1], own[0]), jnp.where(even, own[0], own[1])
    prev, after = jnp.where(even, got[1], got[0]), jnp.where(even, got[0], got[1])
    prev = jnp.where(position > 0, prev, 0.0)
    after = jnp.where(position < devices - 1, after, 0.0)
    joined = jnp.concatenate(
        [jnp.concatenate([prev, head[:, :TAIL]], axis=1), jnp.concatenate([tail, after[:, :TAIL]], axis=1)], axis=0
    )
    for i in range(HALO):
        start = LEAD - HALO * HOP + i * HOP
        base, shift = start // LANES * LANES, start % LANES
        turned = joined if shift == 0 else pltpu.roll(joined, joined.shape[1] - shift, 1)
        framed_ref[2 * MICS * i : 2 * MICS * (i + 1), :] = turned[:, base : base + NFFT]
    used = 2 * MICS * HALO
    framed_ref[used:, :] = jnp.zeros((framed_ref.shape[0] - used, NFFT), jnp.float32)
    spec = jnp.dot(framed_ref[...].astype(jnp.bfloat16), table_ref[...], preferred_element_type=jnp.float32)
    for tile in range(2 * TILES):
        spec_ref[tile] = spec[:, tile * LANES : (tile + 1) * LANES]
    for slot, tile in enumerate(slot_tiles(position)):
        sums = (jnp.zeros((MICS, LANES), jnp.float32),) * 18
        for i in range(HALO):
            rows = slice((2 * i + 1) * MICS, (2 * i + 2) * MICS)
            at = MICS - HALO + i
            weights = [edge_weight_ref[tile, k, at : at + 1, :] for k in range(2)]
            sums = add_frame(sums, spec_ref[tile, rows, :], spec_ref[TILES + tile, rows, :], weights)
        total = kept_ref[slot] + kept_sums(sums)
        if slot == 0:
            mine_ref[:STATS, :] = total
        elif slot == 1:
            theirs_ref[:STATS, :] = total
        else:
            last_bin = jnp.transpose(total)[:MICS]
            mine_ref[STATS:, :] = last_bin
            theirs_ref[STATS:, :] = last_bin


def columns_of(kept, sub):
    low = sub < MICS // 2
    diag_re = [kept[0], kept[1], kept[3], kept[5]]
    diag_im = [jnp.zeros_like(kept[0]), kept[2], kept[4], kept[6]]
    turned = pltpu.roll(kept[7], MICS // 2, 0)
    diag_re.append(jnp.where(low, kept[7], turned))
    diag_im.append(jnp.where(low, -turned, kept[7]))
    for shift in range(MICS // 2 + 1, MICS):
        diag_re.append(pltpu.roll(diag_re[MICS - shift], MICS - shift, 0))
        diag_im.append(-pltpu.roll(diag_im[MICS - shift], MICS - shift, 0))
    columns = []
    for n in range(MICS):
        re, im = diag_re[n], diag_im[n]
        for m in range(1, MICS):
            re = jnp.where(sub == m, diag_re[(n - m) % MICS], re)
            im = jnp.where(sub == m, diag_im[(n - m) % MICS], im)
        columns.append((re, im))
    return columns


def beams_of(stats, ref_mic):
    sub = lax.broadcasted_iota(jnp.int32, stats[0].shape, 0)
    answer = columns_of(stats[:MICS], sub)
    matrix = columns_of(stats[MICS:], sub)
    spread = jnp.sum(stats[MICS], axis=0, keepdims=True)
    ridge = loading * spread / MICS + epsilon
    matrix = [(jnp.where(sub == n, re + ridge, re), im) for n, (re, im) in enumerate(matrix)]
    for pivot in range(MICS):
        col_re, col_im = matrix[pivot]
        pivot_re = col_re[pivot : pivot + 1]
        pivot_im = col_im[pivot : pivot + 1]
        modulus = pivot_re * pivot_re + pivot_im * pivot_im
        inverse_re = pivot_re / modulus
        inverse_im = -pivot_im / modulus

        def eliminated(column):
            re, im = column
            row_re, row_im = re[pivot : pivot + 1], im[pivot : pivot + 1]
            lead_re = row_re * inverse_re - row_im * inverse_im
            lead_im = row_re * inverse_im + row_im * inverse_re
            return (
                jnp.where(sub == pivot, lead_re, re - (col_re * lead_re - col_im * lead_im)),
                jnp.where(sub == pivot, lead_im, im - (col_re * lead_im + col_im * lead_re)),
            )

        matrix = [eliminated(c) if n > pivot else c for n, c in enumerate(matrix)]
        answer = [eliminated(c) for c in answer]
    trace = answer[0][0][0:1]
    beam_re, beam_im = answer[0]
    for n in range(1, MICS):
        trace = trace + answer[n][0][n : n + 1]
        beam_re = jnp.where(ref_mic == n, answer[n][0], beam_re)
        beam_im = jnp.where(ref_mic == n, answer[n][1], beam_im)
    scale = 1.0 / (trace + epsilon)
    return beam_re * scale, beam_im * scale


def solve_kernel(stats_ref, ref_mic_ref, beam_ref, last_ref):
    blank = jnp.zeros((LANES - MICS, LANES), jnp.float32)
    last_bin = jnp.transpose(jnp.concatenate([stats_ref[STATS:, :], blank], axis=0))
    for out_ref, stats in ((beam_ref, stats_ref[:STATS, :]), (last_ref, last_bin)):
        kept = [stats[i * MICS : (i + 1) * MICS] for i in range(2 * MICS)]
        beam_re, beam_im = beams_of(kept, ref_mic_ref[0])
        out_ref[:MICS, :] = beam_re
        out_ref[MICS:, :] = beam_im


def power_of(beam_ref, tile, spec_ref, edge_spec_ref):
    beam_re, beam_im = beam_ref[:MICS, :], beam_ref[MICS:, :]
    groups = spec_ref.shape[1] // (MICS * MICS)
    power = []
    for group in range(groups + 1):
        from_ref, first = (spec_ref, group * MICS * MICS) if group < groups else (edge_spec_ref, 0)
        sum_re = sum_im = None
        for m in range(MICS):
            rows = pl.ds(first + m, MICS, stride=MICS)
            x_re, x_im = from_ref[tile, rows, :], from_ref[TILES + tile, rows, :]
            b_re, b_im = beam_re[m : m + 1], beam_im[m : m + 1]
            part_re = b_re * x_re + b_im * x_im
            part_im = b_re * x_im - b_im * x_re
            sum_re = part_re if sum_re is None else sum_re + part_re
            sum_im = part_im if sum_im is None else sum_im + part_im
        power.append(sum_re * sum_re + sum_im * sum_im)
    return jnp.concatenate(power, axis=0)


def mel_of(power, bank):
    return jnp.dot(power, bank, precision=lax.Precision.HIGHEST, preferred_element_type=jnp.float32)


def power_kernel(mine_ref, last_ref, spec_ref, edge_spec_ref, bank_ref, mel_ref):
    mine, _, last = slot_tiles(lax.axis_index("tm"))
    power = [power_of(beam_ref, tile, spec_ref, edge_spec_ref) for beam_ref, tile in ((mine_ref, mine), (last_ref, last))]
    bank = jnp.concatenate([bank_ref[mine], bank_ref[last]], axis=0)
    mel_ref[...] = mel_of(jnp.concatenate(power, axis=1), bank)


def stem_kernel(frames, theirs_ref, mel_ref, spec_ref, edge_spec_ref, valid_ref, bank_ref, conv1_w_ref, conv1_b_ref, conv2_w_ref, conv2_b_ref, proj_w_ref, proj_b_ref, out_ref, logmel_ref, conv1_ref):
    position = lax.axis_index("tm")
    valid = valid_ref[0]
    quarter = frames // 4
    channels = conv1_w_ref.shape[1]
    conv1_ref[...] = jnp.zeros((LANES, channels), jnp.float32)
    for shift_t in range(3):
        conv1_ref[SPAN * shift_t : SPAN * shift_t + 3, :] = conv1_w_ref[3 * shift_t : 3 * shift_t + 3, :].astype(jnp.float32)
    conv1 = conv1_ref[...].astype(jnp.bfloat16)

    theirs = slot_tiles(position)[1]
    mel = mel_ref[...] + mel_of(power_of(theirs_ref, theirs, spec_ref, edge_spec_ref), bank_ref[theirs])
    row = lax.broadcasted_iota(jnp.int32, (frames + MICS, 1), 0)
    edge = (row - frames) // 2 + jnp.where((row - frames) % 2 == 0, -HALO, frames - HALO)
    time = position * frames + jnp.where(row < frames, row, edge)
    live = (time >= 0) & (time < valid)
    logmel = jnp.where(live, jnp.log(mel + epsilon), 0.0)
    logmel = logmel.astype(jnp.bfloat16).astype(jnp.float32)
    for half in range(2):
        part = logmel[:, half * LANES : (half + 1) * LANES]
        logmel_ref[half, HALO : HALO + frames, :] = part[:frames]
        for i in range(HALO):
            logmel_ref[half, i : i + 1, :] = part[frames + 2 * i : frames + 2 * i + 1]
            logmel_ref[half, frames + i : frames + i + 1, :] = part[frames + 2 * i + 1 : frames + 2 * i + 2]

    q_first = (MELS - 3) // 2 + 1
    q_second = (q_first - 3) // 2 + 1
    order = list(range(0, q_first, 2)) + list(range(1, q_first, 2))
    evens = (q_first + 1) // 2
    lane = lax.broadcasted_iota(jnp.int32, (quarter, LANES), 1)
    row = lax.broadcasted_iota(jnp.int32, (quarter, 1), 0)
    windows = []
    for tap in range(3):
        packs = []
        for half in range(2):
            rows = [logmel_ref[half, pl.ds(2 * tap + a, quarter, stride=4), :] for a in range(3)]
            packs.append(jnp.where(lane < SPAN, rows[0], jnp.where(lane < 2 * SPAN, rows[1], rows[2])))
        patches = []
        for q in order:
            half, shift = (0, 2 * q) if q < 20 else (1, 2 * q - 40)
            patches.append(packs[half] if shift == 0 else pltpu.roll(packs[half], LANES - shift, 1))
        patches = jnp.concatenate(patches, axis=0).astype(jnp.bfloat16)
        layer = jnp.dot(patches, conv1, preferred_element_type=jnp.float32) + conv1_b_ref[...]
        layer = jnp.maximum(layer, 0.0)
        if tap == 0:
            keep = jnp.concatenate([row + 2 * quarter * position >= 1] * q_first, axis=0)
            layer = jnp.where(keep, layer, 0.0)
        layer = layer.astype(jnp.bfloat16)
        count = quarter * q_second
        windows.append(layer[:count])
        windows.append(layer[quarter * evens : quarter * evens + count])
        windows.append(layer[quarter : quarter + count])
    second = jnp.dot(jnp.concatenate(windows, axis=1), conv2_w_ref[...], preferred_element_type=jnp.float32)
    second = jnp.maximum(second + conv2_b_ref[...], 0.0).astype(jnp.bfloat16)
    flat = jnp.concatenate([second[quarter * r : quarter * (r + 1)] for r in range(q_second)], axis=1)
    features = jnp.dot(flat, proj_w_ref[...], preferred_element_type=jnp.float32) + proj_b_ref[...]
    features = jnp.where(position * frames + 4 * row < valid, features, 0.0)
    out_ref[0] = features.astype(jnp.bfloat16)


def flipped(block, axis, step):
    size = lax.axis_size(axis)
    return lax.ppermute(block, axis, [(i, i ^ step) for i in range(size)])


def summed_over_chips(block, axis):
    size = lax.axis_size(axis)
    if size & (size - 1):
        return lax.psum(block, axis, axis_index_groups=[list(range(c, size, 2)) for c in range(2)])
    step = 2
    while step < size:
        others = [step] if 2 * step >= size else [step, 2 * step, 3 * step]
        block = sum([flipped(block, axis, other) for other in others], block)
        step *= 4
    return block


def paired(block, first):
    size, meets = lax.axis_size("tm"), lax.axis_size("meet")
    pairs = []
    for meet in range(meets):
        at = meet * size
        pairs += [(at + i, at + i + 1) for i in range(first, size - 1, 2)]
        if first and meets % 2:
            pairs.append((at, at + size - 1))
        elif first and meet % 2 == 0:
            pairs += [(at + end, at + size + end) for end in (0, size - 1)]
    return lax.ppermute(block, ("meet", "tm"), pairs + [(j, i) for i, j in pairs])


def per_device(waveform, masks, valid, ref_mic, conv1_w, conv1_b, conv2_w, conv2_b, proj_w, proj_b):
    frames = masks.shape[1]
    channels = conv1_w.shape[1]
    width = proj_w.shape[1]
    vmem = pl.BlockSpec(memory_space=pltpu.VMEM)
    smem = pl.BlockSpec(memory_space=pltpu.SMEM)
    hbm = pl.BlockSpec(memory_space=pltpu.HBM)
    in_hbm = functools.partial(pltpu.with_memory_space_constraint, memory_space=pltpu.HBM)
    params = pltpu.CompilerParams(vmem_limit_bytes=16 * 1024 * 1024)
    rim = jax.ShapeDtypeStruct((MICS, LEAD), waveform.dtype)
    table = dft_table()
    conv2_w = conv2_w.reshape(-1, channels)
    beside, across, framed, levels, table = pl.pallas_call(
        functools.partial(rims_kernel, frames),
        out_shape=(rim, rim, jax.ShapeDtypeStruct((frames * MICS, NFFT), waveform.dtype))
        + tuple(jax.ShapeDtypeStruct(x.shape, x.dtype) for x in (masks, table)),
        in_specs=[hbm] * 3,
        out_specs=(vmem,) * 5,
        scratch_shapes=[pltpu.VMEM(waveform.shape, waveform.dtype), pltpu.SemaphoreType.DMA((3,))],
        compiler_params=params,
        name="rims",
    )(in_hbm(waveform), in_hbm(masks), in_hbm(table))
    got_across = paired(across, 1)
    got_beside = paired(beside, 0)
    stat_block = jax.ShapeDtypeStruct((STATS + MICS, LANES), jnp.float32)
    spec, kept, edge_weight, conv2_w = pl.pallas_call(
        functools.partial(stats_kernel, frames),
        out_shape=(
            jax.ShapeDtypeStruct((2 * TILES, frames * MICS, LANES), jnp.float32),
            jax.ShapeDtypeStruct((TILES, STATS, LANES), jnp.float32),
            jax.ShapeDtypeStruct((TILES, 2, MICS, LANES), jnp.float32),
            jax.ShapeDtypeStruct(conv2_w.shape, conv2_w.dtype),
        ),
        in_specs=[vmem] * 3 + [hbm, smem],
        out_specs=(vmem,) * 4,
        scratch_shapes=[
            pltpu.VMEM((TILES, 2, frames, LANES), jnp.float32),
            pltpu.SemaphoreType.DMA((1,)),
        ],
        compiler_params=params,
        name="stats",
    )(framed, levels, table, in_hbm(conv2_w), valid)
    edge_spec, mine, theirs = pl.pallas_call(
        functools.partial(edges_kernel, lax.axis_size("tm")),
        out_shape=(jax.ShapeDtypeStruct((2 * TILES, MICS * MICS, LANES), jnp.float32), stat_block, stat_block),
        in_specs=[vmem] * 7,
        out_specs=(vmem,) * 3,
        scratch_shapes=[pltpu.VMEM((MICS * MICS, NFFT), jnp.float32)],
        compiler_params=params,
        name="edges",
    )(beside, across, got_beside, got_across, table, edge_weight, kept)
    stats = summed_over_chips(mine + flipped(theirs, "tm", 1), "tm")
    beam = jax.ShapeDtypeStruct((2 * MICS, LANES), jnp.float32)
    beam_mine, beam_last = pl.pallas_call(
        solve_kernel,
        out_shape=(beam, beam),
        in_specs=[vmem, smem],
        out_specs=(vmem, vmem),
        compiler_params=params,
        name="solve",
    )(stats, ref_mic)
    beam_theirs = flipped(beam_mine, "tm", 1)
    rows = frames + MICS
    bank = packed_mel_bank()
    mel = pl.pallas_call(
        power_kernel,
        out_shape=jax.ShapeDtypeStruct((rows, 2 * LANES), jnp.float32),
        in_specs=[vmem] * 5,
        out_specs=vmem,
        compiler_params=params,
        name="power",
    )(beam_mine, beam_last, spec, edge_spec, bank)
    return pl.pallas_call(
        functools.partial(stem_kernel, frames),
        out_shape=jax.ShapeDtypeStruct((1, frames // 4, width), jnp.bfloat16),
        in_specs=[vmem] * 4 + [smem] + [vmem] * 7,
        out_specs=vmem,
        scratch_shapes=[pltpu.VMEM((2, rows, LANES), jnp.float32), pltpu.VMEM((LANES, channels), jnp.float32)],
        compiler_params=params,
        name="stem",
    )(
        beam_theirs,
        mel,
        spec,
        edge_spec,
        valid,
        bank,
        conv1_w,
        conv1_b[None],
        conv2_w,
        conv2_b[None],
        proj_w,
        proj_b[None],
    )


def solution(mesh):
    return jax.shard_map(
        per_device,
        mesh=mesh,
        in_specs=(
            P(None, ("meet", "tm")),
            P(None, ("meet", "tm"), None),
            P("meet"),
            P("meet"),
            P(),
            P(),
            P(),
            P(),
            P(),
            P(),
        ),
        out_specs=P(None, ("meet", "tm"), None),
        check_vma=False,
    )
```

```python
import functools
import math

import jax
import jax.numpy as jnp
import numpy as np
from jax import lax
from jax.experimental import pallas as pl
from jax.experimental.pallas import tpu as pltpu
from jax.sharding import PartitionSpec as P

NFFT = 512
HOP = 160
MELS = 80
BINS = NFFT // 2 + 1
LANES = 128
MICS = 8
PAD_BINS = -(-BINS // LANES) * LANES
TILES = PAD_BINS // LANES
HALO = 3
LEAD = 512
TAIL = 384
STATS = 2 * MICS * MICS
SPAN = 42

loading = 0.03
epsilon = 1e-06
sample_rate = 16000.0


def dft_table():
    n = np.arange(NFFT)
    f = np.arange(BINS)
    phase = 2.0 * math.pi * ((n[:, None] * f[None, :]) % NFFT) / NFFT
    window = 0.5 - 0.5 * np.cos(2.0 * math.pi * n / NFFT)
    table = np.zeros((NFFT, 2, PAD_BINS), np.float32)
    table[:, 0, :BINS] = window[:, None] * np.cos(phase)
    table[:, 1, :BINS] = -window[:, None] * np.sin(phase)
    return jnp.asarray(table.reshape(NFFT, 2 * PAD_BINS)).astype(jnp.bfloat16)


def mel_bank():
    mel_top = 2595.0 * math.log10(1.0 + sample_rate / 2.0 / 700.0)
    points = np.arange(MELS + 2) * (mel_top / (MELS + 1))
    edges = 700.0 * (np.power(10.0, points / 2595.0) - 1.0)
    freq = np.arange(BINS) * (sample_rate / 2.0 / (BINS - 1))
    lower, centre, upper = edges[:-2], edges[1:-1], edges[2:]
    rising = (freq[:, None] - lower[None, :]) / (centre - lower)[None, :]
    falling = (upper[None, :] - freq[:, None]) / (upper - centre)[None, :]
    return np.maximum(np.minimum(rising, falling), 0.0).astype(np.float32)


def packed_mel_bank():
    bank = mel_bank()
    packed = np.zeros((PAD_BINS, 2, LANES), np.float32)
    for half in range(2):
        part = bank[:, half * 40 : half * 40 + SPAN]
        for copy in range(3):
            packed[:BINS, half, copy * SPAN : copy * SPAN + part.shape[1]] = part
    return jnp.asarray(packed.reshape(TILES, LANES, 2 * LANES))


def cyclic_pairs(x_re, x_im):
    pairs = [x_re * x_re + x_im * x_im]
    for shift in range(1, MICS // 2 + 1):
        y_re = pltpu.roll(x_re, MICS - shift, 0)
        y_im = pltpu.roll(x_im, MICS - shift, 0)
        pairs.append(x_re * y_re + x_im * y_im)
        pairs.append(x_im * y_re - x_re * y_im)
    return pairs


def add_frame(sums, x_re, x_im, weights):
    pairs = cyclic_pairs(x_re, x_im)
    out = []
    for k in range(2):
        w = jnp.broadcast_to(weights[k], (MICS, LANES))
        out.extend(sums[k * len(pairs) + i] + w * pair for i, pair in enumerate(pairs))
    return tuple(out)


def kept_sums(sums):
    low = lax.broadcasted_iota(jnp.int32, (MICS, LANES), 0) < MICS // 2
    kept = []
    for k in range(2):
        own = sums[9 * k : 9 * k + 9]
        kept.extend(list(own[:7]) + [jnp.where(low, own[7], own[8])])
    return jnp.concatenate(kept, axis=0)


def slot_tiles(position):
    core = position % 2
    return core, 1 - core, TILES - 1


def started(pairs, sem):
    copies = [pltpu.make_async_copy(source, target, sem.at[i]) for i, (source, target) in enumerate(pairs)]
    for copy in copies:
        copy.start()
    return copies


def rims_kernel(frames, wave_hbm, masks_hbm, table_hbm, beside_ref, across_ref, framed_ref, masks_ref, table_ref, wave_ref, sem):
    copies = started(((wave_hbm, wave_ref), (table_hbm, table_ref), (masks_hbm, masks_ref)), sem)
    even = lax.axis_index("tm") % 2 == 0
    copies[0].wait()
    head = wave_ref[:, :LEAD].astype(jnp.float32)
    tail = wave_ref[:, wave_ref.shape[1] - LEAD :].astype(jnp.float32)
    beside_ref[...] = jnp.where(even, tail, head).astype(beside_ref.dtype)
    across_ref[...] = jnp.where(even, head, tail).astype(across_ref.dtype)
    wave = wave_ref[...].astype(jnp.float32)
    width = wave.shape[1]
    rolled = {}

    def frame_of(frame):
        if frame >= frames - HALO:
            return jnp.zeros((MICS, NFFT), jnp.float32)
        base, shift = frame * HOP // LANES * LANES, frame * HOP % LANES
        if shift not in rolled:
            rolled[shift] = wave if shift == 0 else pltpu.roll(wave, width - shift, 1)
        return rolled[shift][:, base : base + NFFT]

    for frame in range(0, frames, 2):
        pair = jnp.concatenate([frame_of(frame), frame_of(frame + 1)], axis=0)
        framed_ref[MICS * frame : MICS * (frame + 2), :] = pair.astype(framed_ref.dtype)
    copies[1].wait()
    copies[2].wait()


def last_bin_sums(frames, spec_ref, weight_ref):
    x_re = x_im = jnp.zeros((MICS, LANES), jnp.float32)
    for frame in range(frames):
        rows = slice(MICS * frame, MICS * (frame + 1))
        part_re, part_im = spec_ref[TILES - 1, rows, :], spec_ref[2 * TILES - 1, rows, :]
        x_re = x_re + (pltpu.roll(part_re, frame, 1) if frame else part_re)
        x_im = x_im + (pltpu.roll(part_im, frame, 1) if frame else part_im)
    frame = lax.broadcasted_iota(jnp.int32, (frames, LANES), 0)
    lane = lax.broadcasted_iota(jnp.int32, (frames, LANES), 1)
    sums = []
    for k in range(2):
        weight = weight_ref[TILES - 1, k][:, :1]
        weight = jnp.sum(jnp.where(frame == lane, weight, 0.0), axis=0, keepdims=True)
        for pair in cyclic_pairs(x_re, x_im):
            total = jnp.sum(pair * weight, axis=1, keepdims=True)
            sums.append(jnp.where(lane[:MICS] == 0, total, 0.0))
    return kept_sums(sums)


def stats_kernel(frames, framed_ref, masks_ref, table_ref, conv2_w_hbm, valid_ref, spec_ref, kept_ref, edge_weight_ref, conv2_w_ref, weight_ref, sem):
    copies = started(((conv2_w_hbm, conv2_w_ref),), sem)
    position = lax.axis_index("tm")
    spec = jnp.dot(framed_ref[...], table_ref[...], preferred_element_type=jnp.float32)
    for tile in range(2 * TILES):
        spec_ref[tile] = spec[:, tile * LANES : (tile + 1) * LANES]

    row = lax.broadcasted_iota(jnp.int32, (frames, 1), 0)
    live = jnp.where(position * frames + row < valid_ref[0], 1.0 / 255.0, 0.0)
    weight_ref[TILES - 1] = jnp.zeros((2, frames, LANES), jnp.float32)
    for k in range(2):
        weight = masks_ref[k].astype(jnp.float32) * live
        for tile in range(TILES):
            kept_lanes = min(LANES, BINS - tile * LANES)
            weight_ref[tile, k, :, :kept_lanes] = weight[:, tile * LANES : tile * LANES + kept_lanes]
    edge_weight_ref[...] = weight_ref[:, :, frames - MICS :, :]

    for slot, tile in enumerate(slot_tiles(position)[:2]):

        def add_frames(group, sums):
            first = pl.multiple_of(group * MICS, MICS)
            weights = [weight_ref[tile, k, pl.ds(first, MICS), :] for k in range(2)]
            for frame in range(MICS):
                rows = pl.ds(pl.multiple_of((first + frame) * MICS, MICS), MICS)
                sums = add_frame(
                    sums, spec_ref[tile, rows, :], spec_ref[TILES + tile, rows, :], [w[frame : frame + 1] for w in weights]
                )
            return sums

        zero = jnp.zeros((MICS, LANES), jnp.float32)
        kept_ref[slot] = kept_sums(lax.fori_loop(0, frames // MICS, add_frames, (zero,) * 18))
    kept_ref[2] = last_bin_sums(frames, spec_ref, weight_ref)
    for copy in copies:
        copy.wait()


def edge_frames(tail, head, table, framed_ref):
    joined = jnp.concatenate([tail, head[:, :TAIL]], axis=1)
    for i in range(HALO):
        start = LEAD - HALO * HOP + i * HOP
        base, shift = start // LANES * LANES, start % LANES
        turned = joined if shift == 0 else pltpu.roll(joined, joined.shape[1] - shift, 1)
        framed_ref[MICS * i : MICS * (i + 1), :] = turned[:, base : base + NFFT]
    used = MICS * HALO
    framed_ref[used:, :] = jnp.zeros((framed_ref.shape[0] - used, NFFT), jnp.float32)
    return jnp.dot(framed_ref[...].astype(jnp.bfloat16), table, preferred_element_type=jnp.float32)


def edge_sums(spec_ref, first, tile, weights):
    sums = (jnp.zeros((MICS, LANES), jnp.float32),) * 18
    for i in range(HALO):
        rows = slice(first + MICS * i, first + MICS * (i + 1))
        at = MICS - HALO + i
        sums = add_frame(sums, spec_ref[tile, rows, :], spec_ref[TILES + tile, rows, :], [w[at : at + 1] for w in weights])
    return kept_sums(sums)


def edges_kernel(devices, own_ref, got_ref, beside_ref, table_ref, edge_weight_ref, kept_ref, spec_ref, mine_ref, theirs_ref, framed_ref):
    position = lax.axis_index("tm")
    even = position % 2 == 0
    own = own_ref[...].astype(jnp.float32)
    got = jnp.where((position > 0) & (position < devices - 1), got_ref[...].astype(jnp.float32), 0.0)
    spec = edge_frames(jnp.where(even, got, own), jnp.where(even, own, got), table_ref[...], framed_ref)
    for tile in range(2 * TILES):
        spec_ref[tile] = spec[:, tile * LANES : (tile + 1) * LANES]
    for slot, tile in enumerate(slot_tiles(position)):
        weights = [jnp.where(even, 0.0, edge_weight_ref[tile, k]) for k in range(2)]
        total = kept_ref[slot] + edge_sums(spec_ref, 0, tile, weights)
        if slot == 0:
            mine_ref[:STATS, :] = total
        elif slot == 1:
            theirs_ref[:STATS, :] = total
        else:
            last_bin = jnp.transpose(total)[:MICS]
            mine_ref[STATS:, :] = last_bin
            theirs_ref[STATS : STATS + MICS, :] = last_bin
    first = STATS + MICS
    beside = beside_ref[...].astype(jnp.float32)
    sent = [beside[:, at : at + LANES] for at in range(0, LEAD, LANES)]
    sent += [edge_weight_ref[tile, k] for tile in slot_tiles(position)[1:] for k in range(2)]
    for i, rows in enumerate(sent):
        theirs_ref[first + MICS * i : first + MICS * (i + 1), :] = rows


def chip_kernel(mine_ref, got_ref, beside_ref, table_ref, edge_weight_ref, across_spec_ref, stats_ref, spec_ref, framed_ref):
    position = lax.axis_index("tm")
    even = position % 2 == 0
    first = STATS + MICS
    got = jnp.concatenate([got_ref[first + MICS * i : first + MICS * (i + 1), :] for i in range(LEAD // LANES)], axis=1)
    own = beside_ref[...].astype(jnp.float32)
    spec = edge_frames(jnp.where(even, own, got), jnp.where(even, got, own), table_ref[...], framed_ref)
    used = MICS * HALO
    for tile in range(2 * TILES):
        spec_ref[tile, :used, :] = across_spec_ref[tile, :used, :]
        spec_ref[tile, used : used + framed_ref.shape[0], :] = spec[:, tile * LANES : (tile + 1) * LANES]
        spec_ref[tile, used + framed_ref.shape[0] :, :] = jnp.zeros((MICS, LANES), jnp.float32)
    first += LEAD // LANES * MICS
    for part, tile in enumerate((slot_tiles(position)[0], TILES - 1)):
        weights = []
        for k in range(2):
            at = first + (2 * part + k) * MICS
            weights.append(jnp.where(even, edge_weight_ref[tile, k], got_ref[at : at + MICS, :]))
        total = edge_sums(spec_ref, used, tile, weights)
        if part == 0:
            stats_ref[:STATS, :] = mine_ref[:STATS, :] + got_ref[:STATS, :] + total
        else:
            last_bin = mine_ref[STATS:, :] + got_ref[STATS : STATS + MICS, :]
            stats_ref[STATS:, :] = last_bin + jnp.transpose(total)[:MICS]


def columns_of(kept, sub):
    low = sub < MICS // 2
    diag_re = [kept[0], kept[1], kept[3], kept[5]]
    diag_im = [jnp.zeros_like(kept[0]), kept[2], kept[4], kept[6]]
    turned = pltpu.roll(kept[7], MICS // 2, 0)
    diag_re.append(jnp.where(low, kept[7], turned))
    diag_im.append(jnp.where(low, -turned, kept[7]))
    for shift in range(MICS // 2 + 1, MICS):
        diag_re.append(pltpu.roll(diag_re[MICS - shift], MICS - shift, 0))
        diag_im.append(-pltpu.roll(diag_im[MICS - shift], MICS - shift, 0))
    columns = []
    for n in range(MICS):
        re, im = diag_re[n], diag_im[n]
        for m in range(1, MICS):
            re = jnp.where(sub == m, diag_re[(n - m) % MICS], re)
            im = jnp.where(sub == m, diag_im[(n - m) % MICS], im)
        columns.append((re, im))
    return columns


def beams_of(stats, ref_mic):
    sub = lax.broadcasted_iota(jnp.int32, stats[0].shape, 0)
    answer = columns_of(stats[:MICS], sub)
    matrix = columns_of(stats[MICS:], sub)
    spread = jnp.sum(stats[MICS], axis=0, keepdims=True)
    ridge = loading * spread / MICS + epsilon
    matrix = [(jnp.where(sub == n, re + ridge, re), im) for n, (re, im) in enumerate(matrix)]
    for pivot in range(MICS):
        col_re, col_im = matrix[pivot]
        pivot_re = col_re[pivot : pivot + 1]
        pivot_im = col_im[pivot : pivot + 1]
        modulus = pivot_re * pivot_re + pivot_im * pivot_im
        inverse_re = pivot_re / modulus
        inverse_im = -pivot_im / modulus

        def eliminated(column):
            re, im = column
            row_re, row_im = re[pivot : pivot + 1], im[pivot : pivot + 1]
            lead_re = row_re * inverse_re - row_im * inverse_im
            lead_im = row_re * inverse_im + row_im * inverse_re
            return (
                jnp.where(sub == pivot, lead_re, re - (col_re * lead_re - col_im * lead_im)),
                jnp.where(sub == pivot, lead_im, im - (col_re * lead_im + col_im * lead_re)),
            )

        matrix = [eliminated(c) if n > pivot else c for n, c in enumerate(matrix)]
        answer = [eliminated(c) for c in answer]
    trace = answer[0][0][0:1]
    beam_re, beam_im = answer[0]
    for n in range(1, MICS):
        trace = trace + answer[n][0][n : n + 1]
        beam_re = jnp.where(ref_mic == n, answer[n][0], beam_re)
        beam_im = jnp.where(ref_mic == n, answer[n][1], beam_im)
    scale = 1.0 / (trace + epsilon)
    return beam_re * scale, beam_im * scale


def solve_kernel(stats_ref, ref_mic_ref, beam_ref, last_ref):
    blank = jnp.zeros((LANES - MICS, LANES), jnp.float32)
    last_bin = jnp.transpose(jnp.concatenate([stats_ref[STATS:, :], blank], axis=0))
    for out_ref, stats in ((beam_ref, stats_ref[:STATS, :]), (last_ref, last_bin)):
        kept = [stats[i * MICS : (i + 1) * MICS] for i in range(2 * MICS)]
        beam_re, beam_im = beams_of(kept, ref_mic_ref[0])
        out_ref[:MICS, :] = beam_re
        out_ref[MICS:, :] = beam_im


def power_of(beam_ref, tile, spec_ref, edge_spec_ref):
    beam_re, beam_im = beam_ref[:MICS, :], beam_ref[MICS:, :]
    groups = spec_ref.shape[1] // (MICS * MICS)
    power = []
    for group in range(groups + 1):
        from_ref, first = (spec_ref, group * MICS * MICS) if group < groups else (edge_spec_ref, 0)
        sum_re = sum_im = None
        for m in range(MICS):
            rows = pl.ds(first + m, MICS, stride=MICS)
            x_re, x_im = from_ref[tile, rows, :], from_ref[TILES + tile, rows, :]
            b_re, b_im = beam_re[m : m + 1], beam_im[m : m + 1]
            part_re = b_re * x_re + b_im * x_im
            part_im = b_re * x_im - b_im * x_re
            sum_re = part_re if sum_re is None else sum_re + part_re
            sum_im = part_im if sum_im is None else sum_im + part_im
        power.append(sum_re * sum_re + sum_im * sum_im)
    return jnp.concatenate(power, axis=0)


def mel_of(power, bank):
    return jnp.dot(power, bank, precision=lax.Precision.HIGHEST, preferred_element_type=jnp.float32)


def power_kernel(mine_ref, last_ref, spec_ref, edge_spec_ref, bank_ref, mel_ref):
    mine, _, last = slot_tiles(lax.axis_index("tm"))
    power = [power_of(beam_ref, tile, spec_ref, edge_spec_ref) for beam_ref, tile in ((mine_ref, mine), (last_ref, last))]
    bank = jnp.concatenate([bank_ref[mine], bank_ref[last]], axis=0)
    mel_ref[...] = mel_of(jnp.concatenate(power, axis=1), bank)


def stem_kernel(frames, theirs_ref, mel_ref, spec_ref, edge_spec_ref, valid_ref, bank_ref, conv1_w_ref, conv1_b_ref, conv2_w_ref, conv2_b_ref, proj_w_ref, proj_b_ref, out_ref, logmel_ref, conv1_ref):
    position = lax.axis_index("tm")
    valid = valid_ref[0]
    quarter = frames // 4
    channels = conv1_w_ref.shape[1]
    conv1_ref[...] = jnp.zeros((LANES, channels), jnp.float32)
    for shift_t in range(3):
        conv1_ref[SPAN * shift_t : SPAN * shift_t + 3, :] = conv1_w_ref[3 * shift_t : 3 * shift_t + 3, :].astype(jnp.float32)
    conv1 = conv1_ref[...].astype(jnp.bfloat16)

    theirs = slot_tiles(position)[1]
    mel = mel_ref[...] + mel_of(power_of(theirs_ref, theirs, spec_ref, edge_spec_ref), bank_ref[theirs])
    row = lax.broadcasted_iota(jnp.int32, (frames + MICS, 1), 0)
    even = position % 2 == 0
    slot = row - frames
    before = (slot < HALO) == even
    edge = slot - jnp.where(slot < HALO, 0, HALO) + jnp.where(before, -HALO, frames - HALO)
    time = position * frames + jnp.where(row < frames, row, edge)
    live = (time >= 0) & (time < valid)
    logmel = jnp.where(live, jnp.log(mel + epsilon), 0.0)
    logmel = logmel.astype(jnp.bfloat16).astype(jnp.float32)
    for half in range(2):
        part = logmel[:, half * LANES : (half + 1) * LANES]
        logmel_ref[half, HALO : HALO + frames, :] = part[:frames]
        across, within = part[frames : frames + HALO], part[frames + HALO : frames + 2 * HALO]
        logmel_ref[half, :HALO, :] = jnp.where(even, across, within)
        logmel_ref[half, HALO + frames - HALO : frames + HALO, :] = jnp.where(even, within, across)

    q_first = (MELS - 3) // 2 + 1
    q_second = (q_first - 3) // 2 + 1
    order = list(range(0, q_first, 2)) + list(range(1, q_first, 2))
    evens = (q_first + 1) // 2
    lane = lax.broadcasted_iota(jnp.int32, (quarter, LANES), 1)
    row = lax.broadcasted_iota(jnp.int32, (quarter, 1), 0)
    windows = []
    for tap in range(3):
        packs = []
        for half in range(2):
            rows = [logmel_ref[half, pl.ds(2 * tap + a, quarter, stride=4), :] for a in range(3)]
            packs.append(jnp.where(lane < SPAN, rows[0], jnp.where(lane < 2 * SPAN, rows[1], rows[2])))
        patches = []
        for q in order:
            half, shift = (0, 2 * q) if q < 20 else (1, 2 * q - 40)
            patches.append(packs[half] if shift == 0 else pltpu.roll(packs[half], LANES - shift, 1))
        patches = jnp.concatenate(patches, axis=0).astype(jnp.bfloat16)
        layer = jnp.dot(patches, conv1, preferred_element_type=jnp.float32) + conv1_b_ref[...]
        layer = jnp.maximum(layer, 0.0)
        if tap == 0:
            keep = jnp.concatenate([row + 2 * quarter * position >= 1] * q_first, axis=0)
            layer = jnp.where(keep, layer, 0.0)
        layer = layer.astype(jnp.bfloat16)
        count = quarter * q_second
        windows.append(layer[:count])
        windows.append(layer[quarter * evens : quarter * evens + count])
        windows.append(layer[quarter : quarter + count])
    second = jnp.dot(jnp.concatenate(windows, axis=1), conv2_w_ref[...], preferred_element_type=jnp.float32)
    second = jnp.maximum(second + conv2_b_ref[...], 0.0).astype(jnp.bfloat16)
    flat = jnp.concatenate([second[quarter * r : quarter * (r + 1)] for r in range(q_second)], axis=1)
    features = jnp.dot(flat, proj_w_ref[...], preferred_element_type=jnp.float32) + proj_b_ref[...]
    features = jnp.where(position * frames + 4 * row < valid, features, 0.0)
    out_ref[0] = features.astype(jnp.bfloat16)


def flipped(block, axis, step):
    size = lax.axis_size(axis)
    return lax.ppermute(block, axis, [(i, i ^ step) for i in range(size)])


def summed_over_chips(block, axis):
    size = lax.axis_size(axis)
    if size & (size - 1):
        return lax.psum(block, axis, axis_index_groups=[list(range(c, size, 2)) for c in range(2)])
    step = 2
    while step < size:
        others = [step] if 2 * step >= size else [step, 2 * step, 3 * step]
        block = sum([flipped(block, axis, other) for other in others], block)
        step *= 4
    return block


def paired(block, first):
    size, meets = lax.axis_size("tm"), lax.axis_size("meet")
    pairs = []
    for meet in range(meets):
        at = meet * size
        pairs += [(at + i, at + i + 1) for i in range(first, size - 1, 2)]
        if first and meets % 2:
            pairs.append((at, at + size - 1))
        elif first and meet % 2 == 0:
            pairs += [(at + end, at + size + end) for end in (0, size - 1)]
    return lax.ppermute(block, ("meet", "tm"), pairs + [(j, i) for i, j in pairs])


def per_device(waveform, masks, valid, ref_mic, conv1_w, conv1_b, conv2_w, conv2_b, proj_w, proj_b):
    frames = masks.shape[1]
    channels = conv1_w.shape[1]
    width = proj_w.shape[1]
    vmem = pl.BlockSpec(memory_space=pltpu.VMEM)
    smem = pl.BlockSpec(memory_space=pltpu.SMEM)
    hbm = pl.BlockSpec(memory_space=pltpu.HBM)
    in_hbm = functools.partial(pltpu.with_memory_space_constraint, memory_space=pltpu.HBM)
    params = pltpu.CompilerParams(vmem_limit_bytes=16 * 1024 * 1024)
    rim = jax.ShapeDtypeStruct((MICS, LEAD), waveform.dtype)
    table = dft_table()
    conv2_w = conv2_w.reshape(-1, channels)
    beside, across, framed, levels, table = pl.pallas_call(
        functools.partial(rims_kernel, frames),
        out_shape=(rim, rim, jax.ShapeDtypeStruct((frames * MICS, NFFT), waveform.dtype))
        + tuple(jax.ShapeDtypeStruct(x.shape, x.dtype) for x in (masks, table)),
        in_specs=[hbm] * 3,
        out_specs=(vmem,) * 5,
        scratch_shapes=[pltpu.VMEM(waveform.shape, waveform.dtype), pltpu.SemaphoreType.DMA((3,))],
        compiler_params=params,
        name="rims",
    )(in_hbm(waveform), in_hbm(masks), in_hbm(table))
    got_across = paired(across, 1)
    spec, kept, edge_weight, conv2_w = pl.pallas_call(
        functools.partial(stats_kernel, frames),
        out_shape=(
            jax.ShapeDtypeStruct((2 * TILES, frames * MICS, LANES), jnp.float32),
            jax.ShapeDtypeStruct((TILES, STATS, LANES), jnp.float32),
            jax.ShapeDtypeStruct((TILES, 2, MICS, LANES), jnp.float32),
            jax.ShapeDtypeStruct(conv2_w.shape, conv2_w.dtype),
        ),
        in_specs=[vmem] * 3 + [hbm, smem],
        out_specs=(vmem,) * 4,
        scratch_shapes=[
            pltpu.VMEM((TILES, 2, frames, LANES), jnp.float32),
            pltpu.SemaphoreType.DMA((1,)),
        ],
        compiler_params=params,
        name="stats",
    )(framed, levels, table, in_hbm(conv2_w), valid)
    edge_rows = (HALO + 1) * MICS
    sent_rows = STATS + MICS + LEAD // LANES * MICS + 4 * MICS
    across_spec, mine, theirs = pl.pallas_call(
        functools.partial(edges_kernel, lax.axis_size("tm")),
        out_shape=tuple(
            jax.ShapeDtypeStruct(shape, jnp.float32)
            for shape in ((2 * TILES, edge_rows, LANES), (STATS + MICS, LANES), (sent_rows, LANES))
        ),
        in_specs=[vmem] * 6,
        out_specs=(vmem,) * 3,
        scratch_shapes=[pltpu.VMEM((edge_rows, NFFT), jnp.float32)],
        compiler_params=params,
        name="edges",
    )(across, got_across, beside, table, edge_weight, kept)
    stats, edge_spec = pl.pallas_call(
        chip_kernel,
        out_shape=tuple(
            jax.ShapeDtypeStruct(shape, jnp.float32) for shape in ((STATS + MICS, LANES), (2 * TILES, MICS * MICS, LANES))
        ),
        in_specs=[vmem] * 6,
        out_specs=(vmem,) * 2,
        scratch_shapes=[pltpu.VMEM((edge_rows, NFFT), jnp.float32)],
        compiler_params=params,
        name="chip",
    )(mine, flipped(theirs, "tm", 1), beside, table, edge_weight, across_spec)
    stats = summed_over_chips(stats, "tm")
    beam = jax.ShapeDtypeStruct((2 * MICS, LANES), jnp.float32)
    beam_mine, beam_last = pl.pallas_call(
        solve_kernel,
        out_shape=(beam, beam),
        in_specs=[vmem, smem],
        out_specs=(vmem, vmem),
        compiler_params=params,
        name="solve",
    )(stats, ref_mic)
    beam_theirs = flipped(beam_mine, "tm", 1)
    rows = frames + MICS
    bank = packed_mel_bank()
    mel = pl.pallas_call(
        power_kernel,
        out_shape=jax.ShapeDtypeStruct((rows, 2 * LANES), jnp.float32),
        in_specs=[vmem] * 5,
        out_specs=vmem,
        compiler_params=params,
        name="power",
    )(beam_mine, beam_last, spec, edge_spec, bank)
    return pl.pallas_call(
        functools.partial(stem_kernel, frames),
        out_shape=jax.ShapeDtypeStruct((1, frames // 4, width), jnp.bfloat16),
        in_specs=[vmem] * 4 + [smem] + [vmem] * 7,
        out_specs=vmem,
        scratch_shapes=[pltpu.VMEM((2, rows, LANES), jnp.float32), pltpu.VMEM((LANES, channels), jnp.float32)],
        compiler_params=params,
        name="stem",
    )(
        beam_theirs,
        mel,
        spec,
        edge_spec,
        valid,
        bank,
        conv1_w,
        conv1_b[None],
        conv2_w,
        conv2_b[None],
        proj_w,
        proj_b[None],
    )


def solution(mesh):
    return jax.shard_map(
        per_device,
        mesh=mesh,
        in_specs=(
            P(None, ("meet", "tm")),
            P(None, ("meet", "tm"), None),
            P("meet"),
            P("meet"),
            P(),
            P(),
            P(),
            P(),
            P(),
            P(),
        ),
        out_specs=P(None, ("meet", "tm"), None),
        check_vma=False,
    )
```

```python
import functools
import math

import jax
import jax.numpy as jnp
import numpy as np
from jax import lax
from jax.experimental import pallas as pl
from jax.experimental.pallas import tpu as pltpu
from jax.sharding import PartitionSpec as P

NFFT = 512
HOP = 160
MELS = 80
BINS = NFFT // 2 + 1
LANES = 128
MICS = 8
PAD_BINS = -(-BINS // LANES) * LANES
TILES = PAD_BINS // LANES
HALO = 3
LEAD = 512
TAIL = 384
STATS = 2 * MICS * MICS
SPAN = 42

loading = 0.03
epsilon = 1e-06
sample_rate = 16000.0


def dft_table():
    n = np.arange(NFFT)
    f = np.arange(BINS)
    phase = 2.0 * math.pi * ((n[:, None] * f[None, :]) % NFFT) / NFFT
    window = 0.5 - 0.5 * np.cos(2.0 * math.pi * n / NFFT)
    table = np.zeros((NFFT, 2, PAD_BINS), np.float32)
    table[:, 0, :BINS] = window[:, None] * np.cos(phase)
    table[:, 1, :BINS] = -window[:, None] * np.sin(phase)
    return jnp.asarray(table.reshape(NFFT, 2 * PAD_BINS)).astype(jnp.bfloat16)


def mel_bank():
    mel_top = 2595.0 * math.log10(1.0 + sample_rate / 2.0 / 700.0)
    points = np.arange(MELS + 2) * (mel_top / (MELS + 1))
    edges = 700.0 * (np.power(10.0, points / 2595.0) - 1.0)
    freq = np.arange(BINS) * (sample_rate / 2.0 / (BINS - 1))
    lower, centre, upper = edges[:-2], edges[1:-1], edges[2:]
    rising = (freq[:, None] - lower[None, :]) / (centre - lower)[None, :]
    falling = (upper[None, :] - freq[:, None]) / (upper - centre)[None, :]
    return np.maximum(np.minimum(rising, falling), 0.0).astype(np.float32)


def packed_mel_bank():
    bank = mel_bank()
    packed = np.zeros((PAD_BINS, 2, LANES), np.float32)
    for half in range(2):
        part = bank[:, half * 40 : half * 40 + SPAN]
        for copy in range(3):
            packed[:BINS, half, copy * SPAN : copy * SPAN + part.shape[1]] = part
    return jnp.asarray(packed.reshape(TILES, LANES, 2 * LANES))


def cyclic_pairs(x_re, x_im):
    pairs = [x_re * x_re + x_im * x_im]
    for shift in range(1, MICS // 2):
        y_re = pltpu.roll(x_re, MICS - shift, 0)
        y_im = pltpu.roll(x_im, MICS - shift, 0)
        pairs.append(x_re * y_re + x_im * y_im)
        pairs.append(x_im * y_re - x_re * y_im)
    low = lax.broadcasted_iota(jnp.int32, x_re.shape, 0) < MICS // 2
    y_re, y_im = pltpu.roll(x_re, MICS // 2, 0), pltpu.roll(x_im, MICS // 2, 0)
    pairs.append(jnp.where(low, x_re, x_im) * y_re + jnp.where(low, x_im, -x_re) * y_im)
    return pairs


def add_frame(sums, x_re, x_im, weights):
    pairs = cyclic_pairs(x_re, x_im)
    out = []
    for k in range(2):
        w = jnp.broadcast_to(weights[k], (MICS, LANES))
        out.extend(sums[k * len(pairs) + i] + w * pair for i, pair in enumerate(pairs))
    return tuple(out)


def slot_tiles(position):
    core = position % 2
    return core, 1 - core, TILES - 1


def started(pairs, sem):
    copies = [pltpu.make_async_copy(source, target, sem.at[i]) for i, (source, target) in enumerate(pairs)]
    for copy in copies:
        copy.start()
    return copies


def rims_kernel(frames, wave_hbm, masks_hbm, table_hbm, beside_ref, across_ref, framed_ref, masks_ref, table_ref, wave_ref, sem):
    copies = started(((wave_hbm, wave_ref), (table_hbm, table_ref), (masks_hbm, masks_ref)), sem)
    even = lax.axis_index("tm") % 2 == 0
    copies[0].wait()
    head = wave_ref[:, :LEAD].astype(jnp.float32)
    tail = wave_ref[:, wave_ref.shape[1] - LEAD :].astype(jnp.float32)
    beside_ref[...] = jnp.where(even, tail, head).astype(beside_ref.dtype)
    across_ref[...] = jnp.where(even, head, tail).astype(across_ref.dtype)
    wave = wave_ref[...].astype(jnp.float32)
    width = wave.shape[1]
    rolled = {}

    def frame_of(frame):
        if frame >= frames - HALO:
            return jnp.zeros((MICS, NFFT), jnp.float32)
        base, shift = frame * HOP // LANES * LANES, frame * HOP % LANES
        if shift not in rolled:
            rolled[shift] = wave if shift == 0 else pltpu.roll(wave, width - shift, 1)
        return rolled[shift][:, base : base + NFFT]

    for frame in range(0, frames, 2):
        pair = jnp.concatenate([frame_of(frame), frame_of(frame + 1)], axis=0)
        framed_ref[MICS * frame : MICS * (frame + 2), :] = pair.astype(framed_ref.dtype)
    copies[1].wait()
    copies[2].wait()


def last_bin_sums(frames, spec_ref, weight_ref):
    x_re = x_im = jnp.zeros((MICS, LANES), jnp.float32)
    for frame in range(frames):
        rows = slice(MICS * frame, MICS * (frame + 1))
        part_re, part_im = spec_ref[TILES - 1, rows, :], spec_ref[2 * TILES - 1, rows, :]
        x_re = x_re + (pltpu.roll(part_re, frame, 1) if frame else part_re)
        x_im = x_im + (pltpu.roll(part_im, frame, 1) if frame else part_im)
    frame = lax.broadcasted_iota(jnp.int32, (frames, LANES), 0)
    lane = lax.broadcasted_iota(jnp.int32, (frames, LANES), 1)
    sums = []
    for k in range(2):
        weight = weight_ref[TILES - 1, k][:, :1]
        weight = jnp.sum(jnp.where(frame == lane, weight, 0.0), axis=0, keepdims=True)
        for pair in cyclic_pairs(x_re, x_im):
            total = jnp.sum(pair * weight, axis=1, keepdims=True)
            sums.append(jnp.where(lane[:MICS] == 0, total, 0.0))
    return jnp.concatenate(sums, axis=0)


def stats_kernel(frames, framed_ref, masks_ref, table_ref, conv2_w_hbm, valid_ref, spec_ref, kept_ref, edge_weight_ref, conv2_w_ref, weight_ref, sem):
    copies = started(((conv2_w_hbm, conv2_w_ref),), sem)
    position = lax.axis_index("tm")
    spec = jnp.dot(framed_ref[...], table_ref[...], preferred_element_type=jnp.float32)
    for tile in range(2 * TILES):
        spec_ref[tile] = spec[:, tile * LANES : (tile + 1) * LANES]

    row = lax.broadcasted_iota(jnp.int32, (frames, 1), 0)
    live = jnp.where(position * frames + row < valid_ref[0], 1.0 / 255.0, 0.0)
    weight_ref[TILES - 1] = jnp.zeros((2, frames, LANES), jnp.float32)
    for k in range(2):
        weight = masks_ref[k].astype(jnp.float32) * live
        for tile in range(TILES):
            kept_lanes = min(LANES, BINS - tile * LANES)
            weight_ref[tile, k, :, :kept_lanes] = weight[:, tile * LANES : tile * LANES + kept_lanes]
    edge_weight_ref[...] = weight_ref[:, :, frames - MICS :, :]

    for slot, tile in enumerate(slot_tiles(position)[:2]):

        def add_frames(group, sums):
            first = pl.multiple_of(group * MICS, MICS)
            weights = [weight_ref[tile, k, pl.ds(first, MICS), :] for k in range(2)]
            for frame in range(MICS):
                rows = pl.ds(pl.multiple_of((first + frame) * MICS, MICS), MICS)
                sums = add_frame(
                    sums, spec_ref[tile, rows, :], spec_ref[TILES + tile, rows, :], [w[frame : frame + 1] for w in weights]
                )
            return sums

        zero = jnp.zeros((MICS, LANES), jnp.float32)
        kept_ref[slot] = jnp.concatenate(lax.fori_loop(0, frames // MICS, add_frames, (zero,) * 2 * MICS, unroll=2), axis=0)
    kept_ref[2] = last_bin_sums(frames, spec_ref, weight_ref)
    for copy in copies:
        copy.wait()


def edges_kernel(devices, own0_ref, own1_ref, got0_ref, got1_ref, table_ref, edge_weight_ref, kept_ref, spec_ref, mine_ref, theirs_ref, framed_ref):
    position = lax.axis_index("tm")
    even = position % 2 == 0
    own = [own0_ref[...].astype(jnp.float32), own1_ref[...].astype(jnp.float32)]
    got = [got0_ref[...].astype(jnp.float32), got1_ref[...].astype(jnp.float32)]
    head, tail = jnp.where(even, own[1], own[0]), jnp.where(even, own[0], own[1])
    prev, after = jnp.where(even, got[1], got[0]), jnp.where(even, got[0], got[1])
    prev = jnp.where(position > 0, prev, 0.0)
    after = jnp.where(position < devices - 1, after, 0.0)
    joined = jnp.concatenate(
        [jnp.concatenate([prev, head[:, :TAIL]], axis=1), jnp.concatenate([tail, after[:, :TAIL]], axis=1)], axis=0
    )
    for i in range(HALO):
        start = LEAD - HALO * HOP + i * HOP
        base, shift = start // LANES * LANES, start % LANES
        turned = joined if shift == 0 else pltpu.roll(joined, joined.shape[1] - shift, 1)
        framed_ref[2 * MICS * i : 2 * MICS * (i + 1), :] = turned[:, base : base + NFFT]
    used = 2 * MICS * HALO
    framed_ref[used:, :] = jnp.zeros((framed_ref.shape[0] - used, NFFT), jnp.float32)
    spec = jnp.dot(framed_ref[...].astype(jnp.bfloat16), table_ref[...], preferred_element_type=jnp.float32)
    for tile in range(2 * TILES):
        spec_ref[tile] = spec[:, tile * LANES : (tile + 1) * LANES]
    for slot, tile in enumerate(slot_tiles(position)):
        sums = (jnp.zeros((MICS, LANES), jnp.float32),) * 2 * MICS
        for i in range(HALO):
            rows = slice((2 * i + 1) * MICS, (2 * i + 2) * MICS)
            at = MICS - HALO + i
            weights = [edge_weight_ref[tile, k, at : at + 1, :] for k in range(2)]
            sums = add_frame(sums, spec_ref[tile, rows, :], spec_ref[TILES + tile, rows, :], weights)
        total = kept_ref[slot] + jnp.concatenate(sums, axis=0)
        if slot == 0:
            mine_ref[:STATS, :] = total
        elif slot == 1:
            theirs_ref[:STATS, :] = total
        else:
            last_bin = jnp.transpose(total)[:MICS]
            mine_ref[STATS:, :] = last_bin
            theirs_ref[STATS:, :] = last_bin


def columns_of(kept, sub):
    low = sub < MICS // 2
    diag_re = [kept[0], kept[1], kept[3], kept[5]]
    diag_im = [jnp.zeros_like(kept[0]), kept[2], kept[4], kept[6]]
    turned = pltpu.roll(kept[7], MICS // 2, 0)
    diag_re.append(jnp.where(low, kept[7], turned))
    diag_im.append(jnp.where(low, -turned, kept[7]))
    for shift in range(MICS // 2 + 1, MICS):
        diag_re.append(pltpu.roll(diag_re[MICS - shift], MICS - shift, 0))
        diag_im.append(-pltpu.roll(diag_im[MICS - shift], MICS - shift, 0))
    columns = []
    for n in range(MICS):
        re, im = diag_re[n], diag_im[n]
        for m in range(1, MICS):
            re = jnp.where(sub == m, diag_re[(n - m) % MICS], re)
            im = jnp.where(sub == m, diag_im[(n - m) % MICS], im)
        columns.append((re, im))
    return columns


def beams_of(stats, ref_mic):
    sub = lax.broadcasted_iota(jnp.int32, stats[0].shape, 0)
    answer = columns_of(stats[:MICS], sub)
    matrix = columns_of(stats[MICS:], sub)
    spread = jnp.sum(stats[MICS], axis=0, keepdims=True)
    ridge = loading * spread / MICS + epsilon
    matrix = [(jnp.where(sub == n, re + ridge, re), im) for n, (re, im) in enumerate(matrix)]
    for pivot in range(MICS):
        col_re, col_im = matrix[pivot]
        pivot_re = col_re[pivot : pivot + 1]
        pivot_im = col_im[pivot : pivot + 1]
        modulus = pivot_re * pivot_re + pivot_im * pivot_im
        inverse_re = pivot_re / modulus
        inverse_im = -pivot_im / modulus

        def eliminated(column):
            re, im = column
            row_re, row_im = re[pivot : pivot + 1], im[pivot : pivot + 1]
            lead_re = row_re * inverse_re - row_im * inverse_im
            lead_im = row_re * inverse_im + row_im * inverse_re
            return (
                jnp.where(sub == pivot, lead_re, re - (col_re * lead_re - col_im * lead_im)),
                jnp.where(sub == pivot, lead_im, im - (col_re * lead_im + col_im * lead_re)),
            )

        matrix = [eliminated(c) if n > pivot else c for n, c in enumerate(matrix)]
        answer = [eliminated(c) for c in answer]
    trace = answer[0][0][0:1]
    beam_re, beam_im = answer[0]
    for n in range(1, MICS):
        trace = trace + answer[n][0][n : n + 1]
        beam_re = jnp.where(ref_mic == n, answer[n][0], beam_re)
        beam_im = jnp.where(ref_mic == n, answer[n][1], beam_im)
    scale = 1.0 / (trace + epsilon)
    return beam_re * scale, beam_im * scale


def solve_kernel(stats_ref, ref_mic_ref, beam_ref, last_ref):
    blank = jnp.zeros((LANES - MICS, LANES), jnp.float32)
    last_bin = jnp.transpose(jnp.concatenate([stats_ref[STATS:, :], blank], axis=0))
    for out_ref, stats in ((beam_ref, stats_ref[:STATS, :]), (last_ref, last_bin)):
        kept = [stats[i * MICS : (i + 1) * MICS] for i in range(2 * MICS)]
        beam_re, beam_im = beams_of(kept, ref_mic_ref[0])
        out_ref[:MICS, :] = beam_re
        out_ref[MICS:, :] = beam_im


def power_of(beam_ref, tile, spec_ref, edge_spec_ref):
    beam_re, beam_im = beam_ref[:MICS, :], beam_ref[MICS:, :]
    groups = spec_ref.shape[1] // (MICS * MICS)
    power = []
    for group in range(groups + 1):
        from_ref, first = (spec_ref, group * MICS * MICS) if group < groups else (edge_spec_ref, 0)
        sum_re = sum_im = None
        for m in range(MICS):
            rows = pl.ds(first + m, MICS, stride=MICS)
            x_re, x_im = from_ref[tile, rows, :], from_ref[TILES + tile, rows, :]
            b_re, b_im = beam_re[m : m + 1], beam_im[m : m + 1]
            part_re = b_re * x_re + b_im * x_im
            part_im = b_re * x_im - b_im * x_re
            sum_re = part_re if sum_re is None else sum_re + part_re
            sum_im = part_im if sum_im is None else sum_im + part_im
        power.append(sum_re * sum_re + sum_im * sum_im)
    return jnp.concatenate(power, axis=0)


def mel_of(power, bank):
    return jnp.dot(power, bank, precision=lax.Precision.HIGHEST, preferred_element_type=jnp.float32)


def power_kernel(mine_ref, last_ref, spec_ref, edge_spec_ref, bank_ref, mel_ref):
    mine, _, last = slot_tiles(lax.axis_index("tm"))
    power = [power_of(beam_ref, tile, spec_ref, edge_spec_ref) for beam_ref, tile in ((mine_ref, mine), (last_ref, last))]
    bank = jnp.concatenate([bank_ref[mine], bank_ref[last]], axis=0)
    mel_ref[...] = mel_of(jnp.concatenate(power, axis=1), bank)


def stem_kernel(frames, theirs_ref, mel_ref, spec_ref, edge_spec_ref, valid_ref, bank_ref, conv1_w_ref, conv1_b_ref, conv2_w_ref, conv2_b_ref, proj_w_ref, proj_b_ref, out_ref, logmel_ref, conv1_ref):
    position = lax.axis_index("tm")
    valid = valid_ref[0]
    quarter = frames // 4
    channels = conv1_w_ref.shape[1]
    conv1_ref[...] = jnp.zeros((LANES, channels), jnp.float32)
    for shift_t in range(3):
        conv1_ref[SPAN * shift_t : SPAN * shift_t + 3, :] = conv1_w_ref[3 * shift_t : 3 * shift_t + 3, :].astype(jnp.float32)
    conv1 = conv1_ref[...].astype(jnp.bfloat16)

    theirs = slot_tiles(position)[1]
    mel = mel_ref[...] + mel_of(power_of(theirs_ref, theirs, spec_ref, edge_spec_ref), bank_ref[theirs])
    row = lax.broadcasted_iota(jnp.int32, (frames + MICS, 1), 0)
    edge = (row - frames) // 2 + jnp.where((row - frames) % 2 == 0, -HALO, frames - HALO)
    time = position * frames + jnp.where(row < frames, row, edge)
    live = (time >= 0) & (time < valid)
    logmel = jnp.where(live, jnp.log(mel + epsilon), 0.0)
    logmel = logmel.astype(jnp.bfloat16).astype(jnp.float32)
    for half in range(2):
        part = logmel[:, half * LANES : (half + 1) * LANES]
        logmel_ref[half, HALO : HALO + frames, :] = part[:frames]
        for i in range(HALO):
            logmel_ref[half, i : i + 1, :] = part[frames + 2 * i : frames + 2 * i + 1]
            logmel_ref[half, frames + i : frames + i + 1, :] = part[frames + 2 * i + 1 : frames + 2 * i + 2]

    q_first = (MELS - 3) // 2 + 1
    q_second = (q_first - 3) // 2 + 1
    order = list(range(0, q_first, 2)) + list(range(1, q_first, 2))
    evens = (q_first + 1) // 2
    lane = lax.broadcasted_iota(jnp.int32, (quarter, LANES), 1)
    row = lax.broadcasted_iota(jnp.int32, (quarter, 1), 0)
    windows = []
    for tap in range(3):
        packs = []
        for half in range(2):
            rows = [logmel_ref[half, pl.ds(2 * tap + a, quarter, stride=4), :] for a in range(3)]
            packs.append(jnp.where(lane < SPAN, rows[0], jnp.where(lane < 2 * SPAN, rows[1], rows[2])))
        patches = []
        for q in order:
            half, shift = (0, 2 * q) if q < 20 else (1, 2 * q - 40)
            patches.append(packs[half] if shift == 0 else pltpu.roll(packs[half], LANES - shift, 1))
        patches = jnp.concatenate(patches, axis=0).astype(jnp.bfloat16)
        layer = jnp.dot(patches, conv1, preferred_element_type=jnp.float32) + conv1_b_ref[...]
        layer = jnp.maximum(layer, 0.0)
        if tap == 0:
            keep = jnp.concatenate([row + 2 * quarter * position >= 1] * q_first, axis=0)
            layer = jnp.where(keep, layer, 0.0)
        layer = layer.astype(jnp.bfloat16)
        count = quarter * q_second
        windows.append(layer[:count])
        windows.append(layer[quarter * evens : quarter * evens + count])
        windows.append(layer[quarter : quarter + count])
    second = jnp.dot(jnp.concatenate(windows, axis=1), conv2_w_ref[...], preferred_element_type=jnp.float32)
    second = jnp.maximum(second + conv2_b_ref[...], 0.0).astype(jnp.bfloat16)
    flat = jnp.concatenate([second[quarter * r : quarter * (r + 1)] for r in range(q_second)], axis=1)
    features = jnp.dot(flat, proj_w_ref[...], preferred_element_type=jnp.float32) + proj_b_ref[...]
    features = jnp.where(position * frames + 4 * row < valid, features, 0.0)
    out_ref[0] = features.astype(jnp.bfloat16)


def flipped(block, axis, step):
    size = lax.axis_size(axis)
    return lax.ppermute(block, axis, [(i, i ^ step) for i in range(size)])


def summed_over_chips(block, axis):
    size = lax.axis_size(axis)
    if size & (size - 1):
        return lax.psum(block, axis, axis_index_groups=[list(range(c, size, 2)) for c in range(2)])
    step = 2
    while step < size:
        others = [step] if 2 * step >= size else [step, 2 * step, 3 * step]
        block = sum([flipped(block, axis, other) for other in others], block)
        step *= 4
    return block


def paired(block, first):
    size, meets = lax.axis_size("tm"), lax.axis_size("meet")
    pairs = []
    for meet in range(meets):
        at = meet * size
        pairs += [(at + i, at + i + 1) for i in range(first, size - 1, 2)]
        if first and meets % 2:
            pairs.append((at, at + size - 1))
        elif first and meet % 2 == 0:
            pairs += [(at + end, at + size + end) for end in (0, size - 1)]
    return lax.ppermute(block, ("meet", "tm"), pairs + [(j, i) for i, j in pairs])


def per_device(waveform, masks, valid, ref_mic, conv1_w, conv1_b, conv2_w, conv2_b, proj_w, proj_b):
    frames = masks.shape[1]
    channels = conv1_w.shape[1]
    width = proj_w.shape[1]
    vmem = pl.BlockSpec(memory_space=pltpu.VMEM)
    smem = pl.BlockSpec(memory_space=pltpu.SMEM)
    hbm = pl.BlockSpec(memory_space=pltpu.HBM)
    in_hbm = functools.partial(pltpu.with_memory_space_constraint, memory_space=pltpu.HBM)
    params = pltpu.CompilerParams(vmem_limit_bytes=16 * 1024 * 1024)
    rim = jax.ShapeDtypeStruct((MICS, LEAD), waveform.dtype)
    table = dft_table()
    conv2_w = conv2_w.reshape(-1, channels)
    beside, across, framed, levels, table = pl.pallas_call(
        functools.partial(rims_kernel, frames),
        out_shape=(rim, rim, jax.ShapeDtypeStruct((frames * MICS, NFFT), waveform.dtype))
        + tuple(jax.ShapeDtypeStruct(x.shape, x.dtype) for x in (masks, table)),
        in_specs=[hbm] * 3,
        out_specs=(vmem,) * 5,
        scratch_shapes=[pltpu.VMEM(waveform.shape, waveform.dtype), pltpu.SemaphoreType.DMA((3,))],
        compiler_params=params,
        name="rims",
    )(in_hbm(waveform), in_hbm(masks), in_hbm(table))
    got_across = paired(across, 1)
    got_beside = paired(beside, 0)
    stat_block = jax.ShapeDtypeStruct((STATS + MICS, LANES), jnp.float32)
    spec, kept, edge_weight, conv2_w = pl.pallas_call(
        functools.partial(stats_kernel, frames),
        out_shape=(
            jax.ShapeDtypeStruct((2 * TILES, frames * MICS, LANES), jnp.float32),
            jax.ShapeDtypeStruct((TILES, STATS, LANES), jnp.float32),
            jax.ShapeDtypeStruct((TILES, 2, MICS, LANES), jnp.float32),
            jax.ShapeDtypeStruct(conv2_w.shape, conv2_w.dtype),
        ),
        in_specs=[vmem] * 3 + [hbm, smem],
        out_specs=(vmem,) * 4,
        scratch_shapes=[
            pltpu.VMEM((TILES, 2, frames, LANES), jnp.float32),
            pltpu.SemaphoreType.DMA((1,)),
        ],
        compiler_params=params,
        name="stats",
    )(framed, levels, table, in_hbm(conv2_w), valid)
    edge_spec, mine, theirs = pl.pallas_call(
        functools.partial(edges_kernel, lax.axis_size("tm")),
        out_shape=(jax.ShapeDtypeStruct((2 * TILES, MICS * MICS, LANES), jnp.float32), stat_block, stat_block),
        in_specs=[vmem] * 7,
        out_specs=(vmem,) * 3,
        scratch_shapes=[pltpu.VMEM((MICS * MICS, NFFT), jnp.float32)],
        compiler_params=params,
        name="edges",
    )(beside, across, got_beside, got_across, table, edge_weight, kept)
    stats = summed_over_chips(mine + flipped(theirs, "tm", 1), "tm")
    beam = jax.ShapeDtypeStruct((2 * MICS, LANES), jnp.float32)
    beam_mine, beam_last = pl.pallas_call(
        solve_kernel,
        out_shape=(beam, beam),
        in_specs=[vmem, smem],
        out_specs=(vmem, vmem),
        compiler_params=params,
        name="solve",
    )(stats, ref_mic)
    beam_theirs = flipped(beam_mine, "tm", 1)
    rows = frames + MICS
    bank = packed_mel_bank()
    mel = pl.pallas_call(
        power_kernel,
        out_shape=jax.ShapeDtypeStruct((rows, 2 * LANES), jnp.float32),
        in_specs=[vmem] * 5,
        out_specs=vmem,
        compiler_params=params,
        name="power",
    )(beam_mine, beam_last, spec, edge_spec, bank)
    return pl.pallas_call(
        functools.partial(stem_kernel, frames),
        out_shape=jax.ShapeDtypeStruct((1, frames // 4, width), jnp.bfloat16),
        in_specs=[vmem] * 4 + [smem] + [vmem] * 7,
        out_specs=vmem,
        scratch_shapes=[pltpu.VMEM((2, rows, LANES), jnp.float32), pltpu.VMEM((LANES, channels), jnp.float32)],
        compiler_params=params,
        name="stem",
    )(
        beam_theirs,
        mel,
        spec,
        edge_spec,
        valid,
        bank,
        conv1_w,
        conv1_b[None],
        conv2_w,
        conv2_b[None],
        proj_w,
        proj_b[None],
    )


def solution(mesh):
    return jax.shard_map(
        per_device,
        mesh=mesh,
        in_specs=(
            P(None, ("meet", "tm")),
            P(None, ("meet", "tm"), None),
            P("meet"),
            P("meet"),
            P(),
            P(),
            P(),
            P(),
            P(),
            P(),
        ),
        out_specs=P(None, ("meet", "tm"), None),
        check_vma=False,
    )
```

```python
import functools
import math

import jax
import jax.numpy as jnp
import numpy as np
from jax import lax
from jax.experimental import pallas as pl
from jax.experimental.pallas import tpu as pltpu
from jax.sharding import PartitionSpec as P

NFFT = 512
HOP = 160
MELS = 80
BINS = NFFT // 2 + 1
LANES = 128
MICS = 8
PAD_BINS = -(-BINS // LANES) * LANES
TILES = PAD_BINS // LANES
HALO = 3
LEAD = 512
TAIL = 384
STATS = 2 * MICS * MICS
SPAN = 42

loading = 0.03
epsilon = 1e-06
sample_rate = 16000.0


def dft_table():
    n = np.arange(NFFT)
    f = np.arange(BINS)
    phase = 2.0 * math.pi * ((n[:, None] * f[None, :]) % NFFT) / NFFT
    window = 0.5 - 0.5 * np.cos(2.0 * math.pi * n / NFFT)
    table = np.zeros((NFFT, 2, PAD_BINS), np.float32)
    table[:, 0, :BINS] = window[:, None] * np.cos(phase)
    table[:, 1, :BINS] = -window[:, None] * np.sin(phase)
    return jnp.asarray(table.reshape(NFFT, 2 * PAD_BINS)).astype(jnp.bfloat16)


def mel_bank():
    mel_top = 2595.0 * math.log10(1.0 + sample_rate / 2.0 / 700.0)
    points = np.arange(MELS + 2) * (mel_top / (MELS + 1))
    edges = 700.0 * (np.power(10.0, points / 2595.0) - 1.0)
    freq = np.arange(BINS) * (sample_rate / 2.0 / (BINS - 1))
    lower, centre, upper = edges[:-2], edges[1:-1], edges[2:]
    rising = (freq[:, None] - lower[None, :]) / (centre - lower)[None, :]
    falling = (upper[None, :] - freq[:, None]) / (upper - centre)[None, :]
    return np.maximum(np.minimum(rising, falling), 0.0).astype(np.float32)


def packed_mel_bank():
    bank = mel_bank()
    packed = np.zeros((PAD_BINS, 2, LANES), np.float32)
    for half in range(2):
        part = bank[:, half * 40 : half * 40 + SPAN]
        for copy in range(3):
            packed[:BINS, half, copy * SPAN : copy * SPAN + part.shape[1]] = part
    return jnp.asarray(packed.reshape(TILES, LANES, 2 * LANES))


def cyclic_pairs(x_re, x_im):
    pairs = [x_re * x_re + x_im * x_im]
    for shift in range(1, MICS // 2):
        y_re = pltpu.roll(x_re, MICS - shift, 0)
        y_im = pltpu.roll(x_im, MICS - shift, 0)
        pairs.append(x_re * y_re + x_im * y_im)
        pairs.append(x_im * y_re - x_re * y_im)
    low = lax.broadcasted_iota(jnp.int32, x_re.shape, 0) < MICS // 2
    y_re, y_im = pltpu.roll(x_re, MICS // 2, 0), pltpu.roll(x_im, MICS // 2, 0)
    pairs.append(jnp.where(low, x_re, x_im) * y_re + jnp.where(low, x_im, -x_re) * y_im)
    return pairs


def add_frame(sums, x_re, x_im, weights):
    pairs = cyclic_pairs(x_re, x_im)
    out = []
    for k in range(2):
        w = jnp.broadcast_to(weights[k], (MICS, LANES))
        out.extend(sums[k * len(pairs) + i] + w * pair for i, pair in enumerate(pairs))
    return tuple(out)


def slot_tiles(position):
    core = position % 2
    return core, 1 - core, TILES - 1


def started(pairs, sem):
    copies = [pltpu.make_async_copy(source, target, sem.at[i]) for i, (source, target) in enumerate(pairs)]
    for copy in copies:
        copy.start()
    return copies


def rims_kernel(frames, wave_hbm, masks_hbm, table_hbm, beside_ref, across_ref, framed_ref, masks_ref, table_ref, wave_ref, sem):
    copies = started(((wave_hbm, wave_ref), (table_hbm, table_ref), (masks_hbm, masks_ref)), sem)
    even = lax.axis_index("tm") % 2 == 0
    copies[0].wait()
    head = wave_ref[:, :LEAD].astype(jnp.float32)
    tail = wave_ref[:, wave_ref.shape[1] - LEAD :].astype(jnp.float32)
    beside_ref[...] = jnp.where(even, tail, head).astype(beside_ref.dtype)
    across_ref[...] = jnp.where(even, head, tail).astype(across_ref.dtype)
    wave = wave_ref[...].astype(jnp.float32)
    width = wave.shape[1]
    rolled = {}

    def frame_of(frame):
        if frame >= frames - HALO:
            return jnp.zeros((MICS, NFFT), jnp.float32)
        base, shift = frame * HOP // LANES * LANES, frame * HOP % LANES
        if shift not in rolled:
            rolled[shift] = wave if shift == 0 else pltpu.roll(wave, width - shift, 1)
        return rolled[shift][:, base : base + NFFT]

    for frame in range(0, frames, 2):
        pair = jnp.concatenate([frame_of(frame), frame_of(frame + 1)], axis=0)
        framed_ref[MICS * frame : MICS * (frame + 2), :] = pair.astype(framed_ref.dtype)
    copies[1].wait()
    copies[2].wait()


def last_bin_sums(frames, spec_ref, weight_ref):
    x_re = x_im = jnp.zeros((MICS, LANES), jnp.float32)
    for frame in range(frames):
        rows = slice(MICS * frame, MICS * (frame + 1))
        part_re, part_im = spec_ref[TILES - 1, rows, :], spec_ref[2 * TILES - 1, rows, :]
        x_re = x_re + (pltpu.roll(part_re, frame, 1) if frame else part_re)
        x_im = x_im + (pltpu.roll(part_im, frame, 1) if frame else part_im)
    frame = lax.broadcasted_iota(jnp.int32, (frames, LANES), 0)
    lane = lax.broadcasted_iota(jnp.int32, (frames, LANES), 1)
    sums = []
    for k in range(2):
        weight = weight_ref[TILES - 1, k][:, :1]
        weight = jnp.sum(jnp.where(frame == lane, weight, 0.0), axis=0, keepdims=True)
        for pair in cyclic_pairs(x_re, x_im):
            total = jnp.sum(pair * weight, axis=1, keepdims=True)
            sums.append(jnp.where(lane[:MICS] == 0, total, 0.0))
    return jnp.concatenate(sums, axis=0)


def stats_kernel(frames, framed_ref, masks_ref, table_ref, conv2_w_hbm, valid_ref, spec_ref, kept_ref, edge_weight_ref, conv2_w_ref, weight_ref, sem):
    copies = started(((conv2_w_hbm, conv2_w_ref),), sem)
    position = lax.axis_index("tm")
    spec = jnp.dot(framed_ref[...], table_ref[...], preferred_element_type=jnp.float32)
    for tile in range(2 * TILES):
        spec_ref[tile] = spec[:, tile * LANES : (tile + 1) * LANES]

    row = lax.broadcasted_iota(jnp.int32, (frames, 1), 0)
    live = jnp.where(position * frames + row < valid_ref[0], 1.0 / 255.0, 0.0)
    weight_ref[TILES - 1] = jnp.zeros((2, frames, LANES), jnp.float32)
    for k in range(2):
        weight = masks_ref[k].astype(jnp.float32) * live
        for tile in range(TILES):
            kept_lanes = min(LANES, BINS - tile * LANES)
            weight_ref[tile, k, :, :kept_lanes] = weight[:, tile * LANES : tile * LANES + kept_lanes]
    edge_weight_ref[...] = weight_ref[:, :, frames - MICS :, :]

    for slot, tile in enumerate(slot_tiles(position)[:2]):

        def add_frames(group, sums):
            first = pl.multiple_of(group * MICS, MICS)
            weights = [weight_ref[tile, k, pl.ds(first, MICS), :] for k in range(2)]
            for frame in range(MICS):
                rows = pl.ds(pl.multiple_of((first + frame) * MICS, MICS), MICS)
                sums = add_frame(
                    sums, spec_ref[tile, rows, :], spec_ref[TILES + tile, rows, :], [w[frame : frame + 1] for w in weights]
                )
            return sums

        zero = jnp.zeros((MICS, LANES), jnp.float32)
        kept_ref[slot] = jnp.concatenate(lax.fori_loop(0, frames // MICS, add_frames, (zero,) * 2 * MICS, unroll=2), axis=0)
    kept_ref[2] = last_bin_sums(frames, spec_ref, weight_ref)
    for copy in copies:
        copy.wait()


def edges_kernel(devices, own0_ref, own1_ref, got0_ref, got1_ref, table_ref, edge_weight_ref, kept_ref, spec_ref, mine_ref, theirs_ref, framed_ref):
    position = lax.axis_index("tm")
    even = position % 2 == 0
    own = [own0_ref[...].astype(jnp.float32), own1_ref[...].astype(jnp.float32)]
    got = [got0_ref[...].astype(jnp.float32), got1_ref[...].astype(jnp.float32)]
    head, tail = jnp.where(even, own[1], own[0]), jnp.where(even, own[0], own[1])
    prev, after = jnp.where(even, got[1], got[0]), jnp.where(even, got[0], got[1])
    prev = jnp.where(position > 0, prev, 0.0)
    after = jnp.where(position < devices - 1, after, 0.0)
    joined = jnp.concatenate(
        [jnp.concatenate([prev, head[:, :TAIL]], axis=1), jnp.concatenate([tail, after[:, :TAIL]], axis=1)], axis=0
    )
    for i in range(HALO):
        start = LEAD - HALO * HOP + i * HOP
        base, shift = start // LANES * LANES, start % LANES
        turned = joined if shift == 0 else pltpu.roll(joined, joined.shape[1] - shift, 1)
        framed_ref[2 * MICS * i : 2 * MICS * (i + 1), :] = turned[:, base : base + NFFT]
    used = 2 * MICS * HALO
    framed_ref[used:, :] = jnp.zeros((framed_ref.shape[0] - used, NFFT), jnp.float32)
    spec = jnp.dot(framed_ref[...].astype(jnp.bfloat16), table_ref[...], preferred_element_type=jnp.float32)
    for tile in range(2 * TILES):
        spec_ref[tile] = spec[:, tile * LANES : (tile + 1) * LANES]
    for slot, tile in enumerate(slot_tiles(position)):
        sums = (jnp.zeros((MICS, LANES), jnp.float32),) * 2 * MICS
        for i in range(HALO):
            rows = slice((2 * i + 1) * MICS, (2 * i + 2) * MICS)
            at = MICS - HALO + i
            weights = [edge_weight_ref[tile, k, at : at + 1, :] for k in range(2)]
            sums = add_frame(sums, spec_ref[tile, rows, :], spec_ref[TILES + tile, rows, :], weights)
        total = kept_ref[slot] + jnp.concatenate(sums, axis=0)
        if slot == 0:
            mine_ref[:STATS, :] = total
        elif slot == 1:
            theirs_ref[:STATS, :] = total
        else:
            last_bin = jnp.transpose(total)[:MICS]
            mine_ref[STATS:, :] = last_bin
            theirs_ref[STATS:, :] = last_bin


def columns_of(kept, sub):
    low = sub < MICS // 2
    diag_re = [kept[0], kept[1], kept[3], kept[5]]
    diag_im = [jnp.zeros_like(kept[0]), kept[2], kept[4], kept[6]]
    turned = pltpu.roll(kept[7], MICS // 2, 0)
    diag_re.append(jnp.where(low, kept[7], turned))
    diag_im.append(jnp.where(low, -turned, kept[7]))
    for shift in range(MICS // 2 + 1, MICS):
        diag_re.append(pltpu.roll(diag_re[MICS - shift], MICS - shift, 0))
        diag_im.append(-pltpu.roll(diag_im[MICS - shift], MICS - shift, 0))
    columns = []
    for n in range(MICS):
        re, im = diag_re[n], diag_im[n]
        for m in range(1, MICS):
            re = jnp.where(sub == m, diag_re[(n - m) % MICS], re)
            im = jnp.where(sub == m, diag_im[(n - m) % MICS], im)
        columns.append((re, im))
    return columns


def beams_of(stats, ref_mic):
    sub = lax.broadcasted_iota(jnp.int32, stats[0].shape, 0)
    answer = columns_of(stats[:MICS], sub)
    matrix = columns_of(stats[MICS:], sub)
    spread = jnp.sum(stats[MICS], axis=0, keepdims=True)
    ridge = loading * spread / MICS + epsilon
    matrix = [(jnp.where(sub == n, re + ridge, re), im) for n, (re, im) in enumerate(matrix)]
    for pivot in range(MICS):
        col_re, col_im = matrix[pivot]
        pivot_re = col_re[pivot : pivot + 1]
        pivot_im = col_im[pivot : pivot + 1]
        modulus = pivot_re * pivot_re + pivot_im * pivot_im
        inverse_re = pivot_re / modulus
        inverse_im = -pivot_im / modulus

        def eliminated(column):
            re, im = column
            row_re, row_im = re[pivot : pivot + 1], im[pivot : pivot + 1]
            lead_re = row_re * inverse_re - row_im * inverse_im
            lead_im = row_re * inverse_im + row_im * inverse_re
            return (
                jnp.where(sub == pivot, lead_re, re - (col_re * lead_re - col_im * lead_im)),
                jnp.where(sub == pivot, lead_im, im - (col_re * lead_im + col_im * lead_re)),
            )

        matrix = [eliminated(c) if n > pivot else c for n, c in enumerate(matrix)]
        answer = [eliminated(c) for c in answer]
    trace = answer[0][0][0:1]
    beam_re, beam_im = answer[0]
    for n in range(1, MICS):
        trace = trace + answer[n][0][n : n + 1]
        beam_re = jnp.where(ref_mic == n, answer[n][0], beam_re)
        beam_im = jnp.where(ref_mic == n, answer[n][1], beam_im)
    scale = 1.0 / (trace + epsilon)
    return beam_re * scale, beam_im * scale


def solve_kernel(stats_ref, ref_mic_ref, beam_ref, last_ref):
    blank = jnp.zeros((LANES - MICS, LANES), jnp.float32)
    last_bin = jnp.transpose(jnp.concatenate([stats_ref[STATS:, :], blank], axis=0))
    for out_ref, stats in ((beam_ref, stats_ref[:STATS, :]), (last_ref, last_bin)):
        kept = [stats[i * MICS : (i + 1) * MICS] for i in range(2 * MICS)]
        beam_re, beam_im = beams_of(kept, ref_mic_ref[0])
        out_ref[:MICS, :] = beam_re
        out_ref[MICS:, :] = beam_im


def power_of(beam_ref, tile, spec_ref, edge_spec_ref):
    beam_re, beam_im = beam_ref[:MICS, :], beam_ref[MICS:, :]
    groups = spec_ref.shape[1] // (MICS * MICS)
    power = []
    for group in range(groups + 1):
        from_ref, first = (spec_ref, group * MICS * MICS) if group < groups else (edge_spec_ref, 0)
        sum_re = sum_im = None
        for m in range(MICS):
            rows = pl.ds(first + m, MICS, stride=MICS)
            x_re, x_im = from_ref[tile, rows, :], from_ref[TILES + tile, rows, :]
            b_re, b_im = beam_re[m : m + 1], beam_im[m : m + 1]
            part_re = b_re * x_re + b_im * x_im
            part_im = b_re * x_im - b_im * x_re
            sum_re = part_re if sum_re is None else sum_re + part_re
            sum_im = part_im if sum_im is None else sum_im + part_im
        power.append(sum_re * sum_re + sum_im * sum_im)
    return jnp.concatenate(power, axis=0)


def mel_of(power, bank):
    return jnp.dot(power, bank, precision=lax.Precision.HIGHEST, preferred_element_type=jnp.float32)


def power_kernel(mine_ref, last_ref, spec_ref, edge_spec_ref, bank_ref, conv1_w_ref, mel_ref, taps_ref, padded_ref):
    padded_ref[...] = jnp.zeros(padded_ref.shape, jnp.float32)
    for shift_t in range(3):
        padded_ref[SPAN * shift_t : SPAN * shift_t + 3, :] = conv1_w_ref[3 * shift_t : 3 * shift_t + 3, :].astype(jnp.float32)
    taps_ref[...] = padded_ref[...].astype(taps_ref.dtype)
    mine, _, last = slot_tiles(lax.axis_index("tm"))
    power = [power_of(beam_ref, tile, spec_ref, edge_spec_ref) for beam_ref, tile in ((mine_ref, mine), (last_ref, last))]
    bank = jnp.concatenate([bank_ref[mine], bank_ref[last]], axis=0)
    mel_ref[...] = mel_of(jnp.concatenate(power, axis=1), bank)


def stem_kernel(frames, theirs_ref, mel_ref, spec_ref, edge_spec_ref, valid_ref, bank_ref, taps_ref, conv1_b_ref, conv2_w_ref, conv2_b_ref, proj_w_ref, proj_b_ref, out_ref, logmel_ref):
    position = lax.axis_index("tm")
    valid = valid_ref[0]
    quarter = frames // 4
    theirs = slot_tiles(position)[1]
    mel = mel_ref[...] + mel_of(power_of(theirs_ref, theirs, spec_ref, edge_spec_ref), bank_ref[theirs])
    row = lax.broadcasted_iota(jnp.int32, (frames + MICS, 1), 0)
    edge = (row - frames) // 2 + jnp.where((row - frames) % 2 == 0, -HALO, frames - HALO)
    time = position * frames + jnp.where(row < frames, row, edge)
    live = (time >= 0) & (time < valid)
    logmel = jnp.where(live, jnp.log(mel + epsilon), 0.0)
    logmel = logmel.astype(jnp.bfloat16).astype(jnp.float32)
    for half in range(2):
        part = logmel[:, half * LANES : (half + 1) * LANES]
        logmel_ref[half, HALO : HALO + frames, :] = part[:frames]
        for i in range(HALO):
            logmel_ref[half, i : i + 1, :] = part[frames + 2 * i : frames + 2 * i + 1]
            logmel_ref[half, frames + i : frames + i + 1, :] = part[frames + 2 * i + 1 : frames + 2 * i + 2]

    q_first = (MELS - 3) // 2 + 1
    q_second = (q_first - 3) // 2 + 1
    order = list(range(0, q_first, 2)) + list(range(1, q_first, 2))
    evens = (q_first + 1) // 2
    lane = lax.broadcasted_iota(jnp.int32, (quarter, LANES), 1)
    row = lax.broadcasted_iota(jnp.int32, (quarter, 1), 0)
    windows = []
    for tap in range(3):
        packs = []
        for half in range(2):
            rows = [logmel_ref[half, pl.ds(2 * tap + a, quarter, stride=4), :] for a in range(3)]
            packs.append(jnp.where(lane < SPAN, rows[0], jnp.where(lane < 2 * SPAN, rows[1], rows[2])))
        patches = []
        for q in order:
            half, shift = (0, 2 * q) if q < 20 else (1, 2 * q - 40)
            patches.append(packs[half] if shift == 0 else pltpu.roll(packs[half], LANES - shift, 1))
        patches = jnp.concatenate(patches, axis=0).astype(jnp.bfloat16)
        layer = jnp.dot(patches, taps_ref[...], preferred_element_type=jnp.float32) + conv1_b_ref[...]
        layer = jnp.maximum(layer, 0.0)
        if tap == 0:
            keep = jnp.concatenate([row + 2 * quarter * position >= 1] * q_first, axis=0)
            layer = jnp.where(keep, layer, 0.0)
        layer = layer.astype(jnp.bfloat16)
        count = quarter * q_second
        windows.append(layer[:count])
        windows.append(layer[quarter * evens : quarter * evens + count])
        windows.append(layer[quarter : quarter + count])
    second = jnp.dot(jnp.concatenate(windows, axis=1), conv2_w_ref[...], preferred_element_type=jnp.float32)
    second = jnp.maximum(second + conv2_b_ref[...], 0.0).astype(jnp.bfloat16)
    flat = jnp.concatenate([second[quarter * r : quarter * (r + 1)] for r in range(q_second)], axis=1)
    features = jnp.dot(flat, proj_w_ref[...], preferred_element_type=jnp.float32) + proj_b_ref[...]
    features = jnp.where(position * frames + 4 * row < valid, features, 0.0)
    out_ref[0] = features.astype(jnp.bfloat16)


def flipped(block, axis, step):
    size = lax.axis_size(axis)
    return lax.ppermute(block, axis, [(i, i ^ step) for i in range(size)])


def summed_over_chips(block, axis):
    size = lax.axis_size(axis)
    if size & (size - 1):
        return lax.psum(block, axis, axis_index_groups=[list(range(c, size, 2)) for c in range(2)])
    step = 2
    while step < size:
        others = [step] if 2 * step >= size else [step, 2 * step, 3 * step]
        block = sum([flipped(block, axis, other) for other in others], block)
        step *= 4
    return block


def paired(block, first):
    size, meets = lax.axis_size("tm"), lax.axis_size("meet")
    pairs = []
    for meet in range(meets):
        at = meet * size
        pairs += [(at + i, at + i + 1) for i in range(first, size - 1, 2)]
        if first and meets % 2:
            pairs.append((at, at + size - 1))
        elif first and meet % 2 == 0:
            pairs += [(at + end, at + size + end) for end in (0, size - 1)]
    return lax.ppermute(block, ("meet", "tm"), pairs + [(j, i) for i, j in pairs])


def per_device(waveform, masks, valid, ref_mic, conv1_w, conv1_b, conv2_w, conv2_b, proj_w, proj_b):
    frames = masks.shape[1]
    channels = conv1_w.shape[1]
    width = proj_w.shape[1]
    vmem = pl.BlockSpec(memory_space=pltpu.VMEM)
    smem = pl.BlockSpec(memory_space=pltpu.SMEM)
    hbm = pl.BlockSpec(memory_space=pltpu.HBM)
    in_hbm = functools.partial(pltpu.with_memory_space_constraint, memory_space=pltpu.HBM)
    params = pltpu.CompilerParams(vmem_limit_bytes=16 * 1024 * 1024)
    rim = jax.ShapeDtypeStruct((MICS, LEAD), waveform.dtype)
    table = dft_table()
    conv2_w = conv2_w.reshape(-1, channels)
    beside, across, framed, levels, table = pl.pallas_call(
        functools.partial(rims_kernel, frames),
        out_shape=(rim, rim, jax.ShapeDtypeStruct((frames * MICS, NFFT), waveform.dtype))
        + tuple(jax.ShapeDtypeStruct(x.shape, x.dtype) for x in (masks, table)),
        in_specs=[hbm] * 3,
        out_specs=(vmem,) * 5,
        scratch_shapes=[pltpu.VMEM(waveform.shape, waveform.dtype), pltpu.SemaphoreType.DMA((3,))],
        compiler_params=params,
        name="rims",
    )(in_hbm(waveform), in_hbm(masks), in_hbm(table))
    got_across = paired(across, 1)
    got_beside = paired(beside, 0)
    stat_block = jax.ShapeDtypeStruct((STATS + MICS, LANES), jnp.float32)
    spec, kept, edge_weight, conv2_w = pl.pallas_call(
        functools.partial(stats_kernel, frames),
        out_shape=(
            jax.ShapeDtypeStruct((2 * TILES, frames * MICS, LANES), jnp.float32),
            jax.ShapeDtypeStruct((TILES, STATS, LANES), jnp.float32),
            jax.ShapeDtypeStruct((TILES, 2, MICS, LANES), jnp.float32),
            jax.ShapeDtypeStruct(conv2_w.shape, conv2_w.dtype),
        ),
        in_specs=[vmem] * 3 + [hbm, smem],
        out_specs=(vmem,) * 4,
        scratch_shapes=[
            pltpu.VMEM((TILES, 2, frames, LANES), jnp.float32),
            pltpu.SemaphoreType.DMA((1,)),
        ],
        compiler_params=params,
        name="stats",
    )(framed, levels, table, in_hbm(conv2_w), valid)
    edge_spec, mine, theirs = pl.pallas_call(
        functools.partial(edges_kernel, lax.axis_size("tm")),
        out_shape=(jax.ShapeDtypeStruct((2 * TILES, MICS * MICS, LANES), jnp.float32), stat_block, stat_block),
        in_specs=[vmem] * 7,
        out_specs=(vmem,) * 3,
        scratch_shapes=[pltpu.VMEM((MICS * MICS, NFFT), jnp.float32)],
        compiler_params=params,
        name="edges",
    )(beside, across, got_beside, got_across, table, edge_weight, kept)
    stats = summed_over_chips(mine + flipped(theirs, "tm", 1), "tm")
    beam = jax.ShapeDtypeStruct((2 * MICS, LANES), jnp.float32)
    beam_mine, beam_last = pl.pallas_call(
        solve_kernel,
        out_shape=(beam, beam),
        in_specs=[vmem, smem],
        out_specs=(vmem, vmem),
        compiler_params=params,
        name="solve",
    )(stats, ref_mic)
    beam_theirs = flipped(beam_mine, "tm", 1)
    rows = frames + MICS
    bank = packed_mel_bank()
    mel, taps = pl.pallas_call(
        power_kernel,
        out_shape=(
            jax.ShapeDtypeStruct((rows, 2 * LANES), jnp.float32),
            jax.ShapeDtypeStruct((LANES, channels), conv1_w.dtype),
        ),
        in_specs=[vmem] * 6,
        out_specs=(vmem,) * 2,
        scratch_shapes=[pltpu.VMEM((LANES, channels), jnp.float32)],
        compiler_params=params,
        name="power",
    )(beam_mine, beam_last, spec, edge_spec, bank, conv1_w)
    return pl.pallas_call(
        functools.partial(stem_kernel, frames),
        out_shape=jax.ShapeDtypeStruct((1, frames // 4, width), jnp.bfloat16),
        in_specs=[vmem] * 4 + [smem] + [vmem] * 7,
        out_specs=vmem,
        scratch_shapes=[pltpu.VMEM((2, rows, LANES), jnp.float32)],
        compiler_params=params,
        name="stem",
    )(
        beam_theirs,
        mel,
        spec,
        edge_spec,
        valid,
        bank,
        taps,
        conv1_b[None],
        conv2_w,
        conv2_b[None],
        proj_w,
        proj_b[None],
    )


def solution(mesh):
    return jax.shard_map(
        per_device,
        mesh=mesh,
        in_specs=(
            P(None, ("meet", "tm")),
            P(None, ("meet", "tm"), None),
            P("meet"),
            P("meet"),
            P(),
            P(),
            P(),
            P(),
            P(),
            P(),
        ),
        out_specs=P(None, ("meet", "tm"), None),
        check_vma=False,
    )
```
